512 devices in a mesh: wide: 64 (over y, z_lo, x), tp: 8 (over z_hi, core).
Axes of the slice: x: 4, y: 8, z: 8 (z_hi: 4, z_lo: 2; z = z_hi * 2 + z_lo), core: 2. Of those that a mesh axis runs over, the one named last changes fastest.
Arguments:
- query: bfloat16 [256, 2048], P('wide', 'tp'), may hold values from -120 to 120
- key_cache: bfloat16 [256, 128, 1024], P('wide', None, 'tp'), may hold values from -6 to 6
- value_cache: bfloat16 [256, 128, 1024], P('wide', None, 'tp'), may hold values from -6 to 6
- new_key: bfloat16 [256, 1024], P('wide', 'tp'), may hold values from -6 to 6
- new_value: bfloat16 [256, 1024], P('wide', 'tp'), may hold values from -6 to 6
- cache_lengths: int32 [256], P('wide'), may hold values from 1 to 128
- out_weight: bfloat16 [2048, 4096], P('tp'), may hold values from -0.125 to 0.125
- delta_index: int32 [64], P('wide'), may hold values from 0 to 63
- delta_values: bfloat16 [64, 1024, 128], P('wide', 'tp'), may hold values from -0.5 to 0.5
- fin_route: int32 [4096, 1], P('wide'), may hold values from 0 to 63; in each aligned block of 64 rows (0 to 63, 64 to 127, ...) at most 2 rows name the same one
- fin_lengths: int32 [4096], P('wide'), may hold values from 1 to 8
- fin_rows: bfloat16 [4096, 8, 8192], P('wide', None, 'tp'), may hold values from -6 to 6
- reward_query: bfloat16 [8192, 512], P('tp'), may hold values from -0.0625 to 0.0625
- rubric_keys: bfloat16 [64, 1024, 128], P('wide'), may hold values from -240 to 240
- rubric_values: bfloat16 [64, 1024, 128], P('wide'), may hold values from -6 to 6
- score_weight: bfloat16 [512], replicated, may hold values from -3 to 3
Outputs:
- decoded: bfloat16 [256, 4096], P('wide', 'tp')
- rewards: float32 [4096], P('wide')
The draws below stay inside these ranges and needn't reach their ends.
Inputs may be any that keep to these rules, and one draw needn't show every extreme that they name: `fin_route`: in the rows of one wide index no reward group is named more than 2 times.
All inputs are finite; a program needn't handle non-finite values.
Results may differ from the reference program's by a relative error of at most 0.0095.
Values may be sent and summed in bfloat16 or wider, within the bound.
No kernel may reach another device: no remote copies, remote signals or barrier semaphores. Data moves between devices by JAX's collectives and lax.ppermute only.
A program may use at most 64 MiB of HBM per device.

```python
import math
import jax
import jax.numpy as jnp
import numpy as np
from jax import lax

D = 4096
HD = 128
QH = 16
KVH = 8
BLK = 128
RD = 8192
RHEADS = 4
PLEN = 1024
LEN = 128
FIN_DEV = 64
RLEN = 8
RQ = 512
SEQS = 256
DELTAS = 64
GROUPS = 64
FINISHED = 4096
CAP = 2
RB = 2
CB = 32
N_WIDE = 64
N_TP = 8


def shared_keys(key):
    base = jax.random.normal(key, (SEQS, LEN, KVH * HD), jnp.float32)
    return jnp.clip(base, -6.0, 6.0)


def draw_key_cache(key, part):
    cached = shared_keys(key)
    return cached.astype(jnp.bfloat16)


def draw_query(key, part):
    key = jax.random.fold_in(key, 7)
    normal_key = jax.random.fold_in(key, 0)
    queries = jnp.clip(jax.random.normal(normal_key, (SEQS, QH * HD), jnp.float32), -6.0, 6.0)
    return queries.astype(jnp.bfloat16)


def draw_rubric_keys(key, part):
    key = jax.random.fold_in(key, 11)
    normal_key = jax.random.fold_in(key, 0)
    keys_drawn = jnp.clip(jax.random.normal(normal_key, (GROUPS, PLEN, HD), jnp.float32), -4.0, 4.0)
    return keys_drawn.astype(jnp.bfloat16)


def set_ends(values, own_key, low, largest):
    longest = values.shape.index(max(values.shape))
    spots = []
    for shift in (0, 1):
        where = [jax.random.randint(jax.random.fold_in(own_key, axis), (), 0, length) for axis, length in enumerate(values.shape)]
        where[longest] = (where[longest] + shift) % values.shape[longest]
        spots.append(tuple(where))
    return values.at[spots[0]].set(low).at[spots[1]].set(largest)


def shard_levels(rng, shape, pieces, low, high):
    def one(dim, blocks):
        heights = jax.random.uniform(jax.random.fold_in(jax.random.fold_in(rng, 6), dim), (blocks,), jnp.float32, low / len(pieces), high / len(pieces))
        return jnp.repeat(jnp.exp(heights), shape[dim] // blocks).reshape((-1,) + (1,) * (len(shape) - dim - 1))

    gain = one(*pieces[0])
    for cut in pieces[1:]:
        gain = gain * one(*cut)
    return gain


def routed_block(key, own, number, rows, count, top, most, slope):
    sequence = jax.random.permutation(key, count)
    packed, ordinary = portions_of(count, rows * top, most, slope, True), portions_of(count, rows * top, most, slope, False)
    places = jnp.arange(count)

    def named(tallies, turn):
        used = int((tallies > 0).sum())
        fixed = max(1, used // 4)
        shifted = fixed + (places - fixed + turn * (used - fixed)) % max(1, count - fixed)
        return jnp.zeros((count,), jnp.int32).at[sequence[jnp.where(places < fixed, places, shifted)]].set(jnp.asarray(tallies, jnp.int32))

    tallies = jnp.where(number % 4 == 0, named(packed, number // 4), named(ordinary, number - number // 4 - 1))
    mixed = jax.random.permutation(jax.random.fold_in(own, 3), count)
    giver, sink = mixed[0:count // 2 * 2:2], mixed[1:count // 2 * 2:2]
    slack = jnp.minimum(tallies[giver] - 1, most - tallies[sink]) // 2
    slack = jnp.where((giver == sequence[0]) | (sink == sequence[0]) | (tallies[sink] == 0), 0, jnp.maximum(slack, 0))
    shifted = jax.random.randint(jax.random.fold_in(own, 4), (count // 2,), 0, 1 << 20) % (slack + 1)
    tallies = tallies.at[giver].add(-shifted).at[sink].add(shifted)
    items = jnp.searchsorted(jnp.cumsum(tallies), jnp.arange(rows * top), side="right").astype(jnp.int32)
    listing = items.reshape(top, rows).T
    listing = listing[jax.random.permutation(jax.random.fold_in(own, 1), rows)]
    turn = jax.random.randint(jax.random.fold_in(own, 2), (rows, 1), 0, top)
    return jnp.take_along_axis(listing, (jnp.arange(top)[None, :] + turn) % top, axis=1)


def portions_of(number_of, total, limit, lean, full):
    loads = [(1 << 20) // math.isqrt(rank ** lean) + 1 for rank in range(1, number_of + 1)]
    largest = limit if full else min(limit, max(-(-total // number_of), total * loads[0] // sum(loads)))
    least = 1 if total - largest >= number_of - 1 else 0
    holding, surplus = [largest] + [least] * (number_of - 1), total - largest - least * (number_of - 1)
    while surplus > 0:
        free = [i for i in range(1, number_of) if holding[i] < largest] or [i for i in range(1, number_of) if holding[i] < limit]
        whole, left = sum([loads[i] for i in free]), surplus
        for i in free:
            more = min(limit - holding[i], max(1, left * loads[i] // whole), surplus)
            holding[i] = holding[i] + more
            surplus = surplus - more
    return np.array(holding)


def gaussian(stream_key, extent, deviation, limit, cuts=(), kind=jnp.bfloat16):
    values = deviation * jax.random.normal(stream_key, extent, jnp.float32)
    if cuts:
        values = values * shard_levels(stream_key, extent, cuts, -0.22, 0.18)
    return jnp.clip(values, -limit, limit).astype(kind)


def setup_inputs(seed: int = 0) -> dict:
    seeds = jax.random.split(jax.random.key(seed), 17)
    query = draw_query(jax.random.fold_in(seeds[16], 71), 0)
    key_cache = draw_key_cache(jax.random.fold_in(seeds[16], 71), 0)
    value_cache = gaussian(seeds[2], (SEQS, LEN, KVH * HD), 1.0, 6.0, ((0, 64), (2, 8)))
    new_key = gaussian(seeds[3], (SEQS, KVH * HD), 1.0, 6.0, ((0, 64), (1, 8)))
    new_value = gaussian(seeds[4], (SEQS, KVH * HD), 1.0, 6.0, ((0, 64), (1, 8)))
    cache_lengths = set_ends(jax.random.randint(seeds[5], (SEQS,), 1, LEN + 1), jax.random.fold_in(seeds[5], 1), 1, LEN).astype(jnp.int32)
    out_weight = gaussian(seeds[6], (QH * HD, D), (QH * HD) ** -0.5, 0.125, ((0, 8),))
    delta_index = set_ends(jax.random.randint(seeds[7], (DELTAS,), 0, RB * CB), jax.random.fold_in(seeds[7], 1), 0, (RB * CB) - 1).astype(jnp.int32)
    delta_values = gaussian(seeds[8], (DELTAS, N_TP * BLK, BLK), BLK ** -0.5, 0.5, ((0, 64), (1, 8)))
    fin_route_keys = jax.random.split(jax.random.fold_in(seeds[9], 1), FINISHED // FIN_DEV)
    fin_route_turns = jax.random.permutation(jax.random.fold_in(seeds[9], 3), FINISHED // FIN_DEV)
    fin_route = jax.vmap(lambda own, number: routed_block(jax.random.fold_in(seeds[9], 2), own, number, FIN_DEV, N_WIDE, 1, CAP, 2))(fin_route_keys, fin_route_turns).reshape((FINISHED, 1))
    fin_lengths = set_ends(jax.random.randint(seeds[10], (FINISHED,), 1, RLEN + 1), jax.random.fold_in(seeds[10], 1), 1, RLEN).astype(jnp.int32)
    fin_rows = gaussian(seeds[11], (FINISHED, RLEN, RD), 1.0, 6.0, ((0, 64), (2, 8)))
    reward_query = gaussian(seeds[12], (RD, RQ), RD ** -0.5, 0.0625, ((0, 8),))
    rubric_keys = draw_rubric_keys(jax.random.fold_in(seeds[16], 71), 0)
    rubric_values = gaussian(seeds[14], (GROUPS, PLEN, HD), 1.0, 6.0, ((0, 64),))
    score_weight = gaussian(seeds[15], (RQ,), 4 ** -0.5, 3.0)
    return {"query": query, "key_cache": key_cache, "value_cache": value_cache, "new_key": new_key, "new_value": new_value, "cache_lengths": cache_lengths, "out_weight": out_weight, "delta_index": delta_index, "delta_values": delta_values, "fin_route": fin_route, "fin_lengths": fin_lengths, "fin_rows": fin_rows, "reward_query": reward_query, "rubric_keys": rubric_keys, "rubric_values": rubric_values, "score_weight": score_weight}


def attend(query, key_cache, value_cache, new_key, new_value, cache_lengths):
    group_size = QH // KVH
    queries = query.astype(jnp.float32).reshape(SEQS, KVH, group_size, HD)
    cached_keys = key_cache.astype(jnp.float32).reshape(SEQS, LEN, KVH, HD)
    cached_values = value_cache.astype(jnp.float32).reshape(SEQS, LEN, KVH, HD)
    fresh_keys = new_key.astype(jnp.float32).reshape(SEQS, KVH, HD)
    fresh_values = new_value.astype(jnp.float32).reshape(SEQS, KVH, HD)
    scale_factor = 1.0 / math.sqrt(HD)
    scores = jnp.einsum('skgd,slkd->skgl', queries, cached_keys, precision=lax.Precision.HIGHEST) * scale_factor
    own_score = jnp.einsum('skgd,skd->skg', queries, fresh_keys, precision=lax.Precision.HIGHEST) * scale_factor
    valid = jnp.arange(LEN)[None, :] < cache_lengths[:, None]
    scores = jnp.where(valid[:, None, None, :], scores, -jnp.inf)
    highest = jnp.maximum(lax.optimization_barrier(jnp.max(scores, axis=-1)), own_score)
    weights = jnp.exp(scores - highest[..., None])
    own_weight = jnp.exp(own_score - highest)
    denominator = lax.optimization_barrier(jnp.sum(weights, axis=-1)) + own_weight
    probs = (weights / denominator[..., None]).astype(jnp.bfloat16)
    own_prob = (own_weight / denominator).astype(jnp.bfloat16)
    mixed = jnp.einsum('skgl,slkd->skgd', probs.astype(jnp.float32), cached_values, precision=lax.Precision.HIGHEST)
    mixed = mixed + own_prob.astype(jnp.float32)[..., None] * fresh_values[:, :, None, :]
    return mixed.astype(jnp.bfloat16).reshape(SEQS, QH * HD)

def delta_matrix(delta_index, delta_values):
    row_pick = (delta_index[:, None] // CB == jnp.arange(RB)[None, :]).astype(jnp.float32)
    col_pick = (delta_index[:, None] % CB == jnp.arange(CB)[None, :]).astype(jnp.float32)
    blocks = delta_values.astype(jnp.float32).reshape(DELTAS, N_TP, BLK, BLK)
    dense = jnp.einsum('jr,jc,jtab->tracb', row_pick, col_pick, blocks, precision=lax.Precision.HIGHEST)
    return dense.reshape(QH * HD, D)

def reference(query, key_cache, value_cache, new_key, new_value, cache_lengths, out_weight, delta_index, delta_values, fin_route, fin_lengths, fin_rows, reward_query, rubric_keys, rubric_values, score_weight):
    attn = attend(query, key_cache, value_cache, new_key, new_value, cache_lengths)
    dense = delta_matrix(delta_index, delta_values)
    decoded = jnp.dot(attn, out_weight, preferred_element_type=jnp.float32)
    decoded = decoded + jnp.dot(attn.astype(jnp.float32), dense, precision=lax.Precision.HIGHEST)
    decoded = decoded.astype(jnp.bfloat16)
    scorer = score_weight.astype(jnp.float32)

    def score_one(item):
        rows_one, target, length_one = item
        keys_one = lax.dynamic_index_in_dim(rubric_keys, target, 0, keepdims=False).astype(jnp.float32)
        values_one = lax.dynamic_index_in_dim(rubric_values, target, 0, keepdims=False).astype(jnp.float32)
        projected = jnp.dot(rows_one, reward_query, preferred_element_type=jnp.float32)
        squares = lax.optimization_barrier(jnp.sum(jnp.square(rows_one.astype(jnp.float32)), axis=-1))
        normed = projected * lax.rsqrt(squares / RD + 1e-05)[:, None]
        heads = normed.reshape(RLEN, RHEADS, HD)
        scores = jnp.einsum('thd,pd->thp', heads, keys_one, precision=lax.Precision.HIGHEST) / math.sqrt(HD)
        highest = lax.optimization_barrier(jnp.max(scores, axis=-1, keepdims=True))
        weights = jnp.exp(scores - highest)
        probs = (weights / lax.optimization_barrier(jnp.sum(weights, axis=-1, keepdims=True))).astype(jnp.bfloat16)
        context = jnp.einsum('thp,pd->thd', probs.astype(jnp.float32), values_one, precision=lax.Precision.HIGHEST)
        context = context.reshape(RLEN, RQ)
        token_score = lax.optimization_barrier(jnp.sum(jax.nn.silu(context) * scorer[None, :], axis=-1))
        mask = jnp.arange(RLEN) < length_one
        length_float = length_one.astype(jnp.float32)
        return jnp.sum(jnp.where(mask, token_score, 0.0)) / length_float
    rewards = lax.map(score_one, (fin_rows, fin_route[:, 0].astype(jnp.int32), fin_lengths))
    return (decoded, rewards)
```

```python
import functools
import math

import jax
import jax.numpy as jnp
from jax import lax
from jax.experimental import pallas as pl
from jax.experimental.pallas import tpu as pltpu
from jax.sharding import PartitionSpec as P

HD = 128
RD = 8192
CAP = 2
F32 = jnp.float32
BF16 = jnp.bfloat16


def split3(x):
    high = x.astype(BF16)
    rest = x - high.astype(F32)
    mid = rest.astype(BF16)
    low = (rest - mid.astype(F32)).astype(BF16)
    return high, mid, low


def mm(a, b):
    return jnp.dot(a, b, preferred_element_type=F32)


def mm_t(a, b):
    return lax.dot_general(a, b, (((1,), (1,)), ((), ())), preferred_element_type=F32)


def rows_at(first, count, stride):
    return pl.ds(first, count, stride=stride)


def whole(shape):
    return pl.BlockSpec(shape, lambda *_: (0,) * len(shape))


def project_kernel(row_len, per_token, rows_ref, wq_ref, out_ref, acc_ref, sq_ref):
    step = pl.program_id(0)
    rows = rows_ref[...]
    chunk = rows.shape[0] // row_len
    heads = wq_ref.shape[1] // HD
    seqs = (per_token - 8) // heads
    many = rows.shape[0]
    product = mm(rows, wq_ref[...])
    for h in range(heads):
        acc_ref[h * many : (h + 1) * many, :] = product[:, h * HD : (h + 1) * HD]
    wide_rows = rows.astype(F32)
    sums = jnp.sum(wide_rows * wide_rows, axis=1, keepdims=True)
    sq_ref[...] = jnp.broadcast_to(sums, sq_ref.shape)

    @pl.when(step == 0)
    def _():
        for t in range(row_len):
            out_ref[t * per_token + heads * seqs : (t + 1) * per_token, :] = jnp.zeros((8, HD), F32)

    base = pl.multiple_of(step * chunk, chunk)
    here = lax.broadcasted_iota(jnp.int32, (chunk, HD), 0) + step * chunk
    lane = lax.broadcasted_iota(jnp.int32, (chunk, HD), 1)
    for t in range(row_len):
        for h in range(heads):
            out_ref[pl.ds(t * per_token + h * seqs + base, chunk), :] = acc_ref[
                rows_at(h * many + t, chunk, row_len), :
            ]
        picked = jnp.where(here == lane, sq_ref[rows_at(t, chunk, row_len), :], 0.0)
        tail = slice(t * per_token + heads * seqs, (t + 1) * per_token)
        out_ref[tail, :] += jnp.sum(picked, axis=0, keepdims=True)


def decode_kernel(
    lens_ref, q_ref, k_ref, v_ref, nk_ref, nv_ref, w_ref, route_ref, attn_ref, out_ref, place_ref
):
    seqs = q_ref.shape[0]
    rows = 2 * seqs
    scale = 1.0 / math.sqrt(HD)
    q = q_ref[...].astype(F32)
    queries = jnp.concatenate([q[:, :HD], q[:, HD:]], axis=0)
    nk = nk_ref[...].astype(F32)
    nv = nv_ref[...].astype(F32)
    own_key = jnp.concatenate([nk, nk], axis=0)
    own_value = jnp.concatenate([nv, nv], axis=0)
    row = lax.broadcasted_iota(jnp.int32, (rows, HD), 0) % seqs
    place_in = lax.broadcasted_iota(jnp.int32, (rows, HD), 1)
    queries16 = queries.astype(BF16)
    scores = jnp.zeros((rows, HD), F32)
    length = jnp.zeros((rows, HD), jnp.int32)
    for s in range(seqs):
        scores = jnp.where(row == s, mm_t(queries16, k_ref[s]), scores)
        length = jnp.where(row == s, lens_ref[s], length)
    scores = jnp.where(place_in < length, scores * scale, -jnp.inf)
    own_score = jnp.sum(queries * own_key, axis=1, keepdims=True) * scale
    highest = jnp.maximum(jnp.max(scores, axis=1, keepdims=True), own_score)
    weights = jnp.exp(scores - highest)
    own_weight = jnp.exp(own_score - highest)
    denominator = jnp.sum(weights, axis=1, keepdims=True) + own_weight
    probs = (weights / denominator).astype(BF16)
    own_prob = (own_weight / denominator).astype(BF16).astype(F32)
    mixed = jnp.zeros((rows, HD), F32)
    for s in range(seqs):
        mixed = jnp.where(row == s, mm(probs, v_ref[s]), mixed)
    attn = (mixed + own_prob * own_value).astype(BF16).astype(F32)
    attn_ref[...] = attn
    turned = jnp.concatenate([attn[seqs:], attn[:seqs]], axis=0)
    both = jnp.concatenate([attn, turned], axis=1).astype(BF16)
    blocks = w_ref.shape[1] // HD
    for first in range(0, blocks, 4):
        part = mm(both, w_ref[:, first * HD : (first + 4) * HD])
        for c in range(4):
            out_ref[(first + c) * rows : (first + c + 1) * rows, :] = part[:, c * HD : (c + 1) * HD]
    slots = place_ref.shape[0]
    groups = slots // CAP
    down = lax.broadcasted_iota(jnp.int32, (HD, HD), 0)
    across = lax.broadcasted_iota(jnp.int32, (HD, HD), 1)
    target = jnp.broadcast_to(route_ref[...], (HD, HD))
    target_down = jnp.sum(jnp.where(down == across, target, 0.0), axis=1, keepdims=True)
    earlier = jnp.where(jnp.logical_and(target == target_down, down < across), 1.0, 0.0)
    rank = jnp.sum(earlier, axis=0, keepdims=True)
    slot = lax.broadcasted_iota(jnp.int32, (slots, HD), 0)
    group = (slot % groups).astype(F32)
    order = (slot // groups).astype(F32)
    held = jnp.logical_and(route_ref[...] == group, rank == order)
    place_ref[...] = jnp.where(held, 1.0, 0.0).astype(BF16)


def place_kernel(sources, per_token, heads, x_ref, attn_ref, place_ref, out_ref):
    seqs = (per_token - 8) // heads
    groups = place_ref.shape[0] // CAP
    each = out_ref.shape[0] // groups
    total = x_ref[0:per_token, :]
    for k in range(1, sources):
        total = total + x_ref[k * per_token : (k + 1) * per_token, :]
    squares = total[heads * seqs : heads * seqs + 1, :]
    inverse = lax.rsqrt(squares / RD + 1e-05)
    down = lax.broadcasted_iota(jnp.int32, (seqs, HD), 0)
    across = lax.broadcasted_iota(jnp.int32, (seqs, HD), 1)
    factor = jnp.sum(jnp.where(down == across, inverse, 0.0), axis=1, keepdims=True)
    normed = jnp.concatenate(
        [total[h * seqs : (h + 1) * seqs, :] * factor for h in range(heads)], axis=1
    )
    if seqs < HD:
        normed = jnp.concatenate([normed, jnp.zeros((HD - seqs, heads * HD), F32)], axis=0)
    place = place_ref[...]
    high, mid, low = split3(normed)
    placed = (mm(place, low) + mm(place, mid)) + mm(place, high)
    for r in range(CAP):
        for h in range(heads):
            out_ref[rows_at(r * heads + h, groups, each), :] = placed[
                r * groups : (r + 1) * groups, h * HD : (h + 1) * HD
            ]
    attn = attn_ref[...]
    for g in range(groups):
        out_ref[g * each + CAP * heads : (g + 1) * each, :] = attn


def score_kernel(heads, index_ref, x_ref, keys_ref, values_ref, weight_ref, delta_ref, out_ref):
    tile = CAP * heads
    senders = x_ref.shape[0]
    keys = keys_ref[...]
    keys3 = jnp.concatenate([keys, keys, keys], axis=1)
    values = values_ref[...]
    delta = delta_ref[...]
    weight = weight_ref[...].astype(F32)
    weight = jnp.concatenate([weight] * CAP, axis=0)[None]
    scale = 1.0 / math.sqrt(HD)
    block = index_ref[0]
    columns = 32
    row_block = block // columns
    column = (block % columns).astype(F32)
    at_once = min(16, senders)
    row = lax.broadcasted_iota(jnp.int32, (at_once, tile, HD), 1)
    lane = lax.broadcasted_iota(jnp.int32, (at_once, tile, HD), 2)
    for first in range(0, senders, at_once):
        x = x_ref[first : first + at_once]
        pieces = split3(x[:, :tile, :].reshape(at_once * tile, HD))
        scores = mm_t(jnp.concatenate(pieces, axis=1), keys3) * scale
        highest = jnp.max(scores, axis=1, keepdims=True)
        weights = jnp.exp(scores - highest)
        probs = (weights * (1.0 / jnp.sum(weights, axis=1, keepdims=True))).astype(BF16)
        context = mm(probs, values)
        gated = context / (1.0 + jnp.exp(-context))
        terms = gated.reshape(at_once, tile, HD) * weight
        by_head = jnp.sum(terms, axis=2, keepdims=True)
        attn = x[:, tile:, :].reshape(at_once * tile, HD).astype(BF16)
        product = mm(attn, delta).reshape(at_once, tile, HD)
        seqs = tile // 2
        turned = jnp.concatenate([product[:, seqs:], product[:, :seqs]], axis=1)
        result = jnp.where(row_block == 0, product, turned)
        result = jnp.where(row < seqs, result, 0.0)
        for r in range(CAP):
            mine = jnp.logical_and(row >= r * heads, row < (r + 1) * heads)
            score = jnp.sum(jnp.where(mine, by_head, 0.0), axis=1, keepdims=True)
            result = jnp.where(jnp.logical_and(row == seqs, lane == r), score, result)
        result = jnp.where(jnp.logical_and(row == seqs, lane == CAP), column, result)
        out_ref[first : first + at_once] = result


def merge_kernel(tile, x_ref, partial_ref, place_ref, out_ref):
    senders = x_ref.shape[0] // tile
    blocks = partial_ref.shape[0] // tile
    seqs = tile // 2
    extra = x_ref[rows_at(seqs, senders, tile), :]
    column = extra[:, CAP : CAP + 1]
    pieces = split3(
        jnp.concatenate([x_ref[rows_at(s, senders, tile), :] for s in range(seqs)], axis=1)
    )
    down = lax.broadcasted_iota(jnp.int32, (senders, senders), 0)
    across = lax.broadcasted_iota(jnp.int32, (senders, senders), 1)
    column_across = jnp.sum(
        jnp.where(down == across, jnp.broadcast_to(column, (senders, senders)), 0.0),
        axis=0,
        keepdims=True,
    )
    wanted = lax.broadcasted_iota(jnp.int32, (blocks, senders), 0).astype(F32)
    pick = jnp.where(wanted == column_across, 1.0, 0.0).astype(BF16)
    high, mid, low = pieces
    added = (mm(pick, low) + mm(pick, mid)) + mm(pick, high)
    out_ref[...] = partial_ref[...]
    for s in range(seqs):
        where = rows_at(s, blocks, tile)
        out_ref[where, :] = partial_ref[where, :] + added[:, s * HD : (s + 1) * HD]
    place = place_ref[...].astype(F32)
    score = jnp.concatenate([extra[:, r : r + 1] for r in range(CAP)], axis=0)
    back = jnp.sum(place * score, axis=0, keepdims=True)
    shards = 8
    out_ref[rows_at(seqs, shards, blocks // shards * tile), :] = jnp.broadcast_to(
        back, (shards, HD)
    )


def final_kernel(tile, x_ref, length_ref, decoded_ref, rewards_ref):
    seqs = tile // 2
    total = x_ref[0]
    for k in range(1, x_ref.shape[0]):
        total = total + x_ref[k]
    for c in range(total.shape[0] // tile):
        decoded_ref[:, c * HD : (c + 1) * HD] = total[c * tile : c * tile + seqs, :].astype(BF16)
    length = length_ref[...]
    count = rewards_ref.shape[1]
    reward = jnp.zeros((1, HD), F32)
    for k in range(x_ref.shape[0]):
        reward = reward + jnp.where(length > k, x_ref[k, seqs : seqs + 1, :], 0.0)
    rewards_ref[...] = (reward / length)[:, :count]


def per_device(
    query,
    key_cache,
    value_cache,
    new_key,
    new_value,
    cache_lengths,
    out_weight,
    delta_index,
    delta_values,
    fin_route,
    fin_lengths,
    fin_rows,
    reward_query,
    rubric_keys,
    rubric_values,
    score_weight,
):
    wide_count = lax.axis_size("wide")
    tp_count = lax.axis_size("tp")
    finished, row_len, features = fin_rows.shape
    heads = reward_query.shape[1] // HD
    seq_count = query.shape[0]
    tile = 2 * seq_count
    blocks = out_weight.shape[1] // HD
    slots = CAP * wide_count
    per_token = heads * finished + 8
    smem = pl.BlockSpec(memory_space=pltpu.SMEM)
    chunks = 4 if finished % 32 == 0 else 1

    rows = fin_rows.reshape(finished * row_len, features)
    chunk_rows = finished * row_len // chunks
    partial_tokens = pl.pallas_call(
        functools.partial(project_kernel, row_len, per_token),
        grid=(chunks,),
        in_specs=[
            pl.BlockSpec((chunk_rows, features), lambda m: (m, 0)),
            whole(reward_query.shape),
        ],
        out_specs=whole((row_len * per_token, HD)),
        out_shape=jax.ShapeDtypeStruct((row_len * per_token, HD), F32),
        scratch_shapes=[
            pltpu.VMEM((heads * chunk_rows, HD), F32),
            pltpu.VMEM((chunk_rows, HD), F32),
        ],
        name="project",
    )(rows, reward_query)
    summed_tokens = lax.all_to_all(
        partial_tokens.reshape(tp_count, per_token, HD), "tp", split_axis=0, concat_axis=0, tiled=True
    ).reshape(tp_count * per_token, HD)

    pad = ((0, 0), (0, HD - finished))
    route = jnp.pad(fin_route.reshape(1, finished).astype(F32), pad, constant_values=-1.0)
    lengths = jnp.pad(fin_lengths.reshape(1, finished).astype(F32), pad, constant_values=1.0)
    attn, partial_out, place = pl.pallas_call(
        decode_kernel,
        in_specs=[smem]
        + [
            whole(a.shape)
            for a in (query, key_cache, value_cache, new_key, new_value, out_weight, route)
        ],
        out_specs=[whole((tile, HD)), whole((blocks * tile, HD)), whole((slots, HD))],
        out_shape=[
            jax.ShapeDtypeStruct((tile, HD), F32),
            jax.ShapeDtypeStruct((blocks * tile, HD), F32),
            jax.ShapeDtypeStruct((slots, HD), BF16),
        ],
        grid=(1,),
        name="decode",
    )(
        cache_lengths,
        query,
        key_cache,
        value_cache,
        new_key,
        new_value,
        out_weight,
        route,
    )

    each = CAP * heads + tile
    outgoing = pl.pallas_call(
        functools.partial(place_kernel, tp_count, per_token, heads),
        in_specs=[
            whole((tp_count * per_token, HD)),
            whole((tile, HD)),
            whole((slots, HD)),
        ],
        out_specs=whole((wide_count * each, HD)),
        out_shape=jax.ShapeDtypeStruct((wide_count * each, HD), F32),
        grid=(1,),
        name="place",
    )(summed_tokens, attn, place)
    received = lax.all_to_all(
        outgoing.reshape(wide_count, each, HD), "wide", split_axis=0, concat_axis=0, tiled=True
    )

    answers = pl.pallas_call(
        functools.partial(score_kernel, heads),
        in_specs=[
            smem,
            whole((wide_count, each, HD)),
            whole(rubric_keys.shape[1:]),
            whole(rubric_values.shape[1:]),
            whole((heads, HD)),
            whole(delta_values.shape[1:]),
        ],
        out_specs=whole((wide_count, tile, HD)),
        out_shape=jax.ShapeDtypeStruct((wide_count, tile, HD), F32),
        grid=(1,),
        name="score",
    )(
        delta_index,
        received,
        rubric_keys[0],
        rubric_values[0],
        score_weight.reshape(heads, HD),
        delta_values[0],
    )
    returned = lax.all_to_all(answers, "wide", split_axis=0, concat_axis=0, tiled=True)

    merged = pl.pallas_call(
        functools.partial(merge_kernel, tile),
        in_specs=[
            whole((wide_count * tile, HD)),
            whole((blocks * tile, HD)),
            whole((slots, HD)),
        ],
        out_specs=whole((blocks * tile, HD)),
        out_shape=jax.ShapeDtypeStruct((blocks * tile, HD), F32),
        grid=(1,),
        name="merge",
    )(returned.reshape(wide_count * tile, HD), partial_out, place)
    shares = lax.all_to_all(
        merged.reshape(tp_count, blocks // tp_count * tile, HD),
        "tp",
        split_axis=0,
        concat_axis=0,
        tiled=True,
    )

    decoded, rewards = pl.pallas_call(
        functools.partial(final_kernel, tile),
        in_specs=[whole(shares.shape), whole((1, HD))],
        out_specs=[whole((seq_count, blocks // tp_count * HD)), whole((1, finished))],
        out_shape=[
            jax.ShapeDtypeStruct((seq_count, blocks // tp_count * HD), BF16),
            jax.ShapeDtypeStruct((1, finished), F32),
        ],
        grid=(1,),
        name="final",
    )(shares, lengths)
    return decoded, rewards.reshape(finished)


def solution(mesh):
    in_specs = (
        P("wide", "tp"),
        P("wide", None, "tp"),
        P("wide", None, "tp"),
        P("wide", "tp"),
        P("wide", "tp"),
        P("wide"),
        P("tp", None),
        P("wide"),
        P("wide", "tp", None),
        P("wide", None),
        P("wide"),
        P("wide", None, "tp"),
        P("tp", None),
        P("wide", None, None),
        P("wide", None, None),
        P(),
    )
    out_specs = (P("wide", "tp"), P("wide"))
    return jax.shard_map(
        per_device, mesh=mesh, in_specs=in_specs, out_specs=out_specs, check_vma=False
    )
```

```python
import functools
import math

import jax
import jax.numpy as jnp
from jax import lax
from jax.experimental import pallas as pl
from jax.experimental.pallas import tpu as pltpu
from jax.sharding import PartitionSpec as P

HD = 128
RD = 8192
CAP = 2
CORES = 2
PAIR = 2
VMEM_LIMIT = 16 * 2**20
WEIGHT_COPIES = 4
F32 = jnp.float32
BF16 = jnp.bfloat16


def split2(x):
    high = x.astype(BF16)
    return high, (x - high.astype(F32)).astype(BF16)


def split3(x):
    high, mid = split2(x)
    return high, mid, (x - high.astype(F32) - mid.astype(F32)).astype(BF16)


def mm(a, b):
    return jnp.dot(a, b, preferred_element_type=F32)


def mm_t(a, b):
    return lax.dot_general(a, b, (((1,), (1,)), ((), ())), preferred_element_type=F32)


def rows_at(first, count, stride):
    return pl.ds(first, count, stride=stride)


def local_call(kernel, name, operands, outs, scratch=(), scalars=0, fetched=0, pinned=()):
    vmem = pl.BlockSpec(memory_space=pltpu.VMEM)
    smem = pl.BlockSpec(memory_space=pltpu.SMEM)
    hbm = pl.BlockSpec(memory_space=pltpu.HBM)
    kept = len(operands) - fetched
    operands = list(operands)
    for k in range(len(operands)):
        if k >= kept:
            operands[k] = pltpu.with_memory_space_constraint(operands[k], pltpu.HBM)
        elif k in pinned:
            operands[k] = pltpu.with_memory_space_constraint(operands[k], pltpu.VMEM)
    return pl.pallas_call(
        kernel,
        in_specs=[smem] * scalars + [vmem] * (kept - scalars) + [hbm] * fetched,
        out_specs=[vmem] * len(outs),
        out_shape=outs,
        scratch_shapes=list(scratch),
        compiler_params=pltpu.CompilerParams(vmem_limit_bytes=VMEM_LIMIT),
        name=name,
    )(*operands)


def start_copies(pairs, sems):
    copies = [pltpu.make_async_copy(a, b, sems.at[k]) for k, (a, b) in enumerate(pairs)]
    for copy in copies:
        copy.start()
    return copies


def project_kernel(
    row_len, chunks, rows_hbm, wq_hbm, theirs_ref, kept_ref, rows_ref, wq_ref, acc_ref, sq_ref, sems
):
    many = rows_ref.shape[0] // chunks
    depth = wq_ref.shape[0] // WEIGHT_COPIES
    pieces = [(wq_hbm, wq_ref, k * depth, depth) for k in range(WEIGHT_COPIES)]
    pieces += [(rows_hbm, rows_ref, k * many, many) for k in range(chunks)]
    copies = start_copies(
        [(a.at[pl.ds(first, n)], b.at[pl.ds(first, n)]) for a, b, first, n in pieces], sems
    )
    chunk = many // row_len
    width = wq_ref.shape[1] // CORES
    heads = width // HD
    pairs = row_len // PAIR
    each = kept_ref.shape[0] // pairs
    body = each - 8
    seqs = body // (heads * PAIR)
    core = lax.axis_index("tc")
    across = lax.broadcasted_iota(jnp.int32, (chunk, HD), 0)
    lane = lax.broadcasted_iota(jnp.int32, (chunk, HD), 1)
    squares = [jnp.zeros((1, HD), F32) for _ in range(pairs)]
    for copy in copies[:WEIGHT_COPIES]:
        copy.wait()
    for step in range(chunks):
        copies[WEIGHT_COPIES + step].wait()
        rows = rows_ref[step * many : (step + 1) * many, :]
        for turn, (half, out_ref) in enumerate([(1 - core, theirs_ref), (core, kept_ref)]):
            columns = pl.ds(pl.multiple_of(half * width, width), width)
            product = mm(rows, wq_ref[:, columns])
            slab = (step * 2 + turn) * heads * many
            for h in range(heads):
                acc_ref[slab + h * many : slab + (h + 1) * many, :] = product[
                    :, h * HD : (h + 1) * HD
                ]
            for t in range(row_len):
                for h in range(heads):
                    first = (t // PAIR) * each + (h * PAIR + t % PAIR) * seqs + step * chunk
                    out_ref[first : first + chunk, :] = acc_ref[
                        rows_at(slab + h * many + t, chunk, row_len), :
                    ]
        wide_rows = rows.astype(F32)
        sums = jnp.sum(wide_rows * wide_rows, axis=1, keepdims=True)
        sq_ref[step * many : (step + 1) * many, :] = jnp.broadcast_to(sums, (many, HD))
        for t in range(row_len):
            spot = lane == across + ((t % PAIR) * seqs + step * chunk)
            picked = jnp.where(spot, sq_ref[rows_at(step * many + t, chunk, row_len), :], 0.0)
            squares[t // PAIR] += jnp.sum(picked, axis=0, keepdims=True)
    for p in range(pairs):
        tail = jnp.broadcast_to(squares[p], (8, HD))
        for out_ref in (theirs_ref, kept_ref):
            out_ref[p * each + body : (p + 1) * each, :] = tail


def add_kernel(a_ref, b_ref, out_ref):
    out_ref[...] = a_ref[...] + b_ref[...]


def decode_kernel(
    lens_hbm,
    q_hbm,
    nk_hbm,
    nv_hbm,
    route_hbm,
    score_hbm,
    delta_hbm,
    k_hbm,
    v_hbm,
    w_hbm,
    attn_ref,
    out_ref,
    place_ref,
    tile_ref,
    delta_ref,
    lens_ref,
    q_ref,
    nk_ref,
    nv_ref,
    route_ref,
    score_ref,
    k_ref,
    v_ref,
    w_ref,
    sems,
):
    w_cols = w_ref.shape[1] // WEIGHT_COPIES
    copies = start_copies(
        [
            (lens_hbm, lens_ref),
            (q_hbm, q_ref),
            (nk_hbm, nk_ref),
            (nv_hbm, nv_ref),
            (route_hbm, route_ref),
            (score_hbm, score_ref),
            (delta_hbm, delta_ref),
            (k_hbm, k_ref),
            (v_hbm, v_ref),
        ]
        + [
            (w_hbm.at[:, pl.ds(c, w_cols)], w_ref.at[:, pl.ds(c, w_cols)])
            for c in range(0, w_ref.shape[1], w_cols)
        ],
        sems,
    )
    for copy in copies[:-WEIGHT_COPIES]:
        copy.wait()
    seqs = q_ref.shape[0]
    rows = 2 * seqs
    scale = 1.0 / math.sqrt(HD)
    q = q_ref[...].astype(F32)
    queries = jnp.concatenate([q[:, :HD], q[:, HD:]], axis=0)
    nk = nk_ref[...].astype(F32)
    nv = nv_ref[...].astype(F32)
    own_key = jnp.concatenate([nk, nk], axis=0)
    own_value = jnp.concatenate([nv, nv], axis=0)
    row = lax.broadcasted_iota(jnp.int32, (rows, HD), 0) % seqs
    place_in = lax.broadcasted_iota(jnp.int32, (rows, HD), 1)
    queries16 = queries.astype(BF16)
    scores = jnp.zeros((rows, HD), F32)
    length = jnp.zeros((rows, HD), jnp.int32)
    for s in range(seqs):
        scores = jnp.where(row == s, mm_t(queries16, k_ref[s]), scores)
        length = jnp.where(row == s, lens_ref[s], length)
    scores = jnp.where(place_in < length, scores * scale, -jnp.inf)
    own_score = jnp.sum(queries * own_key, axis=1, keepdims=True) * scale
    highest = jnp.maximum(jnp.max(scores, axis=1, keepdims=True), own_score)
    weights = jnp.exp(scores - highest)
    own_weight = jnp.exp(own_score - highest)
    denominator = jnp.sum(weights, axis=1, keepdims=True) + own_weight
    probs = (weights / denominator).astype(BF16)
    own_prob = (own_weight / denominator).astype(BF16).astype(F32)
    mixed = jnp.zeros((rows, HD), F32)
    for s in range(seqs):
        mixed = jnp.where(row == s, mm(probs, v_ref[s]), mixed)
    attn = (mixed + own_prob * own_value).astype(BF16).astype(F32)
    attn_ref[...] = attn
    turned = jnp.concatenate([attn[seqs:], attn[:seqs]], axis=0)
    both = jnp.concatenate([attn, turned], axis=1).astype(BF16)
    blocks = w_ref.shape[1] // HD
    for copy in copies[-WEIGHT_COPIES:]:
        copy.wait()
    for first in range(0, blocks, 4):
        part = mm(both, w_ref[:, first * HD : (first + 4) * HD])
        for c in range(4):
            out_ref[(first + c) * rows : (first + c + 1) * rows, :] = part[:, c * HD : (c + 1) * HD]
    slots = place_ref.shape[0]
    groups = slots // CAP
    down = lax.broadcasted_iota(jnp.int32, (HD, HD), 0)
    across = lax.broadcasted_iota(jnp.int32, (HD, HD), 1)
    target = jnp.broadcast_to(route_ref[...], (HD, HD))
    target_down = jnp.sum(jnp.where(down == across, target, 0.0), axis=1, keepdims=True)
    earlier = jnp.where(jnp.logical_and(target == target_down, down < across), 1.0, 0.0)
    rank = jnp.sum(earlier, axis=0, keepdims=True)
    slot = lax.broadcasted_iota(jnp.int32, (slots, HD), 0)
    group = (slot % groups).astype(F32)
    order = (slot // groups).astype(F32)
    held = jnp.logical_and(route_ref[...] == group, rank == order)
    place_ref[...] = jnp.where(held, 1.0, 0.0).astype(BF16)
    weight = score_ref[...].astype(F32)
    heads = weight.shape[0] // CORES
    weight = jnp.where(lax.axis_index("tc") == 0, weight[:heads], weight[heads:])
    for h in range(heads):
        own = slice(h * rows // heads, (h + 1) * rows // heads)
        tile_ref[own, :] = jnp.broadcast_to(weight[h : h + 1], (rows // heads, HD))


def place_kernel(sources, x_ref, attn_ref, place_ref, out_ref, lay_ref):
    each = x_ref.shape[0] // sources
    body = each - 8
    groups = place_ref.shape[0] // CAP
    tile = out_ref.shape[1] - attn_ref.shape[0]
    lay = tile // 2
    parts = lay // CAP
    heads = parts // PAIR
    seqs = body // parts
    total = x_ref[0:each, :]
    for k in range(1, sources):
        total = total + x_ref[k * each : (k + 1) * each, :]
    inverse = lax.rsqrt(total[body : body + 1, :] / RD + 1e-05) * (math.log2(math.e) / math.sqrt(HD))
    down = lax.broadcasted_iota(jnp.int32, (HD, HD), 0)
    across = lax.broadcasted_iota(jnp.int32, (HD, HD), 1)
    factor = jnp.sum(jnp.where(down == across, inverse, 0.0), axis=1, keepdims=True)
    pieces = []
    for h in range(heads):
        for p in range(PAIR):
            first = (h * PAIR + p) * seqs
            pieces.append(total[first : first + seqs, :] * factor[p * seqs : (p + 1) * seqs, :])
    normed = jnp.concatenate(pieces, axis=1)
    if seqs < HD:
        normed = jnp.concatenate([normed, jnp.zeros((HD - seqs, parts * HD), F32)], axis=0)
    place = place_ref[...]
    for k, term in enumerate(split2(normed)):
        placed = mm(place, term)
        for r in range(CAP):
            for q in range(parts):
                row = k * lay + (q // PAIR) * CAP * PAIR + r * PAIR + q % PAIR
                lay_ref[rows_at(row, groups, tile), :] = placed[
                    r * groups : (r + 1) * groups, q * HD : (q + 1) * HD
                ]
    attn = jnp.broadcast_to(attn_ref[...].astype(BF16)[None], (groups,) + attn_ref.shape)
    out_ref[:, :tile, :] = lay_ref[...].reshape(groups, tile, HD).astype(BF16)
    out_ref[:, tile:, :] = attn


def score_kernel(index_ref, x_ref, keys_ref, values_ref, weight_ref, delta_ref, out_ref):
    tile = out_ref.shape[1]
    seqs = tile // 2
    senders = x_ref.shape[0]
    keys = keys_ref[...]
    keys2 = jnp.concatenate([keys, keys], axis=1)
    values = values_ref[...]
    weight = weight_ref[...][None]
    delta = delta_ref[...]
    block = index_ref[0]
    columns = 32
    row_block = block // columns
    column = (block % columns).astype(F32)
    at_once = min(16, senders)
    row = lax.broadcasted_iota(jnp.int32, (1, tile, HD), 1)
    lane = lax.broadcasted_iota(jnp.int32, (1, tile, HD), 2)
    named = jnp.logical_and(row == seqs, lane == HD - 1)
    for first in range(0, senders, at_once):
        x = x_ref[first : first + at_once].astype(F32)
        flat = [
            x[:, k * tile : (k + 1) * tile, :].reshape(at_once * tile, HD).astype(BF16)
            for k in range(3)
        ]
        scores = mm_t(jnp.concatenate(flat[:2], axis=1), keys2)
        highest = jnp.max(scores, axis=1, keepdims=True)
        weights = jnp.exp2(scores - highest)
        probs = (weights * (1.0 / jnp.sum(weights, axis=1, keepdims=True))).astype(BF16)
        context = mm(probs, values)
        gated = context / (1.0 + jnp.exp(-context))
        terms = gated.reshape(at_once, tile, HD) * weight
        by_head = jnp.broadcast_to(jnp.sum(terms, axis=2, keepdims=True), terms.shape)
        score = by_head + jnp.concatenate([by_head[:, seqs:], by_head[:, :seqs]], axis=1)
        product = mm(flat[2], delta).reshape(at_once, tile, HD)
        turned = jnp.concatenate([product[:, seqs:], product[:, :seqs]], axis=1)
        result = jnp.where(row_block == 0, product, turned)
        result = jnp.where(row < seqs, result, jnp.where(named, column, score))
        out_ref[first : first + at_once] = result


def merge_kernel(tile, x_ref, partial_ref, place_ref, out_ref):
    senders = x_ref.shape[0] // tile
    blocks = partial_ref.shape[0] // tile
    seqs = tile // 2
    column = x_ref[rows_at(seqs, senders, tile), :][:, HD - 1 :]
    pieces = split3(
        jnp.concatenate([x_ref[rows_at(s, senders, tile), :] for s in range(seqs)], axis=1)
    )
    down = lax.broadcasted_iota(jnp.int32, (senders, senders), 0)
    across = lax.broadcasted_iota(jnp.int32, (senders, senders), 1)
    column_across = jnp.sum(
        jnp.where(down == across, jnp.broadcast_to(column, (senders, senders)), 0.0),
        axis=0,
        keepdims=True,
    )
    wanted = lax.broadcasted_iota(jnp.int32, (blocks, senders), 0).astype(F32)
    pick = jnp.where(wanted == column_across, 1.0, 0.0).astype(BF16)
    high, mid, low = pieces
    added = (mm(pick, low) + mm(pick, mid)) + mm(pick, high)
    out_ref[...] = partial_ref[...]
    for s in range(seqs):
        where = rows_at(s, blocks, tile)
        out_ref[where, :] = partial_ref[where, :] + added[:, s * HD : (s + 1) * HD]
    place = place_ref[...].astype(F32)
    shards = 8
    for p in range(PAIR):
        score = jnp.concatenate(
            [x_ref[rows_at(seqs + r * PAIR + p, senders, tile), :] for r in range(CAP)], axis=0
        )[:, :1]
        back = jnp.sum(place * score, axis=0, keepdims=True)
        out_ref[rows_at(seqs + p, shards, blocks // shards * tile), :] = jnp.broadcast_to(
            back, (shards, HD)
        )


def final_kernel(tile, x_ref, length_ref, decoded_ref, rewards_ref):
    seqs = tile // 2
    total = x_ref[0]
    for k in range(1, x_ref.shape[0]):
        total = total + x_ref[k]
    for c in range(total.shape[0] // tile):
        decoded_ref[:, c * HD : (c + 1) * HD] = total[c * tile : c * tile + seqs, :].astype(BF16)
    length = length_ref[...]
    count = rewards_ref.shape[1]
    reward = jnp.zeros((1, HD), F32)
    for k in range(x_ref.shape[0]):
        for p in range(PAIR):
            token = k // CORES * PAIR + p
            row = x_ref[k, seqs + p : seqs + p + 1, :]
            reward = reward + jnp.where(length > token, row, 0.0)
    rewards_ref[...] = (reward / length)[:, :count]


def per_device(
    query,
    key_cache,
    value_cache,
    new_key,
    new_value,
    cache_lengths,
    out_weight,
    delta_index,
    delta_values,
    fin_route,
    fin_lengths,
    fin_rows,
    reward_query,
    rubric_keys,
    rubric_values,
    score_weight,
):
    wide_count = lax.axis_size("wide")
    chips = lax.axis_size("th")
    tp_count = chips * lax.axis_size("tc")
    finished, row_len, features = fin_rows.shape
    heads = reward_query.shape[1] // HD // CORES
    seq_count = query.shape[0]
    tile = 2 * seq_count
    blocks = out_weight.shape[1] // HD
    slots = CAP * wide_count
    parts = PAIR * heads
    message = parts * finished + 8
    chunks = 4 if finished % 32 == 0 else 1
    shape = jax.ShapeDtypeStruct

    rows = fin_rows.reshape(finished * row_len, features)
    partial = shape((chips * message, HD), F32)
    theirs, kept = local_call(
        functools.partial(project_kernel, row_len, chunks),
        "project",
        (rows, reward_query),
        [partial, partial],
        [
            pltpu.VMEM(rows.shape, BF16),
            pltpu.VMEM(reward_query.shape, BF16),
            pltpu.VMEM((CORES * heads * finished * row_len, HD), F32),
            pltpu.VMEM((finished * row_len, HD), F32),
            pltpu.SemaphoreType.DMA((WEIGHT_COPIES + chunks,)),
        ],
        fetched=2,
    )
    got = lax.ppermute(theirs, "tc", [(0, 1), (1, 0)])
    (both,) = local_call(add_kernel, "add", (kept, got), [partial])
    summed_tokens = lax.all_to_all(
        both.reshape(chips, message, HD), "th", split_axis=0, concat_axis=0, tiled=True
    ).reshape(partial.shape)

    pad = ((0, 0), (0, HD - finished))
    route = jnp.pad(fin_route.reshape(1, finished).astype(F32), pad, constant_values=-1.0)
    lengths = jnp.pad(fin_lengths.reshape(1, finished).astype(F32), pad, constant_values=1.0)
    weights = score_weight.reshape(heads * CORES, HD)
    small = (cache_lengths, query, new_key, new_value, route, weights, delta_values[0])
    large = (key_cache, value_cache, out_weight)
    attn, partial_out, place, weight_tile, delta = local_call(
        decode_kernel,
        "decode",
        small + large,
        [
            shape((tile, HD), F32),
            shape((blocks * tile, HD), F32),
            shape((slots, HD), BF16),
            shape((tile, HD), F32),
            shape(delta_values.shape[1:], BF16),
        ],
        [pltpu.SMEM(cache_lengths.shape, jnp.int32)]
        + [pltpu.VMEM(a.shape, a.dtype) for a in small[1:-1] + large]
        + [pltpu.SemaphoreType.DMA((len(small) + 2 + WEIGHT_COPIES,))],
        fetched=len(small) + len(large),
    )

    lay = CAP * parts
    (outgoing,) = local_call(
        functools.partial(place_kernel, chips),
        "place",
        (summed_tokens, attn, place),
        [shape((wide_count, 2 * lay + tile, HD), BF16)],
        [pltpu.VMEM((wide_count * 2 * lay, HD), F32)],
    )
    received = lax.all_to_all(outgoing, "wide", split_axis=0, concat_axis=0, tiled=True)

    (answers,) = local_call(
        score_kernel,
        "score",
        (
            delta_index,
            received,
            rubric_keys[0],
            rubric_values[0],
            weight_tile,
            delta,
        ),
        [shape((wide_count, tile, HD), F32)],
        scalars=1,
    )
    returned = lax.all_to_all(answers, "wide", split_axis=0, concat_axis=0, tiled=True)

    (merged,) = local_call(
        functools.partial(merge_kernel, tile),
        "merge",
        (returned.reshape(wide_count * tile, HD), partial_out, place),
        [shape((blocks * tile, HD), F32)],
    )
    shares = lax.all_to_all(
        merged.reshape(tp_count, blocks // tp_count * tile, HD),
        ("th", "tc"),
        split_axis=0,
        concat_axis=0,
        tiled=True,
    )

    decoded, rewards = local_call(
        functools.partial(final_kernel, tile),
        "final",
        (shares, lengths),
        [shape((seq_count, blocks // tp_count * HD), BF16), shape((1, finished), F32)],
    )
    return decoded, rewards.reshape(finished)


def solution(mesh):
    tp = ("th", "tc")
    wide_count, tp_count = mesh.devices.shape
    split = jax.sharding.Mesh(
        mesh.devices.reshape(wide_count, tp_count // CORES, CORES), ("wide",) + tp
    )
    in_specs = (
        P("wide", tp),
        P("wide", None, tp),
        P("wide", None, tp),
        P("wide", tp),
        P("wide", tp),
        P("wide"),
        P(tp, None),
        P("wide"),
        P("wide", tp, None),
        P("wide", None),
        P("wide"),
        P("wide", None, tp),
        P(tp, None),
        P("wide", None, None),
        P("wide", None, None),
        P(),
    )
    out_specs = (P("wide", tp), P("wide"))
    return jax.shard_map(
        per_device, mesh=split, in_specs=in_specs, out_specs=out_specs, check_vma=False
    )
```

```python
import functools
import math

import jax
import jax.numpy as jnp
from jax import lax
from jax.experimental import pallas as pl
from jax.experimental.pallas import tpu as pltpu
from jax.sharding import PartitionSpec as P

HD = 128
RD = 8192
CAP = 2
CORES = 2
PAIR = 2
VMEM_LIMIT = 16 * 2**20
WEIGHT_COPIES = 4
AT_ONCE = 32
F32 = jnp.float32
BF16 = jnp.bfloat16


def split2(x):
    high = x.astype(BF16)
    return high, (x - high.astype(F32)).astype(BF16)


def split3(x):
    high, mid = split2(x)
    return high, mid, (x - high.astype(F32) - mid.astype(F32)).astype(BF16)


def mm(a, b):
    return jnp.dot(a, b, preferred_element_type=F32)


def mm_t(a, b):
    return lax.dot_general(a, b, (((1,), (1,)), ((), ())), preferred_element_type=F32)


def rows_at(first, count, stride):
    return pl.ds(first, count, stride=stride)


def local_call(kernel, name, operands, outs, scratch=(), scalars=0, fetched=0, pinned=()):
    vmem = pl.BlockSpec(memory_space=pltpu.VMEM)
    smem = pl.BlockSpec(memory_space=pltpu.SMEM)
    hbm = pl.BlockSpec(memory_space=pltpu.HBM)
    kept = len(operands) - fetched
    operands = list(operands)
    for k in range(len(operands)):
        if k >= kept:
            operands[k] = pltpu.with_memory_space_constraint(operands[k], pltpu.HBM)
        elif k in pinned:
            operands[k] = pltpu.with_memory_space_constraint(operands[k], pltpu.VMEM)
    return pl.pallas_call(
        kernel,
        in_specs=[smem] * scalars + [vmem] * (kept - scalars) + [hbm] * fetched,
        out_specs=[vmem] * len(outs),
        out_shape=outs,
        scratch_shapes=list(scratch),
        compiler_params=pltpu.CompilerParams(vmem_limit_bytes=VMEM_LIMIT),
        name=name,
    )(*operands)


def start_copies(pairs, sems):
    copies = [pltpu.make_async_copy(a, b, sems.at[k]) for k, (a, b) in enumerate(pairs)]
    for copy in copies:
        copy.start()
    return copies


def project_kernel(mine, row_len, chunks, *refs):
    if mine:
        squares_ref, rows_ref, wq_ref, out_ref, acc_ref = refs
    else:
        rows_hbm, wq_hbm, out_ref, squares_ref, rows_ref, wq_ref, acc_ref, sq_ref, sems = refs
    many = rows_ref.shape[0] // chunks
    depth = wq_ref.shape[0] // WEIGHT_COPIES
    width = wq_ref.shape[1] // CORES
    heads = width // HD
    core = lax.axis_index("tc")
    half = core if mine else 1 - core
    columns = pl.ds(pl.multiple_of(half * width, width), width)
    if not mine:
        pieces = [(wq_hbm, wq_ref, pl.ds(k * depth, depth)) for k in range(WEIGHT_COPIES)]
        pieces += [(rows_hbm, rows_ref, pl.ds(k * many, many)) for k in range(chunks)]
        copies = start_copies([(a.at[k], b.at[k]) for a, b, k in pieces], sems)
    chunk = many // row_len
    pairs = row_len // PAIR
    each = out_ref.shape[0] // pairs
    body = each - 8
    seqs = body // (heads * PAIR)
    across = lax.broadcasted_iota(jnp.int32, (chunk, HD), 0)
    lane = lax.broadcasted_iota(jnp.int32, (chunk, HD), 1)
    squares = [jnp.zeros((1, HD), F32) for _ in range(pairs)]
    if not mine:
        for copy in copies[:WEIGHT_COPIES]:
            copy.wait()
    for step in range(chunks):
        if not mine:
            copies[WEIGHT_COPIES + step].wait()
        rows = rows_ref[step * many : (step + 1) * many, :]
        product = mm(rows, wq_ref[:, columns])
        slab = step * heads * many
        for h in range(heads):
            acc_ref[slab + h * many : slab + (h + 1) * many, :] = product[:, h * HD : (h + 1) * HD]
        for t in range(row_len):
            for h in range(heads):
                first = (t // PAIR) * each + (h * PAIR + t % PAIR) * seqs + step * chunk
                out_ref[first : first + chunk, :] = acc_ref[
                    rows_at(slab + h * many + t, chunk, row_len), :
                ]
        if mine:
            continue
        wide_rows = rows.astype(F32)
        sums = jnp.sum(wide_rows * wide_rows, axis=1, keepdims=True)
        sq_ref[step * many : (step + 1) * many, :] = jnp.broadcast_to(sums, (many, HD))
        for t in range(row_len):
            spot = lane == across + ((t % PAIR) * seqs + step * chunk)
            picked = jnp.where(spot, sq_ref[rows_at(step * many + t, chunk, row_len), :], 0.0)
            squares[t // PAIR] += jnp.sum(picked, axis=0, keepdims=True)
    for p in range(pairs):
        if mine:
            tail = squares_ref[p * 8 : (p + 1) * 8, :]
        else:
            tail = jnp.broadcast_to(squares[p], (8, HD))
            squares_ref[p * 8 : (p + 1) * 8, :] = tail
        out_ref[p * each + body : (p + 1) * each, :] = tail


def add_kernel(a_ref, b_ref, out_ref):
    out_ref[...] = a_ref[...] + b_ref[...]


def decode_kernel(
    lens_hbm,
    q_hbm,
    nk_hbm,
    nv_hbm,
    route_hbm,
    score_hbm,
    delta_hbm,
    k_hbm,
    v_hbm,
    w_hbm,
    attn_ref,
    out_ref,
    place_ref,
    tile_ref,
    delta_ref,
    lens_ref,
    q_ref,
    nk_ref,
    nv_ref,
    route_ref,
    score_ref,
    k_ref,
    v_ref,
    w_ref,
    sems,
):
    w_cols = w_ref.shape[1] // WEIGHT_COPIES
    copies = start_copies(
        [
            (lens_hbm, lens_ref),
            (q_hbm, q_ref),
            (nk_hbm, nk_ref),
            (nv_hbm, nv_ref),
            (route_hbm, route_ref),
            (score_hbm, score_ref),
            (delta_hbm, delta_ref),
            (k_hbm, k_ref),
            (v_hbm, v_ref),
        ]
        + [
            (w_hbm.at[:, pl.ds(c, w_cols)], w_ref.at[:, pl.ds(c, w_cols)])
            for c in range(0, w_ref.shape[1], w_cols)
        ],
        sems,
    )
    for copy in copies[:-WEIGHT_COPIES]:
        copy.wait()
    seqs = q_ref.shape[0]
    rows = 2 * seqs
    scale = 1.0 / math.sqrt(HD)
    q = q_ref[...].astype(F32)
    queries = jnp.concatenate([q[:, :HD], q[:, HD:]], axis=0)
    nk = nk_ref[...].astype(F32)
    nv = nv_ref[...].astype(F32)
    own_key = jnp.concatenate([nk, nk], axis=0)
    own_value = jnp.concatenate([nv, nv], axis=0)
    row = lax.broadcasted_iota(jnp.int32, (rows, HD), 0) % seqs
    place_in = lax.broadcasted_iota(jnp.int32, (rows, HD), 1)
    queries16 = queries.astype(BF16)
    scores = jnp.zeros((rows, HD), F32)
    length = jnp.zeros((rows, HD), jnp.int32)
    for s in range(seqs):
        scores = jnp.where(row == s, mm_t(queries16, k_ref[s]), scores)
        length = jnp.where(row == s, lens_ref[s], length)
    scores = jnp.where(place_in < length, scores * scale, -jnp.inf)
    own_score = jnp.sum(queries * own_key, axis=1, keepdims=True) * scale
    highest = jnp.maximum(jnp.max(scores, axis=1, keepdims=True), own_score)
    weights = jnp.exp(scores - highest)
    own_weight = jnp.exp(own_score - highest)
    denominator = jnp.sum(weights, axis=1, keepdims=True) + own_weight
    probs = (weights / denominator).astype(BF16)
    own_prob = (own_weight / denominator).astype(BF16).astype(F32)
    mixed = jnp.zeros((rows, HD), F32)
    for s in range(seqs):
        mixed = jnp.where(row == s, mm(probs, v_ref[s]), mixed)
    attn = (mixed + own_prob * own_value).astype(BF16).astype(F32)
    attn_ref[...] = attn
    turned = jnp.concatenate([attn[seqs:], attn[:seqs]], axis=0)
    both = jnp.concatenate([attn, turned], axis=1).astype(BF16)
    blocks = w_ref.shape[1] // HD
    shards = blocks // 4
    for copy in copies[-WEIGHT_COPIES:]:
        copy.wait()
    for first in range(0, blocks, 4):
        part = mm(both, w_ref[:, first * HD : (first + 4) * HD])
        for c in range(4):
            own = rows_at(c * seqs * shards + first // 4, seqs, shards)
            out_ref[own, :] = part[:seqs, c * HD : (c + 1) * HD]
    slots = place_ref.shape[0]
    groups = slots // CAP
    down = lax.broadcasted_iota(jnp.int32, (HD, HD), 0)
    across = lax.broadcasted_iota(jnp.int32, (HD, HD), 1)
    target = jnp.broadcast_to(route_ref[...], (HD, HD))
    target_down = jnp.sum(jnp.where(down == across, target, 0.0), axis=1, keepdims=True)
    earlier = jnp.where(jnp.logical_and(target == target_down, down < across), 1.0, 0.0)
    rank = jnp.sum(earlier, axis=0, keepdims=True)
    slot = lax.broadcasted_iota(jnp.int32, (slots, HD), 0)
    group = (slot % groups).astype(F32)
    order = (slot // groups).astype(F32)
    held = jnp.logical_and(route_ref[...] == group, rank == order)
    place_ref[...] = jnp.where(held, 1.0, 0.0).astype(BF16)
    weight = score_ref[...].astype(F32)
    heads = weight.shape[0] // CORES
    weight = jnp.where(lax.axis_index("tc") == 0, weight[:heads], weight[heads:])
    for h in range(heads):
        own = slice(h * rows // heads, (h + 1) * rows // heads)
        tile_ref[own, :] = jnp.broadcast_to(weight[h : h + 1], (rows // heads, HD))


def place_kernel(sources, x_ref, attn_ref, place_ref, out_ref, lay_ref):
    each = x_ref.shape[0] // sources
    body = each - 8
    groups = place_ref.shape[0] // CAP
    tile = out_ref.shape[1] - attn_ref.shape[0]
    lay = tile // 2
    parts = lay // CAP
    heads = parts // PAIR
    seqs = body // parts
    total = x_ref[0:each, :]
    for k in range(1, sources):
        total = total + x_ref[k * each : (k + 1) * each, :]
    inverse = lax.rsqrt(total[body : body + 1, :] / RD + 1e-05) * (math.log2(math.e) / math.sqrt(HD))
    down = lax.broadcasted_iota(jnp.int32, (HD, HD), 0)
    across = lax.broadcasted_iota(jnp.int32, (HD, HD), 1)
    factor = jnp.sum(jnp.where(down == across, inverse, 0.0), axis=1, keepdims=True)
    pieces = []
    for h in range(heads):
        for p in range(PAIR):
            first = (h * PAIR + p) * seqs
            pieces.append(total[first : first + seqs, :] * factor[p * seqs : (p + 1) * seqs, :])
    normed = jnp.concatenate(pieces, axis=1)
    if seqs < HD:
        normed = jnp.concatenate([normed, jnp.zeros((HD - seqs, parts * HD), F32)], axis=0)
    place = place_ref[...]
    for k, term in enumerate(split2(normed)):
        placed = mm(place, term)
        for r in range(CAP):
            for q in range(parts):
                row = k * lay + (q // PAIR) * CAP * PAIR + r * PAIR + q % PAIR
                lay_ref[rows_at(row, groups, tile), :] = placed[
                    r * groups : (r + 1) * groups, q * HD : (q + 1) * HD
                ]
    attn = jnp.broadcast_to(attn_ref[...].astype(BF16)[None], (groups,) + attn_ref.shape)
    out_ref[:, :tile, :] = lay_ref[...].reshape(groups, tile, HD).astype(BF16)
    out_ref[:, tile:, :] = attn


def score_kernel(
    seqs, index_ref, x_ref, keys_ref, values_ref, weight_ref, delta_ref, out_ref, lay_ref
):
    tile = 2 * seqs
    senders = x_ref.shape[0]
    keys = keys_ref[...]
    keys2 = jnp.concatenate([keys, keys], axis=1)
    values = values_ref[...]
    weight = weight_ref[...][None]
    delta = delta_ref[...]
    block = index_ref[0]
    columns = 32
    row_block = block // columns
    column = (block % columns).astype(F32)
    at_once = min(AT_ONCE, senders)
    row = lax.broadcasted_iota(jnp.int32, (1, tile, HD), 1)
    for first in range(0, senders, at_once):
        x = x_ref[first : first + at_once].astype(F32)
        flat = [
            x[:, k * tile : (k + 1) * tile, :].reshape(at_once * tile, HD).astype(BF16)
            for k in range(3)
        ]
        scores = mm_t(jnp.concatenate(flat[:2], axis=1), keys2)
        highest = jnp.max(scores, axis=1, keepdims=True)
        weights = jnp.exp2(scores - highest)
        probs = (weights * (1.0 / jnp.sum(weights, axis=1, keepdims=True))).astype(BF16)
        context = mm(probs, values)
        gated = context / (1.0 + jnp.exp(-context))
        terms = gated.reshape(at_once, tile, HD) * weight
        by_head = jnp.broadcast_to(jnp.sum(terms, axis=2, keepdims=True), terms.shape)
        score = by_head + jnp.concatenate([by_head[:, seqs:], by_head[:, :seqs]], axis=1)
        product = mm(flat[2], delta).reshape(at_once, tile, HD)
        turned = jnp.concatenate([product[:, seqs:], product[:, :seqs]], axis=1)
        result = jnp.where(row_block == 0, product, turned)
        result = jnp.where(row < seqs, result, score)
        span = slice(first * tile, (first + at_once) * tile)
        lay_ref[span, :] = result.reshape(at_once * tile, HD)
    for q in range(seqs):
        out_ref[rows_at(q, senders, seqs + 1), :] = lay_ref[rows_at(q, senders, tile), :]
    lane = lax.broadcasted_iota(jnp.int32, (senders, HD), 1)
    last = jnp.broadcast_to(column, (senders, HD))
    for q in range(seqs):
        last = jnp.where(lane == q, lay_ref[rows_at(seqs + q, senders, tile), :], last)
    out_ref[rows_at(seqs, senders, seqs + 1), :] = last


def merge_kernel(seqs, shards, x_ref, partial_ref, place_ref, out_ref):
    each = seqs + 1
    senders = x_ref.shape[0] // each
    blocks = partial_ref.shape[0] // seqs
    own_blocks = blocks // shards
    message = out_ref.shape[0] // shards
    last = x_ref[rows_at(seqs, senders, each), :]
    column = last[:, HD - 1 :]
    pieces = split3(
        jnp.concatenate([x_ref[rows_at(s, senders, each), :] for s in range(seqs)], axis=1)
    )
    down = lax.broadcasted_iota(jnp.int32, (senders, senders), 0)
    across = lax.broadcasted_iota(jnp.int32, (senders, senders), 1)
    column_across = jnp.sum(
        jnp.where(down == across, jnp.broadcast_to(column, (senders, senders)), 0.0),
        axis=0,
        keepdims=True,
    )
    order = lax.broadcasted_iota(jnp.int32, (blocks, senders), 0)
    wanted = (order % shards * own_blocks + order // shards).astype(F32)
    pick = jnp.where(wanted == column_across, 1.0, 0.0).astype(BF16)
    high, mid, low = pieces
    added = (mm(pick, low) + mm(pick, mid)) + mm(pick, high)
    for c in range(own_blocks):
        for s in range(seqs):
            q = c * seqs + s
            out_ref[rows_at(q, shards, message), :] = (
                partial_ref[q * shards : (q + 1) * shards, :]
                + added[c * shards : (c + 1) * shards, s * HD : (s + 1) * HD]
            )
    place = place_ref[...].astype(F32)
    for p in range(PAIR):
        score = jnp.concatenate(
            [last[:, r * PAIR + p : r * PAIR + p + 1] for r in range(CAP)], axis=0
        )
        back = jnp.sum(place * score, axis=0, keepdims=True)
        out_ref[rows_at(own_blocks * seqs + p, shards, message), :] = jnp.broadcast_to(
            back, (shards, HD)
        )


def final_kernel(shards, x_ref, length_ref, decoded_ref, rewards_ref):
    each = x_ref.shape[0] // shards
    seqs = decoded_ref.shape[0]
    body = each - PAIR
    parts = [x_ref[k * each : (k + 1) * each, :] for k in range(shards)]
    total = parts[0]
    for part in parts[1:]:
        total = total + part
    for c in range(body // seqs):
        decoded_ref[:, c * HD : (c + 1) * HD] = total[c * seqs : (c + 1) * seqs, :].astype(BF16)
    length = length_ref[...]
    count = rewards_ref.shape[1]
    reward = jnp.zeros((1, HD), F32)
    for k in range(shards):
        for p in range(PAIR):
            token = k // CORES * PAIR + p
            row = parts[k][body + p : body + p + 1, :]
            reward = reward + jnp.where(length > token, row, 0.0)
    rewards_ref[...] = (reward / length)[:, :count]


def per_device(
    query,
    key_cache,
    value_cache,
    new_key,
    new_value,
    cache_lengths,
    out_weight,
    delta_index,
    delta_values,
    fin_route,
    fin_lengths,
    fin_rows,
    reward_query,
    rubric_keys,
    rubric_values,
    score_weight,
):
    wide_count = lax.axis_size("wide")
    chips = lax.axis_size("th")
    tp_count = chips * lax.axis_size("tc")
    finished, row_len, features = fin_rows.shape
    heads = reward_query.shape[1] // HD // CORES
    seq_count = query.shape[0]
    tile = 2 * seq_count
    blocks = out_weight.shape[1] // HD
    slots = CAP * wide_count
    parts = PAIR * heads
    message = parts * finished + 8
    chunks = 1
    shape = jax.ShapeDtypeStruct

    rows = fin_rows.reshape(finished * row_len, features)
    partial = shape((chips * message, HD), F32)
    squares_shape = shape((chips * 8, HD), F32)
    acc = pltpu.VMEM((heads * finished * row_len, HD), F32)
    theirs, squares, rows, weights = local_call(
        functools.partial(project_kernel, False, row_len, chunks),
        "project_theirs",
        (rows, reward_query),
        [partial, squares_shape, shape(rows.shape, BF16), shape(reward_query.shape, BF16)],
        [
            acc,
            pltpu.VMEM((finished * row_len, HD), F32),
            pltpu.SemaphoreType.DMA((WEIGHT_COPIES + chunks,)),
        ],
        fetched=2,
    )
    got = lax.ppermute(theirs, "tc", [(0, 1), (1, 0)])
    (kept,) = local_call(
        functools.partial(project_kernel, True, row_len, chunks),
        "project_kept",
        (squares, rows, weights),
        [partial],
        [acc],
    )
    (both,) = local_call(add_kernel, "add", (kept, got), [partial])
    summed_tokens = lax.all_to_all(
        both.reshape(chips, message, HD), "th", split_axis=0, concat_axis=0, tiled=True
    ).reshape(partial.shape)

    pad = ((0, 0), (0, HD - finished))
    route = jnp.pad(fin_route.reshape(1, finished).astype(F32), pad, constant_values=-1.0)
    lengths = jnp.pad(fin_lengths.reshape(1, finished).astype(F32), pad, constant_values=1.0)
    weights = score_weight.reshape(heads * CORES, HD)
    small = (cache_lengths, query, new_key, new_value, route, weights, delta_values[0])
    large = (key_cache, value_cache, out_weight)
    attn, partial_out, place, weight_tile, delta = local_call(
        decode_kernel,
        "decode",
        small + large,
        [
            shape((tile, HD), F32),
            shape((blocks * seq_count, HD), F32),
            shape((slots, HD), BF16),
            shape((tile, HD), F32),
            shape(delta_values.shape[1:], BF16),
        ],
        [pltpu.SMEM(cache_lengths.shape, jnp.int32)]
        + [pltpu.VMEM(a.shape, a.dtype) for a in small[1:-1] + large]
        + [pltpu.SemaphoreType.DMA((len(small) + 2 + WEIGHT_COPIES,))],
        fetched=len(small) + len(large),
    )

    lay = CAP * parts
    (outgoing,) = local_call(
        functools.partial(place_kernel, chips),
        "place",
        (summed_tokens, attn, place),
        [shape((wide_count, 2 * lay + tile, HD), BF16)],
        [pltpu.VMEM((wide_count * 2 * lay, HD), F32)],
    )
    received = lax.all_to_all(outgoing, "wide", split_axis=0, concat_axis=0, tiled=True)

    answer = seq_count + 1
    (answers,) = local_call(
        functools.partial(score_kernel, seq_count),
        "score",
        (
            delta_index,
            received,
            rubric_keys[0],
            rubric_values[0],
            weight_tile,
            delta,
        ),
        [shape((wide_count * answer, HD), F32)],
        [pltpu.VMEM((wide_count * tile, HD), F32)],
        scalars=1,
    )
    returned = lax.all_to_all(
        answers.reshape(wide_count, 1, answer * HD), "wide", split_axis=0, concat_axis=0, tiled=True
    ).reshape(answers.shape)

    share = blocks // tp_count * seq_count + PAIR
    (merged,) = local_call(
        functools.partial(merge_kernel, seq_count, tp_count),
        "merge",
        (returned, partial_out, place),
        [shape((tp_count * share, HD), F32)],
    )
    shares = lax.all_to_all(
        merged.reshape(tp_count, 1, share * HD),
        ("th", "tc"),
        split_axis=0,
        concat_axis=0,
        tiled=True,
    ).reshape(merged.shape)

    decoded, rewards = local_call(
        functools.partial(final_kernel, tp_count),
        "final",
        (shares, lengths),
        [shape((seq_count, blocks // tp_count * HD), BF16), shape((1, finished), F32)],
    )
    return decoded, rewards.reshape(finished)


def solution(mesh):
    tp = ("th", "tc")
    wide_count, tp_count = mesh.devices.shape
    split = jax.sharding.Mesh(
        mesh.devices.reshape(wide_count, tp_count // CORES, CORES), ("wide",) + tp
    )
    in_specs = (
        P("wide", tp),
        P("wide", None, tp),
        P("wide", None, tp),
        P("wide", tp),
        P("wide", tp),
        P("wide"),
        P(tp, None),
        P("wide"),
        P("wide", tp, None),
        P("wide", None),
        P("wide"),
        P("wide", None, tp),
        P(tp, None),
        P("wide", None, None),
        P("wide", None, None),
        P(),
    )
    out_specs = (P("wide", tp), P("wide"))
    return jax.shard_map(
        per_device, mesh=split, in_specs=in_specs, out_specs=out_specs, check_vma=False
    )
```

```python
import functools
import math

import jax
import jax.numpy as jnp
from jax import lax
from jax.experimental import pallas as pl
from jax.experimental.pallas import tpu as pltpu
from jax.sharding import PartitionSpec as P

HD = 128
RD = 8192
CAP = 2
CORES = 2
PAIR = 2
VMEM_LIMIT = 16 * 2**20
WEIGHT_COPIES = 4
AT_ONCE = 32
F32 = jnp.float32
BF16 = jnp.bfloat16


def split2(x):
    high = x.astype(BF16)
    return high, (x - high.astype(F32)).astype(BF16)


def split3(x):
    high, mid = split2(x)
    return high, mid, (x - high.astype(F32) - mid.astype(F32)).astype(BF16)


def mm(a, b):
    return jnp.dot(a, b, preferred_element_type=F32)


def mm_t(a, b):
    return lax.dot_general(a, b, (((1,), (1,)), ((), ())), preferred_element_type=F32)


def rows_at(first, count, stride):
    return pl.ds(first, count, stride=stride)


def local_call(kernel, name, operands, outs, scratch=(), fetched=0):
    vmem = pl.BlockSpec(memory_space=pltpu.VMEM)
    hbm = pl.BlockSpec(memory_space=pltpu.HBM)
    kept = len(operands) - fetched
    operands = list(operands[:kept]) + [
        pltpu.with_memory_space_constraint(a, pltpu.HBM) for a in operands[kept:]
    ]
    return pl.pallas_call(
        kernel,
        in_specs=[vmem] * kept + [hbm] * fetched,
        out_specs=[vmem] * len(outs),
        out_shape=outs,
        scratch_shapes=list(scratch),
        compiler_params=pltpu.CompilerParams(vmem_limit_bytes=VMEM_LIMIT),
        name=name,
    )(*operands)


def start_copies(pairs, sems):
    copies = [pltpu.make_async_copy(a, b, sems.at[k]) for k, (a, b) in enumerate(pairs)]
    for copy in copies:
        copy.start()
    return copies


def project_kernel(mine, row_len, chunks, *refs):
    if mine:
        squares_ref, rows_ref, wq_ref, out_ref, acc_ref = refs
    else:
        rows_hbm, wq_hbm, out_ref, squares_ref, rows_ref, wq_ref, acc_ref, sq_ref, sems = refs
    many = rows_ref.shape[0] // chunks
    depth = wq_ref.shape[0] // WEIGHT_COPIES
    width = wq_ref.shape[1] // CORES
    heads = width // HD
    core = lax.axis_index("tc")
    half = core if mine else 1 - core
    columns = pl.ds(pl.multiple_of(half * width, width), width)
    if not mine:
        kept = pl.ds(pl.multiple_of(core * width, width), width)
        weights = [pl.ds(k * depth, depth) for k in range(WEIGHT_COPIES)]
        pieces = [(wq_hbm.at[k, columns], wq_ref.at[k, columns]) for k in weights]
        pieces += [(rows_hbm, rows_ref)]
        pieces += [(wq_hbm.at[k, kept], wq_ref.at[k, kept]) for k in weights]
        copies = start_copies(pieces, sems)
    chunk = many // row_len
    pairs = row_len // PAIR
    each = out_ref.shape[0] // pairs
    body = each - 8
    seqs = body // (heads * PAIR)
    across = lax.broadcasted_iota(jnp.int32, (chunk, HD), 0)
    lane = lax.broadcasted_iota(jnp.int32, (chunk, HD), 1)
    squares = [jnp.zeros((1, HD), F32) for _ in range(pairs)]
    if not mine:
        for copy in copies[: WEIGHT_COPIES + 1]:
            copy.wait()
    for step in range(chunks):
        rows = rows_ref[step * many : (step + 1) * many, :]
        product = mm(rows, wq_ref[:, columns])
        slab = step * heads * many
        for h in range(heads):
            acc_ref[slab + h * many : slab + (h + 1) * many, :] = product[:, h * HD : (h + 1) * HD]
        for t in range(row_len):
            for h in range(heads):
                first = (t // PAIR) * each + (h * PAIR + t % PAIR) * seqs + step * chunk
                out_ref[first : first + chunk, :] = acc_ref[
                    rows_at(slab + h * many + t, chunk, row_len), :
                ]
        if mine:
            continue
        wide_rows = rows.astype(F32)
        sums = jnp.sum(wide_rows * wide_rows, axis=1, keepdims=True)
        sq_ref[step * many : (step + 1) * many, :] = jnp.broadcast_to(sums, (many, HD))
        for t in range(row_len):
            spot = lane == across + ((t % PAIR) * seqs + step * chunk)
            picked = jnp.where(spot, sq_ref[rows_at(step * many + t, chunk, row_len), :], 0.0)
            squares[t // PAIR] += jnp.sum(picked, axis=0, keepdims=True)
    if not mine:
        for copy in copies[WEIGHT_COPIES + 1 :]:
            copy.wait()
    for p in range(pairs):
        if mine:
            tail = squares_ref[p * 8 : (p + 1) * 8, :]
        else:
            tail = jnp.broadcast_to(squares[p], (8, HD))
            squares_ref[p * 8 : (p + 1) * 8, :] = tail
        out_ref[p * each + body : (p + 1) * each, :] = tail


def add_kernel(a_ref, b_ref, out_ref):
    out_ref[...] = a_ref[...] + b_ref[...]


def decode_kernel(
    lens_hbm,
    q_hbm,
    nk_hbm,
    nv_hbm,
    route_hbm,
    score_hbm,
    delta_hbm,
    k_hbm,
    v_hbm,
    w_hbm,
    attn_ref,
    out_ref,
    place_ref,
    tile_ref,
    delta_ref,
    length_ref,
    lens_ref,
    q_ref,
    nk_ref,
    nv_ref,
    route_ref,
    score_ref,
    k_ref,
    v_ref,
    w_ref,
    sems,
):
    w_cols = w_ref.shape[1] // WEIGHT_COPIES
    copies = start_copies(
        [
            (lens_hbm, lens_ref),
            (q_hbm, q_ref),
            (nk_hbm, nk_ref),
            (nv_hbm, nv_ref),
            (route_hbm, route_ref),
            (score_hbm, score_ref),
            (delta_hbm, delta_ref),
            (k_hbm, k_ref),
            (v_hbm, v_ref),
        ]
        + [
            (w_hbm.at[:, pl.ds(c, w_cols)], w_ref.at[:, pl.ds(c, w_cols)])
            for c in range(0, w_ref.shape[1], w_cols)
        ],
        sems,
    )
    for copy in copies[:-WEIGHT_COPIES]:
        copy.wait()
    seqs = q_ref.shape[0]
    rows = 2 * seqs
    scale = 1.0 / math.sqrt(HD)
    q = q_ref[...].astype(F32)
    queries = jnp.concatenate([q[:, :HD], q[:, HD:]], axis=0)
    nk = nk_ref[...].astype(F32)
    nv = nv_ref[...].astype(F32)
    own_key = jnp.concatenate([nk, nk], axis=0)
    own_value = jnp.concatenate([nv, nv], axis=0)
    row = lax.broadcasted_iota(jnp.int32, (rows, HD), 0) % seqs
    place_in = lax.broadcasted_iota(jnp.int32, (rows, HD), 1)
    queries16 = queries.astype(BF16)
    scores = jnp.zeros((rows, HD), F32)
    length = jnp.zeros((rows, HD), jnp.int32)
    for s in range(seqs):
        scores = jnp.where(row == s, mm_t(queries16, k_ref[s]), scores)
        length = jnp.where(row == s, lens_ref[s], length)
    scores = jnp.where(place_in < length, scores * scale, -jnp.inf)
    own_score = jnp.sum(queries * own_key, axis=1, keepdims=True) * scale
    highest = jnp.maximum(jnp.max(scores, axis=1, keepdims=True), own_score)
    weights = jnp.exp(scores - highest)
    own_weight = jnp.exp(own_score - highest)
    denominator = jnp.sum(weights, axis=1, keepdims=True) + own_weight
    probs = (weights / denominator).astype(BF16)
    own_prob = (own_weight / denominator).astype(BF16).astype(F32)
    mixed = jnp.zeros((rows, HD), F32)
    for s in range(seqs):
        mixed = jnp.where(row == s, mm(probs, v_ref[s]), mixed)
    attn = (mixed + own_prob * own_value).astype(BF16).astype(F32)
    attn_ref[...] = attn
    turned = jnp.concatenate([attn[seqs:], attn[:seqs]], axis=0)
    both = jnp.concatenate([attn, turned], axis=1).astype(BF16)
    blocks = w_ref.shape[1] // HD
    shards = blocks // 4
    for copy in copies[-WEIGHT_COPIES:]:
        copy.wait()
    for first in range(0, blocks, 4):
        part = mm(both, w_ref[:, first * HD : (first + 4) * HD])
        for c in range(4):
            own = rows_at(c * seqs * shards + first // 4, seqs, shards)
            out_ref[own, :] = part[:seqs, c * HD : (c + 1) * HD]
    slots = place_ref.shape[0]
    groups = slots // CAP
    down = lax.broadcasted_iota(jnp.int32, (HD, HD), 0)
    across = lax.broadcasted_iota(jnp.int32, (HD, HD), 1)
    route = route_ref[0:1, :]
    target = jnp.broadcast_to(route, (HD, HD))
    target_down = jnp.sum(jnp.where(down == across, target, 0.0), axis=1, keepdims=True)
    earlier = jnp.where(jnp.logical_and(target == target_down, down < across), 1.0, 0.0)
    rank = jnp.sum(earlier, axis=0, keepdims=True)
    slot = lax.broadcasted_iota(jnp.int32, (slots, HD), 0)
    group = (slot % groups).astype(F32)
    order = (slot // groups).astype(F32)
    held = jnp.logical_and(route == group, rank == order)
    place_ref[...] = jnp.where(held, 1.0, 0.0).astype(BF16)
    weight = score_ref[...].astype(F32)
    heads = weight.shape[0] // CORES
    weight = jnp.where(lax.axis_index("tc") == 0, weight[:heads], weight[heads:])
    for h in range(heads):
        own = slice(h * rows // heads, (h + 1) * rows // heads)
        tile_ref[own, :] = jnp.broadcast_to(weight[h : h + 1], (rows // heads, HD))
    block = jnp.broadcast_to(route_ref[2:3, :], (8, HD))
    row_block = jnp.floor(block / blocks)
    tile_ref[rows : rows + 8, :] = row_block
    tile_ref[rows + 8 : rows + 16, :] = block - row_block * blocks
    length_ref[...] = jnp.broadcast_to(route_ref[1:2, :], length_ref.shape)


def place_kernel(sources, x_ref, attn_ref, place_ref, out_ref, lay_ref):
    each = x_ref.shape[0] // sources
    body = each - 8
    groups = place_ref.shape[0] // CAP
    tile = out_ref.shape[1] - attn_ref.shape[0]
    lay = tile // 2
    parts = lay // CAP
    heads = parts // PAIR
    seqs = body // parts
    total = x_ref[0:each, :]
    for k in range(1, sources):
        total = total + x_ref[k * each : (k + 1) * each, :]
    inverse = lax.rsqrt(total[body : body + 1, :] / RD + 1e-05) * (math.log2(math.e) / math.sqrt(HD))
    down = lax.broadcasted_iota(jnp.int32, (HD, HD), 0)
    across = lax.broadcasted_iota(jnp.int32, (HD, HD), 1)
    factor = jnp.sum(jnp.where(down == across, inverse, 0.0), axis=1, keepdims=True)
    pieces = []
    for h in range(heads):
        for p in range(PAIR):
            first = (h * PAIR + p) * seqs
            pieces.append(total[first : first + seqs, :] * factor[p * seqs : (p + 1) * seqs, :])
    normed = jnp.concatenate(pieces, axis=1)
    if seqs < HD:
        normed = jnp.concatenate([normed, jnp.zeros((HD - seqs, parts * HD), F32)], axis=0)
    place = place_ref[...]
    for k, term in enumerate(split2(normed)):
        placed = mm(place, term)
        for r in range(CAP):
            for q in range(parts):
                row = k * lay + (q // PAIR) * CAP * PAIR + r * PAIR + q % PAIR
                lay_ref[rows_at(row, groups, tile), :] = placed[
                    r * groups : (r + 1) * groups, q * HD : (q + 1) * HD
                ]
    attn = jnp.broadcast_to(attn_ref[...].astype(BF16)[None], (groups,) + attn_ref.shape)
    out_ref[:, :tile, :] = lay_ref[...].reshape(groups, tile, HD).astype(BF16)
    out_ref[:, tile:, :] = attn


def score_kernel(
    seqs, x_ref, keys_ref, values_ref, weight_ref, delta_ref, out_ref, lay_ref
):
    tile = 2 * seqs
    senders = x_ref.shape[0]
    keys = keys_ref[...]
    keys2 = jnp.concatenate([keys, keys], axis=1)
    values = values_ref[...]
    weight = weight_ref[0:tile, :][None]
    row_block = weight_ref[tile : tile + 1, :][None]
    column = weight_ref[tile + 8 : tile + 9, :]
    delta = delta_ref[...]
    at_once = min(AT_ONCE, senders)
    row = lax.broadcasted_iota(jnp.int32, (1, tile, HD), 1)
    for first in range(0, senders, at_once):
        x = x_ref[first : first + at_once].astype(F32)
        flat = [
            x[:, k * tile : (k + 1) * tile, :].reshape(at_once * tile, HD).astype(BF16)
            for k in range(3)
        ]
        scores = mm_t(jnp.concatenate(flat[:2], axis=1), keys2)
        highest = jnp.max(scores, axis=1, keepdims=True)
        weights = jnp.exp2(scores - highest)
        probs = (weights * (1.0 / jnp.sum(weights, axis=1, keepdims=True))).astype(BF16)
        context = mm(probs, values)
        gated = context / (1.0 + jnp.exp(-context))
        terms = gated.reshape(at_once, tile, HD) * weight
        by_head = jnp.broadcast_to(jnp.sum(terms, axis=2, keepdims=True), terms.shape)
        score = by_head + jnp.concatenate([by_head[:, seqs:], by_head[:, :seqs]], axis=1)
        product = mm(flat[2], delta).reshape(at_once, tile, HD)
        turned = jnp.concatenate([product[:, seqs:], product[:, :seqs]], axis=1)
        result = jnp.where(row_block == 0.0, product, turned)
        result = jnp.where(row < seqs, result, score)
        span = slice(first * tile, (first + at_once) * tile)
        lay_ref[span, :] = result.reshape(at_once * tile, HD)
    for q in range(seqs):
        out_ref[rows_at(q, senders, seqs + 1), :] = lay_ref[rows_at(q, senders, tile), :]
    lane = lax.broadcasted_iota(jnp.int32, (senders, HD), 1)
    last = jnp.broadcast_to(column, (senders, HD))
    for q in range(seqs):
        last = jnp.where(lane == q, lay_ref[rows_at(seqs + q, senders, tile), :], last)
    out_ref[rows_at(seqs, senders, seqs + 1), :] = last


def merge_kernel(seqs, shards, x_ref, partial_ref, place_ref, out_ref):
    each = seqs + 1
    senders = x_ref.shape[0] // each
    blocks = partial_ref.shape[0] // seqs
    own_blocks = blocks // shards
    message = out_ref.shape[0] // shards
    last = x_ref[rows_at(seqs, senders, each), :]
    column = last[:, HD - 1 :]
    pieces = split3(
        jnp.concatenate([x_ref[rows_at(s, senders, each), :] for s in range(seqs)], axis=1)
    )
    down = lax.broadcasted_iota(jnp.int32, (senders, senders), 0)
    across = lax.broadcasted_iota(jnp.int32, (senders, senders), 1)
    column_across = jnp.sum(
        jnp.where(down == across, jnp.broadcast_to(column, (senders, senders)), 0.0),
        axis=0,
        keepdims=True,
    )
    order = lax.broadcasted_iota(jnp.int32, (blocks, senders), 0)
    wanted = (order % shards * own_blocks + order // shards).astype(F32)
    pick = jnp.where(wanted == column_across, 1.0, 0.0).astype(BF16)
    high, mid, low = pieces
    added = (mm(pick, low) + mm(pick, mid)) + mm(pick, high)
    for c in range(own_blocks):
        for s in range(seqs):
            q = c * seqs + s
            out_ref[rows_at(q, shards, message), :] = (
                partial_ref[q * shards : (q + 1) * shards, :]
                + added[c * shards : (c + 1) * shards, s * HD : (s + 1) * HD]
            )
    place = place_ref[...].astype(F32)
    for p in range(PAIR):
        score = jnp.concatenate(
            [last[:, r * PAIR + p : r * PAIR + p + 1] for r in range(CAP)], axis=0
        )
        back = jnp.sum(place * score, axis=0, keepdims=True)
        out_ref[rows_at(own_blocks * seqs + p, shards, message), :] = jnp.broadcast_to(
            back, (shards, HD)
        )


def final_kernel(shards, x_ref, length_ref, decoded_ref, rewards_ref):
    each = x_ref.shape[0] // shards
    seqs = decoded_ref.shape[0]
    body = each - PAIR
    parts = [x_ref[k * each : (k + 1) * each, :] for k in range(shards)]
    total = parts[0]
    for part in parts[1:]:
        total = total + part
    for c in range(body // seqs):
        decoded_ref[:, c * HD : (c + 1) * HD] = total[c * seqs : (c + 1) * seqs, :].astype(BF16)
    length = length_ref[0:1, :]
    count = rewards_ref.shape[1]
    reward = jnp.zeros((1, HD), F32)
    for k in range(shards):
        for p in range(PAIR):
            token = k // CORES * PAIR + p
            row = parts[k][body + p : body + p + 1, :]
            reward = reward + jnp.where(length > token, row, 0.0)
    rewards_ref[...] = (reward / length)[:, :count]


def per_device(
    query,
    key_cache,
    value_cache,
    new_key,
    new_value,
    cache_lengths,
    out_weight,
    delta_index,
    delta_values,
    fin_route,
    fin_lengths,
    fin_rows,
    reward_query,
    rubric_keys,
    rubric_values,
    score_weight,
):
    wide_count = lax.axis_size("wide")
    chips = lax.axis_size("th")
    tp_count = chips * lax.axis_size("tc")
    finished, row_len, features = fin_rows.shape
    heads = reward_query.shape[1] // HD // CORES
    seq_count = query.shape[0]
    tile = 2 * seq_count
    blocks = out_weight.shape[1] // HD
    slots = CAP * wide_count
    parts = PAIR * heads
    message = parts * finished + 8
    chunks = 1
    shape = jax.ShapeDtypeStruct

    rows = fin_rows.reshape(finished * row_len, features)
    partial = shape((chips * message, HD), F32)
    squares_shape = shape((chips * 8, HD), F32)
    acc = pltpu.VMEM((heads * finished * row_len, HD), F32)
    theirs, squares, rows, weights = local_call(
        functools.partial(project_kernel, False, row_len, chunks),
        "project_theirs",
        (rows, reward_query),
        [partial, squares_shape, shape(rows.shape, BF16), shape(reward_query.shape, BF16)],
        [
            acc,
            pltpu.VMEM((finished * row_len, HD), F32),
            pltpu.SemaphoreType.DMA((2 * WEIGHT_COPIES + 1,)),
        ],
        fetched=2,
    )
    got = lax.ppermute(theirs, "tc", [(0, 1), (1, 0)])
    (kept,) = local_call(
        functools.partial(project_kernel, True, row_len, chunks),
        "project_kept",
        (squares, rows, weights),
        [partial],
        [acc],
    )
    (both,) = local_call(add_kernel, "add", (kept, got), [partial])
    summed_tokens = lax.all_to_all(
        both.reshape(chips, message, HD), "th", split_axis=0, concat_axis=0, tiled=True
    ).reshape(partial.shape)

    pad = ((0, 0), (0, HD - finished))
    routing = jnp.concatenate(
        [
            jnp.pad(fin_route.reshape(1, finished), pad, constant_values=-1),
            jnp.pad(fin_lengths.reshape(1, finished), pad, constant_values=1),
            jnp.broadcast_to(delta_index.reshape(1, 1), (1, HD)),
        ]
    ).astype(F32)
    weights = score_weight.reshape(heads * CORES, HD)
    small = (cache_lengths, query, new_key, new_value, routing, weights, delta_values[0])
    large = (key_cache, value_cache, out_weight)
    attn, partial_out, place, weight_tile, delta, lengths = local_call(
        decode_kernel,
        "decode",
        small + large,
        [
            shape((tile, HD), F32),
            shape((blocks * seq_count, HD), F32),
            shape((slots, HD), BF16),
            shape((tile + 16, HD), F32),
            shape(delta_values.shape[1:], BF16),
            shape((8, HD), F32),
        ],
        [pltpu.SMEM(cache_lengths.shape, jnp.int32)]
        + [pltpu.VMEM(a.shape, a.dtype) for a in small[1:-1] + large]
        + [pltpu.SemaphoreType.DMA((len(small) + 2 + WEIGHT_COPIES,))],
        fetched=len(small) + len(large),
    )

    lay = CAP * parts
    (outgoing,) = local_call(
        functools.partial(place_kernel, chips),
        "place",
        (summed_tokens, attn, place),
        [shape((wide_count, 2 * lay + tile, HD), BF16)],
        [pltpu.VMEM((wide_count * 2 * lay, HD), F32)],
    )
    received = lax.all_to_all(outgoing, "wide", split_axis=0, concat_axis=0, tiled=True)

    answer = seq_count + 1
    (answers,) = local_call(
        functools.partial(score_kernel, seq_count),
        "score",
        (
            received,
            rubric_keys[0],
            rubric_values[0],
            weight_tile,
            delta,
        ),
        [shape((wide_count * answer, HD), F32)],
        [pltpu.VMEM((wide_count * tile, HD), F32)],
    )
    returned = lax.all_to_all(
        answers.reshape(wide_count, 1, answer * HD), "wide", split_axis=0, concat_axis=0, tiled=True
    ).reshape(answers.shape)

    share = blocks // tp_count * seq_count + PAIR
    (merged,) = local_call(
        functools.partial(merge_kernel, seq_count, tp_count),
        "merge",
        (returned, partial_out, place),
        [shape((tp_count * share, HD), F32)],
    )
    shares = lax.all_to_all(
        merged.reshape(tp_count, 1, share * HD),
        ("th", "tc"),
        split_axis=0,
        concat_axis=0,
        tiled=True,
    ).reshape(merged.shape)

    decoded, rewards = local_call(
        functools.partial(final_kernel, tp_count),
        "final",
        (shares, lengths),
        [shape((seq_count, blocks // tp_count * HD), BF16), shape((1, finished), F32)],
    )
    return decoded, rewards.reshape(finished)


def solution(mesh):
    tp = ("th", "tc")
    wide_count, tp_count = mesh.devices.shape
    split = jax.sharding.Mesh(
        mesh.devices.reshape(wide_count, tp_count // CORES, CORES), ("wide",) + tp
    )
    in_specs = (
        P("wide", tp),
        P("wide", None, tp),
        P("wide", None, tp),
        P("wide", tp),
        P("wide", tp),
        P("wide"),
        P(tp, None),
        P("wide"),
        P("wide", tp, None),
        P("wide", None),
        P("wide"),
        P("wide", None, tp),
        P(tp, None),
        P("wide", None, None),
        P("wide", None, None),
        P(),
    )
    out_specs = (P("wide", tp), P("wide"))
    return jax.shard_map(
        per_device, mesh=split, in_specs=in_specs, out_specs=out_specs, check_vma=False
    )
```

```python
import functools
import math

import jax
import jax.numpy as jnp
from jax import lax
from jax.experimental import pallas as pl
from jax.experimental.pallas import tpu as pltpu
from jax.sharding import PartitionSpec as P

HD = 128
RD = 8192
CAP = 2
CORES = 2
PAIR = 2
VMEM_LIMIT = 16 * 2**20
WEIGHT_COPIES = 4
FEATURE_COPIES = 2
AT_ONCE = 32
F32 = jnp.float32
BF16 = jnp.bfloat16


def split2(x):
    high = x.astype(BF16)
    return high, (x - high.astype(F32)).astype(BF16)


def split3(x):
    high, mid = split2(x)
    return high, mid, (x - high.astype(F32) - mid.astype(F32)).astype(BF16)


def mm(a, b):
    return jnp.dot(a, b, preferred_element_type=F32)


def mm_t(a, b):
    return lax.dot_general(a, b, (((1,), (1,)), ((), ())), preferred_element_type=F32)


def rows_at(first, count, stride):
    return pl.ds(first, count, stride=stride)


def local_call(kernel, name, operands, outs, scratch=(), fetched=0):
    vmem = pl.BlockSpec(memory_space=pltpu.VMEM)
    hbm = pl.BlockSpec(memory_space=pltpu.HBM)
    kept = len(operands) - fetched
    operands = list(operands[:kept]) + [
        pltpu.with_memory_space_constraint(a, pltpu.HBM) for a in operands[kept:]
    ]
    return pl.pallas_call(
        kernel,
        in_specs=[vmem] * kept + [hbm] * fetched,
        out_specs=[vmem] * len(outs),
        out_shape=outs,
        scratch_shapes=list(scratch),
        compiler_params=pltpu.CompilerParams(vmem_limit_bytes=VMEM_LIMIT),
        name=name,
    )(*operands)


def start_copies(pairs, sems):
    copies = [pltpu.make_async_copy(a, b, sems.at[k]) for k, (a, b) in enumerate(pairs)]
    for copy in copies:
        copy.start()
    return copies


def project_kernel(mine, row_len, *refs):
    if mine:
        squares_ref, rows_ref, wq_ref, out_ref, acc_ref = refs
    else:
        rows_hbm, wq_hbm, out_ref, squares_ref, rows_ref, wq_ref, acc_ref, sq_ref, sems = refs
    many = rows_ref.shape[0]
    width = wq_ref.shape[1] // CORES
    heads = width // HD
    core = lax.axis_index("tc")
    half = core if mine else 1 - core
    columns = pl.ds(pl.multiple_of(half * width, width), width)
    steps = 1 if mine else FEATURE_COPIES
    depth = wq_ref.shape[0] // steps
    spans = [pl.ds(k * depth, depth) for k in range(steps)]
    if not mine:
        kept = pl.ds(pl.multiple_of(core * width, width), width)
        pieces = []
        for k in spans:
            pieces += [(wq_hbm.at[k, columns], wq_ref.at[k, columns])]
            pieces += [(rows_hbm.at[:, k], rows_ref.at[:, k])]
        pieces += [(wq_hbm.at[:, kept], wq_ref.at[:, kept])]
        copies = start_copies(pieces, sems)
    chunk = many // row_len
    pairs = row_len // PAIR
    each = out_ref.shape[0] // pairs
    body = each - 8
    seqs = body // (heads * PAIR)
    product = sums = None
    for step, k in enumerate(spans):
        if not mine:
            copies[2 * step].wait()
            copies[2 * step + 1].wait()
        rows = rows_ref[:, k]
        part = mm(rows, wq_ref[k, columns])
        product = part if product is None else product + part
        if not mine:
            wide_rows = rows.astype(F32)
            wide_rows = wide_rows * wide_rows
            for first in range(0, depth, HD):
                slab = wide_rows[:, first : first + HD]
                sums = slab if sums is None else sums + slab
    for h in range(heads):
        acc_ref[h * many : (h + 1) * many, :] = product[:, h * HD : (h + 1) * HD]
    for t in range(row_len):
        for h in range(heads):
            first = (t // PAIR) * each + (h * PAIR + t % PAIR) * seqs
            out_ref[first : first + chunk, :] = acc_ref[rows_at(h * many + t, chunk, row_len), :]
    if mine:
        for p in range(pairs):
            tail = slice(p * each + body, (p + 1) * each)
            out_ref[tail, :] = squares_ref[p * 8 : (p + 1) * 8, :]
        return
    sq_ref[...] = jnp.broadcast_to(jnp.sum(sums, axis=1, keepdims=True), sq_ref.shape)
    across = lax.broadcasted_iota(jnp.int32, (chunk, HD), 0)
    lane = lax.broadcasted_iota(jnp.int32, (chunk, HD), 1)
    for p in range(pairs):
        total = jnp.zeros((1, HD), F32)
        for t in range(p * PAIR, (p + 1) * PAIR):
            spot = lane == across + (t % PAIR) * seqs
            picked = jnp.where(spot, sq_ref[rows_at(t, chunk, row_len), :], 0.0)
            total += jnp.sum(picked, axis=0, keepdims=True)
        tail = jnp.broadcast_to(total, (8, HD))
        squares_ref[p * 8 : (p + 1) * 8, :] = tail
        out_ref[p * each + body : (p + 1) * each, :] = tail
    copies[-1].wait()


def add_kernel(a_ref, b_ref, out_ref):
    out_ref[...] = a_ref[...] + b_ref[...]


def decode_kernel(
    lens_hbm,
    q_hbm,
    nk_hbm,
    nv_hbm,
    route_hbm,
    score_hbm,
    delta_hbm,
    k_hbm,
    v_hbm,
    w_hbm,
    attn_ref,
    out_ref,
    place_ref,
    tile_ref,
    delta_ref,
    length_ref,
    lens_ref,
    q_ref,
    nk_ref,
    nv_ref,
    route_ref,
    score_ref,
    k_ref,
    v_ref,
    w_ref,
    sems,
):
    w_cols = w_ref.shape[1] // WEIGHT_COPIES
    copies = start_copies(
        [
            (lens_hbm, lens_ref),
            (q_hbm, q_ref),
            (nk_hbm, nk_ref),
            (nv_hbm, nv_ref),
            (route_hbm, route_ref),
            (score_hbm, score_ref),
            (delta_hbm, delta_ref),
            (k_hbm, k_ref),
            (v_hbm, v_ref),
        ]
        + [
            (w_hbm.at[:, pl.ds(c, w_cols)], w_ref.at[:, pl.ds(c, w_cols)])
            for c in range(0, w_ref.shape[1], w_cols)
        ],
        sems,
    )
    for copy in copies[:-WEIGHT_COPIES]:
        copy.wait()
    seqs = q_ref.shape[0]
    rows = 2 * seqs
    scale = 1.0 / math.sqrt(HD)
    q = q_ref[...].astype(F32)
    queries = jnp.concatenate([q[:, :HD], q[:, HD:]], axis=0)
    nk = nk_ref[...].astype(F32)
    nv = nv_ref[...].astype(F32)
    own_key = jnp.concatenate([nk, nk], axis=0)
    own_value = jnp.concatenate([nv, nv], axis=0)
    row = lax.broadcasted_iota(jnp.int32, (rows, HD), 0) % seqs
    place_in = lax.broadcasted_iota(jnp.int32, (rows, HD), 1)
    queries16 = queries.astype(BF16)
    scores = jnp.zeros((rows, HD), F32)
    length = jnp.zeros((rows, HD), jnp.int32)
    for s in range(seqs):
        scores = jnp.where(row == s, mm_t(queries16, k_ref[s]), scores)
        length = jnp.where(row == s, lens_ref[s], length)
    scores = jnp.where(place_in < length, scores * scale, -jnp.inf)
    own_score = jnp.sum(queries * own_key, axis=1, keepdims=True) * scale
    highest = jnp.maximum(jnp.max(scores, axis=1, keepdims=True), own_score)
    weights = jnp.exp(scores - highest)
    own_weight = jnp.exp(own_score - highest)
    denominator = jnp.sum(weights, axis=1, keepdims=True) + own_weight
    probs = (weights / denominator).astype(BF16)
    own_prob = (own_weight / denominator).astype(BF16).astype(F32)
    mixed = jnp.zeros((rows, HD), F32)
    for s in range(seqs):
        mixed = jnp.where(row == s, mm(probs, v_ref[s]), mixed)
    attn = (mixed + own_prob * own_value).astype(BF16).astype(F32)
    attn_ref[...] = attn
    turned = jnp.concatenate([attn[seqs:], attn[:seqs]], axis=0)
    both = jnp.concatenate([attn, turned], axis=1).astype(BF16)
    blocks = w_ref.shape[1] // HD
    shards = blocks // 4
    for copy in copies[-WEIGHT_COPIES:]:
        copy.wait()
    for first in range(0, blocks, 4):
        part = mm(both, w_ref[:, first * HD : (first + 4) * HD])
        for c in range(4):
            own = rows_at(c * seqs * shards + first // 4, seqs, shards)
            out_ref[own, :] = part[:seqs, c * HD : (c + 1) * HD]
    slots = place_ref.shape[0]
    groups = slots // CAP
    down = lax.broadcasted_iota(jnp.int32, (HD, HD), 0)
    across = lax.broadcasted_iota(jnp.int32, (HD, HD), 1)
    route = route_ref[0:1, :]
    target = jnp.broadcast_to(route, (HD, HD))
    target_down = jnp.sum(jnp.where(down == across, target, 0.0), axis=1, keepdims=True)
    earlier = jnp.where(jnp.logical_and(target == target_down, down < across), 1.0, 0.0)
    rank = jnp.sum(earlier, axis=0, keepdims=True)
    slot = lax.broadcasted_iota(jnp.int32, (slots, HD), 0)
    group = (slot % groups).astype(F32)
    order = (slot // groups).astype(F32)
    held = jnp.logical_and(route == group, rank == order)
    place_ref[...] = jnp.where(held, 1.0, 0.0).astype(BF16)
    weight = score_ref[...].astype(F32)
    heads = weight.shape[0] // CORES
    weight = jnp.where(lax.axis_index("tc") == 0, weight[:heads], weight[heads:])
    for h in range(heads):
        own = slice(h * rows // heads, (h + 1) * rows // heads)
        tile_ref[own, :] = jnp.broadcast_to(weight[h : h + 1], (rows // heads, HD))
    block = jnp.broadcast_to(route_ref[2:3, :], (8, HD))
    row_block = jnp.floor(block / blocks)
    tile_ref[rows : rows + 8, :] = row_block
    tile_ref[rows + 8 : rows + 16, :] = block - row_block * blocks
    length_ref[...] = jnp.broadcast_to(route_ref[1:2, :], length_ref.shape)


def place_kernel(sources, x_ref, attn_ref, place_ref, out_ref, lay_ref):
    each = x_ref.shape[0] // sources
    body = each - 8
    groups = place_ref.shape[0] // CAP
    tile = out_ref.shape[1] - attn_ref.shape[0]
    lay = tile // 2
    parts = lay // CAP
    heads = parts // PAIR
    seqs = body // parts
    total = x_ref[0:each, :]
    for k in range(1, sources):
        total = total + x_ref[k * each : (k + 1) * each, :]
    inverse = lax.rsqrt(total[body : body + 1, :] / RD + 1e-05) * (math.log2(math.e) / math.sqrt(HD))
    down = lax.broadcasted_iota(jnp.int32, (HD, HD), 0)
    across = lax.broadcasted_iota(jnp.int32, (HD, HD), 1)
    factor = jnp.sum(jnp.where(down == across, inverse, 0.0), axis=1, keepdims=True)
    pieces = []
    for h in range(heads):
        for p in range(PAIR):
            first = (h * PAIR + p) * seqs
            pieces.append(total[first : first + seqs, :] * factor[p * seqs : (p + 1) * seqs, :])
    normed = jnp.concatenate(pieces, axis=1)
    if seqs < HD:
        normed = jnp.concatenate([normed, jnp.zeros((HD - seqs, parts * HD), F32)], axis=0)
    place = place_ref[...]
    for k, term in enumerate(split2(normed)):
        placed = mm(place, term)
        for r in range(CAP):
            for q in range(parts):
                row = k * lay + (q // PAIR) * CAP * PAIR + r * PAIR + q % PAIR
                lay_ref[rows_at(row, groups, tile), :] = placed[
                    r * groups : (r + 1) * groups, q * HD : (q + 1) * HD
                ]
    attn = jnp.broadcast_to(attn_ref[...].astype(BF16)[None], (groups,) + attn_ref.shape)
    out_ref[:, :tile, :] = lay_ref[...].reshape(groups, tile, HD).astype(BF16)
    out_ref[:, tile:, :] = attn


def score_kernel(
    seqs, x_ref, keys_ref, values_ref, weight_ref, delta_ref, out_ref, lay_ref
):
    tile = 2 * seqs
    senders = x_ref.shape[0]
    keys = keys_ref[...]
    keys2 = jnp.concatenate([keys, keys], axis=1)
    values = values_ref[...]
    weight = weight_ref[0:tile, :][None]
    row_block = weight_ref[tile : tile + 1, :][None]
    column = weight_ref[tile + 8 : tile + 9, :]
    delta = delta_ref[...]
    at_once = min(AT_ONCE, senders)
    row = lax.broadcasted_iota(jnp.int32, (1, tile, HD), 1)
    for first in range(0, senders, at_once):
        x = x_ref[first : first + at_once].astype(F32)
        flat = [
            x[:, k * tile : (k + 1) * tile, :].reshape(at_once * tile, HD).astype(BF16)
            for k in range(3)
        ]
        scores = mm_t(jnp.concatenate(flat[:2], axis=1), keys2)
        highest = jnp.max(scores, axis=1, keepdims=True)
        weights = jnp.exp2(scores - highest)
        probs = (weights * (1.0 / jnp.sum(weights, axis=1, keepdims=True))).astype(BF16)
        context = mm(probs, values)
        gated = context / (1.0 + jnp.exp(-context))
        terms = gated.reshape(at_once, tile, HD) * weight
        by_head = jnp.broadcast_to(jnp.sum(terms, axis=2, keepdims=True), terms.shape)
        score = by_head + jnp.concatenate([by_head[:, seqs:], by_head[:, :seqs]], axis=1)
        product = mm(flat[2], delta).reshape(at_once, tile, HD)
        turned = jnp.concatenate([product[:, seqs:], product[:, :seqs]], axis=1)
        result = jnp.where(row_block == 0.0, product, turned)
        result = jnp.where(row < seqs, result, score)
        span = slice(first * tile, (first + at_once) * tile)
        lay_ref[span, :] = result.reshape(at_once * tile, HD)
    for q in range(seqs):
        out_ref[rows_at(q, senders, seqs + 1), :] = lay_ref[rows_at(q, senders, tile), :]
    lane = lax.broadcasted_iota(jnp.int32, (senders, HD), 1)
    last = jnp.broadcast_to(column, (senders, HD))
    for q in range(seqs):
        last = jnp.where(lane == q, lay_ref[rows_at(seqs + q, senders, tile), :], last)
    out_ref[rows_at(seqs, senders, seqs + 1), :] = last


def merge_kernel(seqs, shards, x_ref, partial_ref, place_ref, out_ref):
    each = seqs + 1
    senders = x_ref.shape[0] // each
    blocks = partial_ref.shape[0] // seqs
    own_blocks = blocks // shards
    message = out_ref.shape[0] // shards
    last = x_ref[rows_at(seqs, senders, each), :]
    column = last[:, HD - 1 :]
    pieces = split3(
        jnp.concatenate([x_ref[rows_at(s, senders, each), :] for s in range(seqs)], axis=1)
    )
    down = lax.broadcasted_iota(jnp.int32, (senders, senders), 0)
    across = lax.broadcasted_iota(jnp.int32, (senders, senders), 1)
    column_across = jnp.sum(
        jnp.where(down == across, jnp.broadcast_to(column, (senders, senders)), 0.0),
        axis=0,
        keepdims=True,
    )
    order = lax.broadcasted_iota(jnp.int32, (blocks, senders), 0)
    wanted = (order % shards * own_blocks + order // shards).astype(F32)
    pick = jnp.where(wanted == column_across, 1.0, 0.0).astype(BF16)
    high, mid, low = pieces
    added = (mm(pick, low) + mm(pick, mid)) + mm(pick, high)
    for c in range(own_blocks):
        for s in range(seqs):
            q = c * seqs + s
            out_ref[rows_at(q, shards, message), :] = (
                partial_ref[q * shards : (q + 1) * shards, :]
                + added[c * shards : (c + 1) * shards, s * HD : (s + 1) * HD]
            )
    place = place_ref[...].astype(F32)
    for p in range(PAIR):
        score = jnp.concatenate(
            [last[:, r * PAIR + p : r * PAIR + p + 1] for r in range(CAP)], axis=0
        )
        back = jnp.sum(place * score, axis=0, keepdims=True)
        out_ref[rows_at(own_blocks * seqs + p, shards, message), :] = jnp.broadcast_to(
            back, (shards, HD)
        )


def final_kernel(shards, x_ref, length_ref, decoded_ref, rewards_ref):
    each = x_ref.shape[0] // shards
    seqs = decoded_ref.shape[0]
    body = each - PAIR
    parts = [x_ref[k * each : (k + 1) * each, :] for k in range(shards)]
    total = parts[0]
    for part in parts[1:]:
        total = total + part
    for c in range(body // seqs):
        decoded_ref[:, c * HD : (c + 1) * HD] = total[c * seqs : (c + 1) * seqs, :].astype(BF16)
    length = length_ref[0:1, :]
    count = rewards_ref.shape[1]
    reward = jnp.zeros((1, HD), F32)
    for k in range(shards):
        for p in range(PAIR):
            token = k // CORES * PAIR + p
            row = parts[k][body + p : body + p + 1, :]
            reward = reward + jnp.where(length > token, row, 0.0)
    rewards_ref[...] = (reward / length)[:, :count]


def per_device(
    query,
    key_cache,
    value_cache,
    new_key,
    new_value,
    cache_lengths,
    out_weight,
    delta_index,
    delta_values,
    fin_route,
    fin_lengths,
    fin_rows,
    reward_query,
    rubric_keys,
    rubric_values,
    score_weight,
):
    wide_count = lax.axis_size("wide")
    chips = lax.axis_size("th")
    tp_count = chips * lax.axis_size("tc")
    finished, row_len, features = fin_rows.shape
    heads = reward_query.shape[1] // HD // CORES
    seq_count = query.shape[0]
    tile = 2 * seq_count
    blocks = out_weight.shape[1] // HD
    slots = CAP * wide_count
    parts = PAIR * heads
    message = parts * finished + 8
    shape = jax.ShapeDtypeStruct

    rows = fin_rows.reshape(finished * row_len, features)
    partial = shape((chips * message, HD), F32)
    squares_shape = shape((chips * 8, HD), F32)
    acc = pltpu.VMEM((heads * finished * row_len, HD), F32)
    theirs, squares, rows, weights = local_call(
        functools.partial(project_kernel, False, row_len),
        "project_theirs",
        (rows, reward_query),
        [partial, squares_shape, shape(rows.shape, BF16), shape(reward_query.shape, BF16)],
        [
            acc,
            pltpu.VMEM((finished * row_len, HD), F32),
            pltpu.SemaphoreType.DMA((2 * FEATURE_COPIES + 1,)),
        ],
        fetched=2,
    )
    got = lax.ppermute(theirs, "tc", [(0, 1), (1, 0)])
    (kept,) = local_call(
        functools.partial(project_kernel, True, row_len),
        "project_kept",
        (squares, rows, weights),
        [partial],
        [acc],
    )
    (both,) = local_call(add_kernel, "add", (kept, got), [partial])
    summed_tokens = lax.all_to_all(
        both.reshape(chips, message, HD), "th", split_axis=0, concat_axis=0, tiled=True
    ).reshape(partial.shape)

    pad = ((0, 0), (0, HD - finished))
    routing = jnp.concatenate(
        [
            jnp.pad(fin_route.reshape(1, finished), pad, constant_values=-1),
            jnp.pad(fin_lengths.reshape(1, finished), pad, constant_values=1),
            jnp.broadcast_to(delta_index.reshape(1, 1), (1, HD)),
        ]
    ).astype(F32)
    weights = score_weight.reshape(heads * CORES, HD)
    small = (cache_lengths, query, new_key, new_value, routing, weights, delta_values[0])
    large = (key_cache, value_cache, out_weight)
    attn, partial_out, place, weight_tile, delta, lengths = local_call(
        decode_kernel,
        "decode",
        small + large,
        [
            shape((tile, HD), F32),
            shape((blocks * seq_count, HD), F32),
            shape((slots, HD), BF16),
            shape((tile + 16, HD), F32),
            shape(delta_values.shape[1:], BF16),
            shape((8, HD), F32),
        ],
        [pltpu.SMEM(cache_lengths.shape, jnp.int32)]
        + [pltpu.VMEM(a.shape, a.dtype) for a in small[1:-1] + large]
        + [pltpu.SemaphoreType.DMA((len(small) + 2 + WEIGHT_COPIES,))],
        fetched=len(small) + len(large),
    )

    lay = CAP * parts
    (outgoing,) = local_call(
        functools.partial(place_kernel, chips),
        "place",
        (summed_tokens, attn, place),
        [shape((wide_count, 2 * lay + tile, HD), BF16)],
        [pltpu.VMEM((wide_count * 2 * lay, HD), F32)],
    )
    received = lax.all_to_all(outgoing, "wide", split_axis=0, concat_axis=0, tiled=True)

    answer = seq_count + 1
    (answers,) = local_call(
        functools.partial(score_kernel, seq_count),
        "score",
        (
            received,
            rubric_keys[0],
            rubric_values[0],
            weight_tile,
            delta,
        ),
        [shape((wide_count * answer, HD), F32)],
        [pltpu.VMEM((wide_count * tile, HD), F32)],
    )
    returned = lax.all_to_all(
        answers.reshape(wide_count, 1, answer * HD), "wide", split_axis=0, concat_axis=0, tiled=True
    ).reshape(answers.shape)

    share = blocks // tp_count * seq_count + PAIR
    (merged,) = local_call(
        functools.partial(merge_kernel, seq_count, tp_count),
        "merge",
        (returned, partial_out, place),
        [shape((tp_count * share, HD), F32)],
    )
    shares = lax.all_to_all(
        merged.reshape(tp_count, 1, share * HD),
        ("th", "tc"),
        split_axis=0,
        concat_axis=0,
        tiled=True,
    ).reshape(merged.shape)

    decoded, rewards = local_call(
        functools.partial(final_kernel, tp_count),
        "final",
        (shares, lengths),
        [shape((seq_count, blocks // tp_count * HD), BF16), shape((1, finished), F32)],
    )
    return decoded, rewards.reshape(finished)


def solution(mesh):
    tp = ("th", "tc")
    wide_count, tp_count = mesh.devices.shape
    split = jax.sharding.Mesh(
        mesh.devices.reshape(wide_count, tp_count // CORES, CORES), ("wide",) + tp
    )
    in_specs = (
        P("wide", tp),
        P("wide", None, tp),
        P("wide", None, tp),
        P("wide", tp),
        P("wide", tp),
        P("wide"),
        P(tp, None),
        P("wide"),
        P("wide", tp, None),
        P("wide", None),
        P("wide"),
        P("wide", None, tp),
        P(tp, None),
        P("wide", None, None),
        P("wide", None, None),
        P(),
    )
    out_specs = (P("wide", tp), P("wide"))
    return jax.shard_map(
        per_device, mesh=split, in_specs=in_specs, out_specs=out_specs, check_vma=False
    )
```

```python
import functools
import math

import jax
import jax.numpy as jnp
from jax import lax
from jax.experimental import pallas as pl
from jax.experimental.pallas import tpu as pltpu
from jax.sharding import PartitionSpec as P

HD = 128
RD = 8192
CAP = 2
CORES = 2
PAIR = 2
VMEM_LIMIT = 16 * 2**20
WEIGHT_COPIES = 4
FEATURE_COPIES = 2
AT_ONCE = 32
F32 = jnp.float32
BF16 = jnp.bfloat16


def split2(x):
    high = x.astype(BF16)
    return high, (x - high.astype(F32)).astype(BF16)


def split3(x):
    high, mid = split2(x)
    return high, mid, (x - high.astype(F32) - mid.astype(F32)).astype(BF16)


def mm(a, b):
    return jnp.dot(a, b, preferred_element_type=F32)


def mm_t(a, b):
    return lax.dot_general(a, b, (((1,), (1,)), ((), ())), preferred_element_type=F32)


def rows_at(first, count, stride):
    return pl.ds(first, count, stride=stride)


def local_call(kernel, name, operands, outs, scratch=(), fetched=0):
    vmem = pl.BlockSpec(memory_space=pltpu.VMEM)
    hbm = pl.BlockSpec(memory_space=pltpu.HBM)
    kept = len(operands) - fetched
    operands = list(operands[:kept]) + [
        pltpu.with_memory_space_constraint(a, pltpu.HBM) for a in operands[kept:]
    ]
    return pl.pallas_call(
        kernel,
        in_specs=[vmem] * kept + [hbm] * fetched,
        out_specs=[vmem] * len(outs),
        out_shape=outs,
        scratch_shapes=list(scratch),
        compiler_params=pltpu.CompilerParams(vmem_limit_bytes=VMEM_LIMIT),
        name=name,
    )(*operands)


def start_copies(pairs, sems):
    copies = [pltpu.make_async_copy(a, b, sems.at[k]) for k, (a, b) in enumerate(pairs)]
    for copy in copies:
        copy.start()
    return copies


def project_kernel(mine, row_len, *refs):
    if mine:
        squares_ref, rows_ref, wq_ref, out_ref, acc_ref = refs
    else:
        rows_hbm, wq_hbm, out_ref, squares_ref, rows_ref, wq_ref, acc_ref, sq_ref, sems = refs
    many = rows_ref.shape[0]
    width = wq_ref.shape[1] // CORES
    heads = width // HD
    core = lax.axis_index("tc")
    half = core if mine else 1 - core
    columns = pl.ds(pl.multiple_of(half * width, width), width)
    steps = 1 if mine else FEATURE_COPIES
    depth = wq_ref.shape[0] // steps
    spans = [pl.ds(k * depth, depth) for k in range(steps)]
    if not mine:
        kept = pl.ds(pl.multiple_of(core * width, width), width)
        pieces = []
        for k in spans:
            pieces += [(wq_hbm.at[k, columns], wq_ref.at[k, columns])]
            pieces += [(rows_hbm.at[:, k], rows_ref.at[:, k])]
        pieces += [(wq_hbm.at[:, kept], wq_ref.at[:, kept])]
        copies = start_copies(pieces, sems)
    chunk = many // row_len
    pairs = row_len // PAIR
    each = out_ref.shape[0] // pairs
    body = each - 8
    seqs = body // (heads * PAIR)
    product = sums = None
    for step, k in enumerate(spans):
        if not mine:
            copies[2 * step].wait()
            copies[2 * step + 1].wait()
        rows = rows_ref[:, k]
        part = mm(rows, wq_ref[k, columns])
        product = part if product is None else product + part
        if not mine:
            wide_rows = rows.astype(F32)
            wide_rows = wide_rows * wide_rows
            for first in range(0, depth, HD):
                slab = wide_rows[:, first : first + HD]
                sums = slab if sums is None else sums + slab
    for h in range(heads):
        acc_ref[h * many : (h + 1) * many, :] = product[:, h * HD : (h + 1) * HD]
    for t in range(row_len):
        for h in range(heads):
            first = (t // PAIR) * each + (h * PAIR + t % PAIR) * seqs
            out_ref[first : first + chunk, :] = acc_ref[rows_at(h * many + t, chunk, row_len), :]
    if mine:
        for p in range(pairs):
            tail = slice(p * each + body, (p + 1) * each)
            out_ref[tail, :] = squares_ref[p * 8 : (p + 1) * 8, :]
        return
    sq_ref[...] = jnp.broadcast_to(jnp.sum(sums, axis=1, keepdims=True), sq_ref.shape)
    across = lax.broadcasted_iota(jnp.int32, (chunk, HD), 0)
    lane = lax.broadcasted_iota(jnp.int32, (chunk, HD), 1)
    for p in range(pairs):
        total = jnp.zeros((1, HD), F32)
        for t in range(p * PAIR, (p + 1) * PAIR):
            spot = lane == across + (t % PAIR) * seqs
            picked = jnp.where(spot, sq_ref[rows_at(t, chunk, row_len), :], 0.0)
            total += jnp.sum(picked, axis=0, keepdims=True)
        tail = jnp.broadcast_to(total, (8, HD))
        squares_ref[p * 8 : (p + 1) * 8, :] = tail
        out_ref[p * each + body : (p + 1) * each, :] = tail
    copies[-1].wait()


def add_kernel(a_ref, b_ref, out_ref):
    out_ref[...] = a_ref[...] + b_ref[...]


def decode_kernel(
    lens_hbm,
    q_hbm,
    nk_hbm,
    nv_hbm,
    route_hbm,
    score_hbm,
    delta_hbm,
    k_hbm,
    v_hbm,
    w_hbm,
    attn_ref,
    out_ref,
    place_ref,
    tile_ref,
    delta_ref,
    length_ref,
    lens_ref,
    q_ref,
    nk_ref,
    nv_ref,
    route_ref,
    score_ref,
    k_ref,
    v_ref,
    w_ref,
    sems,
):
    w_cols = w_ref.shape[1] // WEIGHT_COPIES
    copies = start_copies(
        [
            (lens_hbm, lens_ref),
            (q_hbm, q_ref),
            (nk_hbm, nk_ref),
            (nv_hbm, nv_ref),
            (route_hbm, route_ref),
            (score_hbm, score_ref),
            (delta_hbm, delta_ref),
            (k_hbm, k_ref),
            (v_hbm, v_ref),
        ]
        + [
            (w_hbm.at[:, pl.ds(c, w_cols)], w_ref.at[:, pl.ds(c, w_cols)])
            for c in range(0, w_ref.shape[1], w_cols)
        ],
        sems,
    )
    for copy in copies[:-WEIGHT_COPIES]:
        copy.wait()
    seqs = q_ref.shape[0]
    rows = 2 * seqs
    scale = 1.0 / math.sqrt(HD)
    q = q_ref[...].astype(F32)
    queries = jnp.concatenate([q[:, :HD], q[:, HD:]], axis=0)
    nk = nk_ref[...].astype(F32)
    nv = nv_ref[...].astype(F32)
    own_key = jnp.concatenate([nk, nk], axis=0)
    own_value = jnp.concatenate([nv, nv], axis=0)
    row = lax.broadcasted_iota(jnp.int32, (rows, HD), 0) % seqs
    place_in = lax.broadcasted_iota(jnp.int32, (rows, HD), 1)
    queries16 = queries.astype(BF16)
    scores = jnp.zeros((rows, HD), F32)
    length = jnp.zeros((rows, HD), jnp.int32)
    for s in range(seqs):
        scores = jnp.where(row == s, mm_t(queries16, k_ref[s]), scores)
        length = jnp.where(row == s, lens_ref[s], length)
    scores = jnp.where(place_in < length, scores * scale, -jnp.inf)
    own_score = jnp.sum(queries * own_key, axis=1, keepdims=True) * scale
    highest = jnp.maximum(jnp.max(scores, axis=1, keepdims=True), own_score)
    weights = jnp.exp(scores - highest)
    own_weight = jnp.exp(own_score - highest)
    denominator = jnp.sum(weights, axis=1, keepdims=True) + own_weight
    probs = (weights / denominator).astype(BF16)
    own_prob = (own_weight / denominator).astype(BF16).astype(F32)
    mixed = jnp.zeros((rows, HD), F32)
    for s in range(seqs):
        mixed = jnp.where(row == s, mm(probs, v_ref[s]), mixed)
    attn = (mixed + own_prob * own_value).astype(BF16).astype(F32)
    attn_ref[...] = attn
    turned = jnp.concatenate([attn[seqs:], attn[:seqs]], axis=0)
    both = jnp.concatenate([attn, turned], axis=1).astype(BF16)
    blocks = w_ref.shape[1] // HD
    shards = blocks // 4
    for copy in copies[-WEIGHT_COPIES:]:
        copy.wait()
    for first in range(0, blocks, 4):
        part = mm(both, w_ref[:, first * HD : (first + 4) * HD])
        for c in range(4):
            own = rows_at(c * seqs * shards + first // 4, seqs, shards)
            out_ref[own, :] = part[:seqs, c * HD : (c + 1) * HD]
    slots = place_ref.shape[0]
    groups = slots // CAP
    down = lax.broadcasted_iota(jnp.int32, (HD, HD), 0)
    across = lax.broadcasted_iota(jnp.int32, (HD, HD), 1)
    routing = route_ref[...]
    route = routing[0:1]
    target = jnp.broadcast_to(route, (HD, HD))
    target_down = jnp.sum(jnp.where(down == across, target, 0.0), axis=1, keepdims=True)
    earlier = jnp.where(jnp.logical_and(target == target_down, down < across), 1.0, 0.0)
    rank = jnp.sum(earlier, axis=0, keepdims=True)
    slot = lax.broadcasted_iota(jnp.int32, (slots, HD), 0)
    group = (slot % groups).astype(F32)
    order = (slot // groups).astype(F32)
    held = jnp.logical_and(route == group, rank == order)
    place_ref[...] = jnp.where(held, 1.0, 0.0).astype(BF16)
    weight = score_ref[...].astype(F32)
    heads = weight.shape[0] // CORES
    weight = jnp.where(lax.axis_index("tc") == 0, weight[:heads], weight[heads:])
    for h in range(heads):
        own = slice(h * rows // heads, (h + 1) * rows // heads)
        tile_ref[own, :] = jnp.broadcast_to(weight[h : h + 1], (rows // heads, HD))
    block = jnp.broadcast_to(routing[2:3], (8, HD))
    row_block = jnp.floor(block / blocks)
    tile_ref[rows : rows + 8, :] = row_block
    tile_ref[rows + 8 : rows + 16, :] = block - row_block * blocks
    length_ref[...] = jnp.broadcast_to(routing[1:2], length_ref.shape)


def place_kernel(sources, x_ref, attn_ref, place_ref, out_ref, lay_ref):
    each = x_ref.shape[0] // sources
    body = each - 8
    groups = place_ref.shape[0] // CAP
    lay = out_ref.shape[1]
    tile = 2 * lay
    parts = lay // CAP
    heads = parts // PAIR
    seqs = body // parts
    total = x_ref[0:each, :]
    for k in range(1, sources):
        total = total + x_ref[k * each : (k + 1) * each, :]
    inverse = lax.rsqrt(total[body : body + 1, :] / RD + 1e-05) * (math.log2(math.e) / math.sqrt(HD))
    down = lax.broadcasted_iota(jnp.int32, (HD, HD), 0)
    across = lax.broadcasted_iota(jnp.int32, (HD, HD), 1)
    factor = jnp.sum(jnp.where(down == across, inverse, 0.0), axis=1, keepdims=True)
    pieces = []
    for h in range(heads):
        for p in range(PAIR):
            first = (h * PAIR + p) * seqs
            pieces.append(total[first : first + seqs, :] * factor[p * seqs : (p + 1) * seqs, :])
    normed = jnp.concatenate(pieces, axis=1)
    if seqs < HD:
        normed = jnp.concatenate([normed, jnp.zeros((HD - seqs, parts * HD), F32)], axis=0)
    place = place_ref[...]
    for k, term in enumerate(split2(normed)):
        placed = mm(place, term)
        for r in range(CAP):
            for q in range(parts):
                row = k * lay + (q // PAIR) * CAP * PAIR + r * PAIR + q % PAIR
                lay_ref[rows_at(row, groups, tile), :] = placed[
                    r * groups : (r + 1) * groups, q * HD : (q + 1) * HD
                ]
    attn = attn_ref[...].astype(BF16)
    for g in range(groups):
        for k in range(2):
            own = slice(g * tile + k * lay, g * tile + (k + 1) * lay)
            out_ref[3 * g + k] = lay_ref[own, :].astype(BF16)
        out_ref[3 * g + 2] = attn


def score_kernel(
    seqs, x_ref, keys_ref, values_ref, weight_ref, delta_ref, out_ref, lay_ref
):
    tile = 2 * seqs
    senders = x_ref.shape[0] // 3
    keys = keys_ref[...]
    keys2 = jnp.concatenate([keys, keys], axis=1)
    values = values_ref[...]
    weight = weight_ref[0:tile, :][None]
    row_block = weight_ref[tile : tile + 1, :][None]
    column = weight_ref[tile + 8 : tile + 9, :]
    delta = delta_ref[...]
    at_once = min(AT_ONCE, senders)
    row = lax.broadcasted_iota(jnp.int32, (1, tile, HD), 1)
    for first in range(0, senders, at_once):
        x = x_ref[3 * first : 3 * (first + at_once)].astype(F32)
        x = x.reshape(at_once, 3, tile, HD)
        flat = [x[:, k].reshape(at_once * tile, HD).astype(BF16) for k in range(3)]
        scores = mm_t(jnp.concatenate(flat[:2], axis=1), keys2)
        highest = jnp.max(scores, axis=1, keepdims=True)
        weights = jnp.exp2(scores - highest)
        probs = (weights * (1.0 / jnp.sum(weights, axis=1, keepdims=True))).astype(BF16)
        context = mm(probs, values)
        gated = context / (1.0 + jnp.exp(-context))
        terms = gated.reshape(at_once, tile, HD) * weight
        by_head = jnp.broadcast_to(jnp.sum(terms, axis=2, keepdims=True), terms.shape)
        score = by_head + jnp.concatenate([by_head[:, seqs:], by_head[:, :seqs]], axis=1)
        product = mm(flat[2], delta).reshape(at_once, tile, HD)
        turned = jnp.concatenate([product[:, seqs:], product[:, :seqs]], axis=1)
        result = jnp.where(row_block == 0.0, product, turned)
        result = jnp.where(row < seqs, result, score)
        span = slice(first * tile, (first + at_once) * tile)
        lay_ref[span, :] = result.reshape(at_once * tile, HD)
    for q in range(seqs):
        out_ref[rows_at(q, senders, seqs + 1), :] = lay_ref[rows_at(q, senders, tile), :]
    lane = lax.broadcasted_iota(jnp.int32, (senders, HD), 1)
    last = jnp.broadcast_to(column, (senders, HD))
    for q in range(seqs):
        last = jnp.where(lane == q, lay_ref[rows_at(seqs + q, senders, tile), :], last)
    out_ref[rows_at(seqs, senders, seqs + 1), :] = last


def merge_kernel(seqs, shards, x_ref, partial_ref, place_ref, out_ref):
    each = seqs + 1
    senders = x_ref.shape[0] // each
    blocks = partial_ref.shape[0] // seqs - 8
    own_blocks = blocks // shards
    message = out_ref.shape[0] // shards
    last = x_ref[rows_at(seqs, senders, each), :]
    column = last[:, HD - 1 :]
    pieces = split3(
        jnp.concatenate([x_ref[rows_at(s, senders, each), :] for s in range(seqs)], axis=1)
    )
    down = lax.broadcasted_iota(jnp.int32, (senders, senders), 0)
    across = lax.broadcasted_iota(jnp.int32, (senders, senders), 1)
    column_across = jnp.sum(
        jnp.where(down == across, jnp.broadcast_to(column, (senders, senders)), 0.0),
        axis=0,
        keepdims=True,
    )
    order = lax.broadcasted_iota(jnp.int32, (blocks, senders), 0)
    wanted = (order % shards * own_blocks + order // shards).astype(F32)
    pick = jnp.where(wanted == column_across, 1.0, 0.0).astype(BF16)
    high, mid, low = pieces
    added = (mm(pick, low) + mm(pick, mid)) + mm(pick, high)
    for c in range(own_blocks):
        for s in range(seqs):
            q = c * seqs + s
            out_ref[rows_at(q, shards, message), :] = (
                partial_ref[q * shards : (q + 1) * shards, :]
                + added[c * shards : (c + 1) * shards, s * HD : (s + 1) * HD]
            )
    place = place_ref[...].astype(F32)
    for p in range(PAIR):
        score = jnp.concatenate(
            [last[:, r * PAIR + p : r * PAIR + p + 1] for r in range(CAP)], axis=0
        )
        back = jnp.sum(place * score, axis=0, keepdims=True)
        out_ref[rows_at(own_blocks * seqs + p, shards, message), :] = jnp.broadcast_to(
            back, (shards, HD)
        )


def final_kernel(shards, x_ref, length_ref, decoded_ref, rewards_ref):
    each = x_ref.shape[0] // shards
    seqs = decoded_ref.shape[0]
    body = each - PAIR
    rows = [x_ref[rows_at(q, shards, each), :] for q in range(each)]
    sums = [jnp.sum(row, axis=0, keepdims=True) for row in rows[:body]]
    for c in range(body // seqs):
        block = jnp.concatenate(sums[c * seqs : (c + 1) * seqs], axis=0)
        decoded_ref[:, c * HD : (c + 1) * HD] = block.astype(BF16)
    length = length_ref[0:1, :]
    count = rewards_ref.shape[1]
    shard = lax.broadcasted_iota(jnp.int32, (shards, HD), 0)
    reward = jnp.zeros((1, HD), F32)
    for p in range(PAIR):
        token = (shard // CORES * PAIR + p).astype(F32)
        scored = jnp.where(length > token, rows[body + p], 0.0)
        reward = reward + jnp.sum(scored, axis=0, keepdims=True)
    rewards_ref[...] = (reward / length)[:, :count]


def per_device(
    query,
    key_cache,
    value_cache,
    new_key,
    new_value,
    cache_lengths,
    out_weight,
    delta_index,
    delta_values,
    fin_route,
    fin_lengths,
    fin_rows,
    reward_query,
    rubric_keys,
    rubric_values,
    score_weight,
):
    wide_count = lax.axis_size("wide")
    chips = lax.axis_size("th")
    tp_count = chips * lax.axis_size("tc")
    finished, row_len, features = fin_rows.shape
    heads = reward_query.shape[1] // HD // CORES
    seq_count = query.shape[0]
    tile = 2 * seq_count
    blocks = out_weight.shape[1] // HD
    slots = CAP * wide_count
    parts = PAIR * heads
    message = parts * finished + 8
    shape = jax.ShapeDtypeStruct

    rows = fin_rows.reshape(finished * row_len, features)
    partial = shape((chips * message, HD), F32)
    squares_shape = shape((chips * 8, HD), F32)
    acc = pltpu.VMEM((heads * finished * row_len, HD), F32)
    theirs, squares, rows, weights = local_call(
        functools.partial(project_kernel, False, row_len),
        "project_theirs",
        (rows, reward_query),
        [partial, squares_shape, shape(rows.shape, BF16), shape(reward_query.shape, BF16)],
        [
            acc,
            pltpu.VMEM((finished * row_len, HD), F32),
            pltpu.SemaphoreType.DMA((2 * FEATURE_COPIES + 1,)),
        ],
        fetched=2,
    )
    got = lax.ppermute(theirs, "tc", [(0, 1), (1, 0)])
    (kept,) = local_call(
        functools.partial(project_kernel, True, row_len),
        "project_kept",
        (squares, rows, weights),
        [partial],
        [acc],
    )
    (both,) = local_call(add_kernel, "add", (kept, got), [partial])
    summed_tokens = lax.all_to_all(
        both.reshape(chips, message, HD), "th", split_axis=0, concat_axis=0, tiled=True
    ).reshape(partial.shape)

    pad = ((0, 0), (0, HD - finished))
    routing = jnp.concatenate(
        [
            jnp.pad(fin_route.reshape(1, finished), pad, constant_values=-1),
            jnp.pad(fin_lengths.reshape(1, finished), pad, constant_values=1),
            jnp.broadcast_to(delta_index.reshape(1, 1), (1, HD)),
        ]
    ).astype(F32)
    weights = score_weight.reshape(heads * CORES, HD)
    small = (cache_lengths, query, new_key, new_value, routing, weights, delta_values[0])
    large = (key_cache, value_cache, out_weight)
    attn, partial_out, place, weight_tile, delta, lengths = local_call(
        decode_kernel,
        "decode",
        small + large,
        [
            shape((tile, HD), F32),
            shape(((blocks + 8) * seq_count, HD), F32),
            shape((slots, HD), BF16),
            shape((tile + 16, HD), F32),
            shape(delta_values.shape[1:], BF16),
            shape((8, HD), F32),
        ],
        [pltpu.SMEM(cache_lengths.shape, jnp.int32)]
        + [pltpu.VMEM(a.shape, a.dtype) for a in small[1:-1] + large]
        + [pltpu.SemaphoreType.DMA((len(small) + 2 + WEIGHT_COPIES,))],
        fetched=len(small) + len(large),
    )

    lay = CAP * parts
    (outgoing,) = local_call(
        functools.partial(place_kernel, chips),
        "place",
        (summed_tokens, attn, place),
        [shape((wide_count * 3, lay, HD), BF16)],
        [pltpu.VMEM((wide_count * 2 * lay, HD), F32)],
    )
    received = lax.all_to_all(outgoing, "wide", split_axis=0, concat_axis=0, tiled=True)

    answer = seq_count + 1
    (answers,) = local_call(
        functools.partial(score_kernel, seq_count),
        "score",
        (
            received,
            rubric_keys[0],
            rubric_values[0],
            weight_tile,
            delta,
        ),
        [shape((wide_count * answer, HD), F32)],
        [pltpu.VMEM((wide_count * tile, HD), F32)],
    )
    returned = lax.all_to_all(
        answers.reshape(wide_count, 1, answer * HD), "wide", split_axis=0, concat_axis=0, tiled=True
    ).reshape(answers.shape)

    share = blocks // tp_count * seq_count + PAIR
    (merged,) = local_call(
        functools.partial(merge_kernel, seq_count, tp_count),
        "merge",
        (returned, partial_out, place),
        [shape((tp_count * share, HD), F32)],
    )
    shares = lax.all_to_all(
        merged.reshape(tp_count, 1, share * HD),
        ("th", "tc"),
        split_axis=0,
        concat_axis=0,
        tiled=True,
    ).reshape(merged.shape)

    decoded, rewards = local_call(
        functools.partial(final_kernel, tp_count),
        "final",
        (shares, lengths),
        [shape((seq_count, blocks // tp_count * HD), BF16), shape((1, finished), F32)],
    )
    return decoded, rewards.reshape(finished)


def solution(mesh):
    tp = ("th", "tc")
    wide_count, tp_count = mesh.devices.shape
    split = jax.sharding.Mesh(
        mesh.devices.reshape(wide_count, tp_count // CORES, CORES), ("wide",) + tp
    )
    in_specs = (
        P("wide", tp),
        P("wide", None, tp),
        P("wide", None, tp),
        P("wide", tp),
        P("wide", tp),
        P("wide"),
        P(tp, None),
        P("wide"),
        P("wide", tp, None),
        P("wide", None),
        P("wide"),
        P("wide", None, tp),
        P(tp, None),
        P("wide", None, None),
        P("wide", None, None),
        P(),
    )
    out_specs = (P("wide", tp), P("wide"))
    return jax.shard_map(
        per_device, mesh=split, in_specs=in_specs, out_specs=out_specs, check_vma=False
    )
```

```python
import functools
import math

import jax
import jax.numpy as jnp
from jax import lax
from jax.experimental import pallas as pl
from jax.experimental.pallas import tpu as pltpu
from jax.sharding import PartitionSpec as P

HD = 128
RD = 8192
CAP = 2
CORES = 2
PAIR = 2
VMEM_LIMIT = 16 * 2**20
WEIGHT_COPIES = 4
FEATURE_COPIES = 2
AT_ONCE = 32
F32 = jnp.float32
BF16 = jnp.bfloat16


def split2(x):
    high = x.astype(BF16)
    return high, (x - high.astype(F32)).astype(BF16)


def split3(x):
    high, mid = split2(x)
    return high, mid, (x - high.astype(F32) - mid.astype(F32)).astype(BF16)


def mm(a, b):
    return jnp.dot(a, b, preferred_element_type=F32)


def mm_t(a, b):
    return lax.dot_general(a, b, (((1,), (1,)), ((), ())), preferred_element_type=F32)


def rows_at(first, count, stride):
    return pl.ds(first, count, stride=stride)


def local_call(kernel, name, operands, outs, scratch=(), fetched=0):
    vmem = pl.BlockSpec(memory_space=pltpu.VMEM)
    hbm = pl.BlockSpec(memory_space=pltpu.HBM)
    kept = len(operands) - fetched
    operands = list(operands[:kept]) + [
        pltpu.with_memory_space_constraint(a, pltpu.HBM) for a in operands[kept:]
    ]
    return pl.pallas_call(
        kernel,
        in_specs=[vmem] * kept + [hbm] * fetched,
        out_specs=[vmem] * len(outs),
        out_shape=outs,
        scratch_shapes=list(scratch),
        compiler_params=pltpu.CompilerParams(vmem_limit_bytes=VMEM_LIMIT),
        name=name,
    )(*operands)


def start_copies(pairs, sems):
    copies = [pltpu.make_async_copy(a, b, sems.at[k]) for k, (a, b) in enumerate(pairs)]
    for copy in copies:
        copy.start()
    return copies


def project_kernel(mine, row_len, *refs):
    if mine:
        squares_ref, rows_ref, wq_ref, out_ref, acc_ref = refs
    else:
        rows_hbm, wq_hbm, out_ref, squares_ref, rows_ref, wq_ref, acc_ref, sq_ref, sems = refs
    many = rows_ref.shape[0]
    width = wq_ref.shape[1] // CORES
    heads = width // HD
    core = lax.axis_index("tc")
    half = core if mine else 1 - core
    columns = pl.ds(pl.multiple_of(half * width, width), width)
    steps = 1 if mine else FEATURE_COPIES
    depth = wq_ref.shape[0] // steps
    spans = [pl.ds(k * depth, depth) for k in range(steps)]
    if not mine:
        kept = pl.ds(pl.multiple_of(core * width, width), width)
        pieces = []
        for k in spans:
            pieces += [(wq_hbm.at[k, columns], wq_ref.at[k, columns])]
            pieces += [(rows_hbm.at[:, k], rows_ref.at[:, k])]
        pieces += [(wq_hbm.at[:, kept], wq_ref.at[:, kept])]
        copies = start_copies(pieces, sems)
    chunk = many // row_len
    pairs = row_len // PAIR
    each = out_ref.shape[0] // pairs
    body = each - 8
    seqs = body // (heads * PAIR)
    product = sums = None
    for step, k in enumerate(spans):
        if not mine:
            copies[2 * step].wait()
            copies[2 * step + 1].wait()
        rows = rows_ref[:, k]
        part = mm(rows, wq_ref[k, columns])
        product = part if product is None else product + part
        if not mine:
            wide_rows = rows.astype(F32)
            wide_rows = wide_rows * wide_rows
            for first in range(0, depth, HD):
                slab = wide_rows[:, first : first + HD]
                sums = slab if sums is None else sums + slab
    for h in range(heads):
        acc_ref[h * many : (h + 1) * many, :] = product[:, h * HD : (h + 1) * HD]
    for t in range(row_len):
        for h in range(heads):
            first = (t // PAIR) * each + (h * PAIR + t % PAIR) * seqs
            out_ref[first : first + chunk, :] = acc_ref[rows_at(h * many + t, chunk, row_len), :]
    if mine:
        for p in range(pairs):
            tail = slice(p * each + body, (p + 1) * each)
            out_ref[tail, :] = squares_ref[p * 8 : (p + 1) * 8, :]
        return
    sq_ref[...] = jnp.broadcast_to(jnp.sum(sums, axis=1, keepdims=True), sq_ref.shape)
    across = lax.broadcasted_iota(jnp.int32, (chunk, HD), 0)
    lane = lax.broadcasted_iota(jnp.int32, (chunk, HD), 1)
    for p in range(pairs):
        total = jnp.zeros((1, HD), F32)
        for t in range(p * PAIR, (p + 1) * PAIR):
            spot = lane == across + (t % PAIR) * seqs
            picked = jnp.where(spot, sq_ref[rows_at(t, chunk, row_len), :], 0.0)
            total += jnp.sum(picked, axis=0, keepdims=True)
        tail = jnp.broadcast_to(total, (8, HD))
        squares_ref[p * 8 : (p + 1) * 8, :] = tail
        out_ref[p * each + body : (p + 1) * each, :] = tail
    copies[-1].wait()


def add_kernel(a_ref, b_ref, out_ref):
    out_ref[...] = a_ref[...] + b_ref[...]


def decode_kernel(
    lens_hbm,
    q_hbm,
    nk_hbm,
    nv_hbm,
    route_hbm,
    score_hbm,
    delta_hbm,
    k_hbm,
    v_hbm,
    w_hbm,
    attn_ref,
    out_ref,
    place_ref,
    tile_ref,
    delta_ref,
    length_ref,
    lens_ref,
    q_ref,
    nk_ref,
    nv_ref,
    route_ref,
    score_ref,
    k_ref,
    v_ref,
    w_ref,
    sems,
):
    w_cols = w_ref.shape[1] // WEIGHT_COPIES
    copies = start_copies(
        [
            (lens_hbm, lens_ref),
            (q_hbm, q_ref),
            (nk_hbm, nk_ref),
            (nv_hbm, nv_ref),
            (route_hbm, route_ref),
            (score_hbm, score_ref),
            (delta_hbm, delta_ref),
            (k_hbm, k_ref),
            (v_hbm, v_ref),
        ]
        + [
            (w_hbm.at[:, pl.ds(c, w_cols)], w_ref.at[:, pl.ds(c, w_cols)])
            for c in range(0, w_ref.shape[1], w_cols)
        ],
        sems,
    )
    for copy in copies[:-WEIGHT_COPIES]:
        copy.wait()
    seqs = q_ref.shape[0]
    rows = 2 * seqs
    scale = 1.0 / math.sqrt(HD)
    q = q_ref[...].astype(F32)
    queries = jnp.concatenate([q[:, :HD], q[:, HD:]], axis=0)
    nk = nk_ref[...].astype(F32)
    nv = nv_ref[...].astype(F32)
    own_key = jnp.concatenate([nk, nk], axis=0)
    own_value = jnp.concatenate([nv, nv], axis=0)
    row = lax.broadcasted_iota(jnp.int32, (rows, HD), 0) % seqs
    place_in = lax.broadcasted_iota(jnp.int32, (rows, HD), 1)
    queries16 = queries.astype(BF16)
    scores = jnp.zeros((rows, HD), F32)
    length = jnp.zeros((rows, HD), jnp.int32)
    for s in range(seqs):
        scores = jnp.where(row == s, mm_t(queries16, k_ref[s]), scores)
        length = jnp.where(row == s, lens_ref[s], length)
    scores = jnp.where(place_in < length, scores * scale, -jnp.inf)
    own_score = jnp.sum(queries * own_key, axis=1, keepdims=True) * scale
    highest = jnp.maximum(jnp.max(scores, axis=1, keepdims=True), own_score)
    weights = jnp.exp(scores - highest)
    own_weight = jnp.exp(own_score - highest)
    denominator = jnp.sum(weights, axis=1, keepdims=True) + own_weight
    probs = (weights / denominator).astype(BF16)
    own_prob = (own_weight / denominator).astype(BF16).astype(F32)
    mixed = jnp.zeros((rows, HD), F32)
    for s in range(seqs):
        mixed = jnp.where(row == s, mm(probs, v_ref[s]), mixed)
    attn = (mixed + own_prob * own_value).astype(BF16).astype(F32)
    attn_ref[...] = attn
    turned = jnp.concatenate([attn[seqs:], attn[:seqs]], axis=0)
    both = jnp.concatenate([attn, turned], axis=1).astype(BF16)
    blocks = w_ref.shape[1] // HD
    shards = blocks // 4
    for copy in copies[-WEIGHT_COPIES:]:
        copy.wait()
    for first in range(0, blocks, 4):
        part = mm(both, w_ref[:, first * HD : (first + 4) * HD])
        for c in range(4):
            own = rows_at(c * seqs * shards + first // 4, seqs, shards)
            out_ref[own, :] = part[:seqs, c * HD : (c + 1) * HD]
    slots = place_ref.shape[0]
    groups = slots // CAP
    down = lax.broadcasted_iota(jnp.int32, (HD, HD), 0)
    across = lax.broadcasted_iota(jnp.int32, (HD, HD), 1)
    routing = route_ref[...]
    route = routing[0:1]
    target = jnp.broadcast_to(route, (HD, HD))
    target_down = jnp.sum(jnp.where(down == across, target, 0.0), axis=1, keepdims=True)
    earlier = jnp.where(jnp.logical_and(target == target_down, down < across), 1.0, 0.0)
    rank = jnp.sum(earlier, axis=0, keepdims=True)
    slot = lax.broadcasted_iota(jnp.int32, (slots, HD), 0)
    group = (slot % groups).astype(F32)
    order = (slot // groups).astype(F32)
    held = jnp.logical_and(route == group, rank == order)
    place_ref[...] = jnp.where(held, 1.0, 0.0).astype(BF16)
    weight = score_ref[...].astype(F32)
    heads = weight.shape[0] // CORES
    weight = jnp.where(lax.axis_index("tc") == 0, weight[:heads], weight[heads:])
    for h in range(heads):
        own = slice(h * rows // heads, (h + 1) * rows // heads)
        tile_ref[own, :] = jnp.broadcast_to(weight[h : h + 1], (rows // heads, HD))
    block = jnp.broadcast_to(routing[2:3], (8, HD))
    row_block = jnp.floor(block / blocks)
    tile_ref[rows : rows + 8, :] = row_block
    tile_ref[rows + 8 : rows + 16, :] = block - row_block * blocks
    length_ref[...] = jnp.broadcast_to(routing[1:2], length_ref.shape)


def place_kernel(sources, x_ref, attn_ref, place_ref, out_ref, lay_ref):
    each = x_ref.shape[0] // sources
    body = each - 8
    groups = place_ref.shape[0] // CAP
    lay = out_ref.shape[1]
    tile = 2 * lay
    parts = lay // CAP
    heads = parts // PAIR
    seqs = body // parts
    total = x_ref[0:each, :]
    for k in range(1, sources):
        total = total + x_ref[k * each : (k + 1) * each, :]
    inverse = lax.rsqrt(total[body : body + 1, :] / RD + 1e-05) * (math.log2(math.e) / math.sqrt(HD))
    down = lax.broadcasted_iota(jnp.int32, (HD, HD), 0)
    across = lax.broadcasted_iota(jnp.int32, (HD, HD), 1)
    factor = jnp.sum(jnp.where(down == across, inverse, 0.0), axis=1, keepdims=True)
    pieces = []
    for h in range(heads):
        for p in range(PAIR):
            first = (h * PAIR + p) * seqs
            pieces.append(total[first : first + seqs, :] * factor[p * seqs : (p + 1) * seqs, :])
    normed = jnp.concatenate(pieces, axis=1)
    if seqs < HD:
        normed = jnp.concatenate([normed, jnp.zeros((HD - seqs, parts * HD), F32)], axis=0)
    place = place_ref[...]
    for k, term in enumerate(split2(normed)):
        placed = mm(place, term)
        for r in range(CAP):
            for q in range(parts):
                row = k * lay + (q // PAIR) * CAP * PAIR + r * PAIR + q % PAIR
                lay_ref[rows_at(row, groups, tile), :] = placed[
                    r * groups : (r + 1) * groups, q * HD : (q + 1) * HD
                ]
    attn = attn_ref[...].astype(BF16)
    for g in range(groups):
        for k in range(2):
            own = slice(g * tile + k * lay, g * tile + (k + 1) * lay)
            out_ref[3 * g + k] = lay_ref[own, :].astype(BF16)
        out_ref[3 * g + 2] = attn


def score_kernel(
    seqs, x_ref, keys_ref, values_ref, weight_ref, delta_ref, out_ref, lay_ref
):
    tile = 2 * seqs
    senders = x_ref.shape[0] // 3
    keys = keys_ref[...]
    keys2 = jnp.concatenate([keys, keys], axis=1)
    values = values_ref[...]
    weight = weight_ref[0:tile, :][None]
    row_block = weight_ref[tile : tile + 1, :][None]
    column = weight_ref[tile + 8 : tile + 9, :]
    delta = delta_ref[...]
    at_once = min(AT_ONCE, senders)
    row = lax.broadcasted_iota(jnp.int32, (1, tile, HD), 1)
    started = []
    for first in range(0, senders, at_once):
        x = x_ref[3 * first : 3 * (first + at_once)].astype(F32)
        x = x.reshape(at_once, 3, tile, HD)
        flat = [x[:, k].reshape(at_once * tile, HD).astype(BF16) for k in range(3)]
        scores = mm_t(jnp.concatenate(flat[:2], axis=1), keys2)
        started.append((first, scores, mm(flat[2], delta)))
    for first, scores, product in started:
        highest = jnp.max(scores, axis=1, keepdims=True)
        weights = jnp.exp2(scores - highest)
        probs = (weights * (1.0 / jnp.sum(weights, axis=1, keepdims=True))).astype(BF16)
        context = mm(probs, values)
        gated = context / (1.0 + jnp.exp(-context))
        terms = gated.reshape(at_once, tile, HD) * weight
        by_head = jnp.broadcast_to(jnp.sum(terms, axis=2, keepdims=True), terms.shape)
        score = by_head + jnp.concatenate([by_head[:, seqs:], by_head[:, :seqs]], axis=1)
        product = product.reshape(at_once, tile, HD)
        turned = jnp.concatenate([product[:, seqs:], product[:, :seqs]], axis=1)
        result = jnp.where(row_block == 0.0, product, turned)
        result = jnp.where(row < seqs, result, score)
        span = slice(first * tile, (first + at_once) * tile)
        lay_ref[span, :] = result.reshape(at_once * tile, HD)
    for q in range(seqs):
        out_ref[rows_at(q, senders, seqs + 1), :] = lay_ref[rows_at(q, senders, tile), :]
    lane = lax.broadcasted_iota(jnp.int32, (senders, HD), 1)
    last = jnp.broadcast_to(column, (senders, HD))
    for q in range(seqs):
        last = jnp.where(lane == q, lay_ref[rows_at(seqs + q, senders, tile), :], last)
    out_ref[rows_at(seqs, senders, seqs + 1), :] = last


def merge_kernel(seqs, shards, x_ref, partial_ref, place_ref, out_ref):
    each = seqs + 1
    senders = x_ref.shape[0] // each
    blocks = partial_ref.shape[0] // seqs - 8
    own_blocks = blocks // shards
    message = out_ref.shape[0] // shards
    last = x_ref[rows_at(seqs, senders, each), :]
    column = last[:, HD - 1 :]
    pieces = split3(
        jnp.concatenate([x_ref[rows_at(s, senders, each), :] for s in range(seqs)], axis=1)
    )
    down = lax.broadcasted_iota(jnp.int32, (senders, senders), 0)
    across = lax.broadcasted_iota(jnp.int32, (senders, senders), 1)
    column_across = jnp.sum(
        jnp.where(down == across, jnp.broadcast_to(column, (senders, senders)), 0.0),
        axis=0,
        keepdims=True,
    )
    order = lax.broadcasted_iota(jnp.int32, (blocks, senders), 0)
    wanted = (order % shards * own_blocks + order // shards).astype(F32)
    pick = jnp.where(wanted == column_across, 1.0, 0.0).astype(BF16)
    high, mid, low = pieces
    added = (mm(pick, low) + mm(pick, mid)) + mm(pick, high)
    for c in range(own_blocks):
        for s in range(seqs):
            q = c * seqs + s
            out_ref[rows_at(q, shards, message), :] = (
                partial_ref[q * shards : (q + 1) * shards, :]
                + added[c * shards : (c + 1) * shards, s * HD : (s + 1) * HD]
            )
    place = place_ref[...].astype(F32)
    for p in range(PAIR):
        score = jnp.concatenate(
            [last[:, r * PAIR + p : r * PAIR + p + 1] for r in range(CAP)], axis=0
        )
        back = jnp.sum(place * score, axis=0, keepdims=True)
        out_ref[rows_at(own_blocks * seqs + p, shards, message), :] = jnp.broadcast_to(
            back, (shards, HD)
        )


def final_kernel(shards, x_ref, length_ref, decoded_ref, rewards_ref):
    each = x_ref.shape[0] // shards
    seqs = decoded_ref.shape[0]
    body = each - PAIR
    rows = [x_ref[rows_at(q, shards, each), :] for q in range(each)]
    sums = [jnp.sum(row, axis=0, keepdims=True) for row in rows[:body]]
    for c in range(body // seqs):
        block = jnp.concatenate(sums[c * seqs : (c + 1) * seqs], axis=0)
        decoded_ref[:, c * HD : (c + 1) * HD] = block.astype(BF16)
    length = length_ref[0:1, :]
    count = rewards_ref.shape[1]
    shard = lax.broadcasted_iota(jnp.int32, (shards, HD), 0)
    reward = jnp.zeros((1, HD), F32)
    for p in range(PAIR):
        token = (shard // CORES * PAIR + p).astype(F32)
        scored = jnp.where(length > token, rows[body + p], 0.0)
        reward = reward + jnp.sum(scored, axis=0, keepdims=True)
    rewards_ref[...] = (reward / length)[:, :count]


def per_device(
    query,
    key_cache,
    value_cache,
    new_key,
    new_value,
    cache_lengths,
    out_weight,
    delta_index,
    delta_values,
    fin_route,
    fin_lengths,
    fin_rows,
    reward_query,
    rubric_keys,
    rubric_values,
    score_weight,
):
    wide_count = lax.axis_size("wide")
    chips = lax.axis_size("th")
    tp_count = chips * lax.axis_size("tc")
    finished, row_len, features = fin_rows.shape
    heads = reward_query.shape[1] // HD // CORES
    seq_count = query.shape[0]
    tile = 2 * seq_count
    blocks = out_weight.shape[1] // HD
    slots = CAP * wide_count
    parts = PAIR * heads
    message = parts * finished + 8
    shape = jax.ShapeDtypeStruct

    rows = fin_rows.reshape(finished * row_len, features)
    partial = shape((chips * message, HD), F32)
    squares_shape = shape((chips * 8, HD), F32)
    acc = pltpu.VMEM((heads * finished * row_len, HD), F32)
    theirs, squares, rows, weights = local_call(
        functools.partial(project_kernel, False, row_len),
        "project_theirs",
        (rows, reward_query),
        [partial, squares_shape, shape(rows.shape, BF16), shape(reward_query.shape, BF16)],
        [
            acc,
            pltpu.VMEM((finished * row_len, HD), F32),
            pltpu.SemaphoreType.DMA((2 * FEATURE_COPIES + 1,)),
        ],
        fetched=2,
    )
    got = lax.ppermute(theirs, "tc", [(0, 1), (1, 0)])
    (kept,) = local_call(
        functools.partial(project_kernel, True, row_len),
        "project_kept",
        (squares, rows, weights),
        [partial],
        [acc],
    )
    (both,) = local_call(add_kernel, "add", (kept, got), [partial])
    summed_tokens = lax.all_to_all(
        both.reshape(chips, message, HD), "th", split_axis=0, concat_axis=0, tiled=True
    ).reshape(partial.shape)

    pad = ((0, 0), (0, HD - finished))
    routing = jnp.concatenate(
        [
            jnp.pad(fin_route.reshape(1, finished), pad, constant_values=-1),
            jnp.pad(fin_lengths.reshape(1, finished), pad, constant_values=1),
            jnp.broadcast_to(delta_index.reshape(1, 1), (1, HD)),
        ]
    ).astype(F32)
    weights = score_weight.reshape(heads * CORES, HD)
    small = (cache_lengths, query, new_key, new_value, routing, weights, delta_values[0])
    large = (key_cache, value_cache, out_weight)
    attn, partial_out, place, weight_tile, delta, lengths = local_call(
        decode_kernel,
        "decode",
        small + large,
        [
            shape((tile, HD), F32),
            shape(((blocks + 8) * seq_count, HD), F32),
            shape((slots, HD), BF16),
            shape((tile + 16, HD), F32),
            shape(delta_values.shape[1:], BF16),
            shape((8, HD), F32),
        ],
        [pltpu.SMEM(cache_lengths.shape, jnp.int32)]
        + [pltpu.VMEM(a.shape, a.dtype) for a in small[1:-1] + large]
        + [pltpu.SemaphoreType.DMA((len(small) + 2 + WEIGHT_COPIES,))],
        fetched=len(small) + len(large),
    )

    lay = CAP * parts
    (outgoing,) = local_call(
        functools.partial(place_kernel, chips),
        "place",
        (summed_tokens, attn, place),
        [shape((wide_count * 3, lay, HD), BF16)],
        [pltpu.VMEM((wide_count * 2 * lay, HD), F32)],
    )
    received = lax.all_to_all(outgoing, "wide", split_axis=0, concat_axis=0, tiled=True)

    answer = seq_count + 1
    (answers,) = local_call(
        functools.partial(score_kernel, seq_count),
        "score",
        (
            received,
            rubric_keys[0],
            rubric_values[0],
            weight_tile,
            delta,
        ),
        [shape((wide_count * answer, HD), F32)],
        [pltpu.VMEM((wide_count * tile, HD), F32)],
    )
    returned = lax.all_to_all(
        answers.reshape(wide_count, 1, answer * HD), "wide", split_axis=0, concat_axis=0, tiled=True
    ).reshape(answers.shape)

    share = blocks // tp_count * seq_count + PAIR
    (merged,) = local_call(
        functools.partial(merge_kernel, seq_count, tp_count),
        "merge",
        (returned, partial_out, place),
        [shape((tp_count * share, HD), F32)],
    )
    shares = lax.all_to_all(
        merged.reshape(tp_count, 1, share * HD),
        ("th", "tc"),
        split_axis=0,
        concat_axis=0,
        tiled=True,
    ).reshape(merged.shape)

    decoded, rewards = local_call(
        functools.partial(final_kernel, tp_count),
        "final",
        (shares, lengths),
        [shape((seq_count, blocks // tp_count * HD), BF16), shape((1, finished), F32)],
    )
    return decoded, rewards.reshape(finished)


def solution(mesh):
    tp = ("th", "tc")
    wide_count, tp_count = mesh.devices.shape
    split = jax.sharding.Mesh(
        mesh.devices.reshape(wide_count, tp_count // CORES, CORES), ("wide",) + tp
    )
    in_specs = (
        P("wide", tp),
        P("wide", None, tp),
        P("wide", None, tp),
        P("wide", tp),
        P("wide", tp),
        P("wide"),
        P(tp, None),
        P("wide"),
        P("wide", tp, None),
        P("wide", None),
        P("wide"),
        P("wide", None, tp),
        P(tp, None),
        P("wide", None, None),
        P("wide", None, None),
        P(),
    )
    out_specs = (P("wide", tp), P("wide"))
    return jax.shard_map(
        per_device, mesh=split, in_specs=in_specs, out_specs=out_specs, check_vma=False
    )
```

```python
import functools
import math

import jax
import jax.numpy as jnp
from jax import lax
from jax.experimental import pallas as pl
from jax.experimental.pallas import tpu as pltpu
from jax.sharding import PartitionSpec as P

HD = 128
RD = 8192
CAP = 2
CORES = 2
PAIR = 2
AXES = ("wide", "th", "tc")
VMEM_LIMIT = 16 * 2**20
WEIGHT_COPIES = 4
FEATURE_COPIES = 2
AT_ONCE = 32
F32 = jnp.float32
BF16 = jnp.bfloat16


def split2(x):
    high = x.astype(BF16)
    return high, (x - high.astype(F32)).astype(BF16)


def split3(x):
    high, mid = split2(x)
    return high, mid, (x - high.astype(F32) - mid.astype(F32)).astype(BF16)


def mm(a, b):
    return jnp.dot(a, b, preferred_element_type=F32)


def mm_t(a, b):
    return lax.dot_general(a, b, (((1,), (1,)), ((), ())), preferred_element_type=F32)


def rows_at(first, count, stride):
    return pl.ds(first, count, stride=stride)


def local_call(kernel, name, operands, outs, scratch=(), fetched=0):
    vmem = pl.BlockSpec(memory_space=pltpu.VMEM)
    hbm = pl.BlockSpec(memory_space=pltpu.HBM)
    kept = len(operands) - fetched
    operands = list(operands[:kept]) + [
        pltpu.with_memory_space_constraint(a, pltpu.HBM) for a in operands[kept:]
    ]
    return pl.pallas_call(
        kernel,
        in_specs=[vmem] * kept + [hbm] * fetched,
        out_specs=[vmem] * len(outs),
        out_shape=outs,
        scratch_shapes=list(scratch),
        compiler_params=pltpu.CompilerParams(vmem_limit_bytes=VMEM_LIMIT),
        name=name,
    )(*operands)


def start_copies(pairs, sems):
    copies = [pltpu.make_async_copy(a, b, sems.at[k]) for k, (a, b) in enumerate(pairs)]
    for copy in copies:
        copy.start()
    return copies


def project_kernel(mine, row_len, *refs):
    if mine:
        squares_ref, rows_ref, wq_ref, out_ref, acc_ref = refs
    else:
        rows_hbm, wq_hbm, out_ref, squares_ref, rows_ref, wq_ref, acc_ref, sq_ref, sems = refs
    many = rows_ref.shape[0]
    width = wq_ref.shape[1] // CORES
    heads = width // HD
    core = lax.axis_index("tc")
    half = core if mine else 1 - core
    columns = pl.ds(pl.multiple_of(half * width, width), width)
    steps = 1 if mine else FEATURE_COPIES
    depth = wq_ref.shape[0] // steps
    spans = [pl.ds(k * depth, depth) for k in range(steps)]
    if not mine:
        kept = pl.ds(pl.multiple_of(core * width, width), width)
        pieces = []
        for k in spans:
            pieces += [(wq_hbm.at[k, columns], wq_ref.at[k, columns])]
            pieces += [(rows_hbm.at[:, k], rows_ref.at[:, k])]
        pieces += [(wq_hbm.at[:, kept], wq_ref.at[:, kept])]
        copies = start_copies(pieces, sems)
    chunk = many // row_len
    pairs = row_len // PAIR
    each = out_ref.shape[0] // pairs
    body = each - 8
    seqs = body // (heads * PAIR)
    product = sums = None
    for step, k in enumerate(spans):
        if not mine:
            copies[2 * step].wait()
            copies[2 * step + 1].wait()
        rows = rows_ref[:, k]
        part = mm(rows, wq_ref[k, columns])
        product = part if product is None else product + part
        if not mine:
            wide_rows = rows.astype(F32)
            wide_rows = wide_rows * wide_rows
            for first in range(0, depth, HD):
                slab = wide_rows[:, first : first + HD]
                sums = slab if sums is None else sums + slab
    for h in range(heads):
        acc_ref[h * many : (h + 1) * many, :] = product[:, h * HD : (h + 1) * HD]
    for t in range(row_len):
        for h in range(heads):
            first = (t // PAIR) * each + (h * PAIR + t % PAIR) * seqs
            out_ref[first : first + chunk, :] = acc_ref[rows_at(h * many + t, chunk, row_len), :]
    if mine:
        for p in range(pairs):
            tail = slice(p * each + body, (p + 1) * each)
            out_ref[tail, :] = squares_ref[p * 8 : (p + 1) * 8, :]
        return
    sq_ref[...] = jnp.broadcast_to(jnp.sum(sums, axis=1, keepdims=True), sq_ref.shape)
    across = lax.broadcasted_iota(jnp.int32, (chunk, HD), 0)
    lane = lax.broadcasted_iota(jnp.int32, (chunk, HD), 1)
    for p in range(pairs):
        total = jnp.zeros((1, HD), F32)
        for t in range(p * PAIR, (p + 1) * PAIR):
            spot = lane == across + (t % PAIR) * seqs
            picked = jnp.where(spot, sq_ref[rows_at(t, chunk, row_len), :], 0.0)
            total += jnp.sum(picked, axis=0, keepdims=True)
        tail = jnp.broadcast_to(total, (8, HD))
        squares_ref[p * 8 : (p + 1) * 8, :] = tail
        out_ref[p * each + body : (p + 1) * each, :] = tail
    copies[-1].wait()


def add_kernel(a_ref, b_ref, out_ref):
    out_ref[...] = a_ref[...] + b_ref[...]


def exchange_both_ways(x):
    wide_count, chips, cores = (lax.axis_size(name) for name in AXES)
    groups = []
    for core in range(cores):
        for chip in range(chips):
            group = [(w * chips + chip) * cores + core for w in range(wide_count)]
            groups.append(group if core == 0 else group[::-1])
    return lax.all_to_all(
        x, AXES, split_axis=0, concat_axis=0, axis_index_groups=groups, tiled=True
    )


def decode_kernel(
    lens_hbm,
    q_hbm,
    nk_hbm,
    nv_hbm,
    route_hbm,
    score_hbm,
    delta_hbm,
    k_hbm,
    v_hbm,
    w_hbm,
    attn_ref,
    out_ref,
    place_ref,
    sent_ref,
    tile_ref,
    delta_ref,
    length_ref,
    lens_ref,
    q_ref,
    nk_ref,
    nv_ref,
    route_ref,
    score_ref,
    k_ref,
    v_ref,
    w_ref,
    sems,
):
    w_cols = w_ref.shape[1] // WEIGHT_COPIES
    copies = start_copies(
        [
            (lens_hbm, lens_ref),
            (q_hbm, q_ref),
            (nk_hbm, nk_ref),
            (nv_hbm, nv_ref),
            (route_hbm, route_ref),
            (score_hbm, score_ref),
            (delta_hbm, delta_ref),
            (k_hbm, k_ref),
            (v_hbm, v_ref),
        ]
        + [
            (w_hbm.at[:, pl.ds(c, w_cols)], w_ref.at[:, pl.ds(c, w_cols)])
            for c in range(0, w_ref.shape[1], w_cols)
        ],
        sems,
    )
    for copy in copies[:-WEIGHT_COPIES]:
        copy.wait()
    seqs = q_ref.shape[0]
    rows = 2 * seqs
    scale = 1.0 / math.sqrt(HD)
    q = q_ref[...].astype(F32)
    queries = jnp.concatenate([q[:, :HD], q[:, HD:]], axis=0)
    nk = nk_ref[...].astype(F32)
    nv = nv_ref[...].astype(F32)
    own_key = jnp.concatenate([nk, nk], axis=0)
    own_value = jnp.concatenate([nv, nv], axis=0)
    row = lax.broadcasted_iota(jnp.int32, (rows, HD), 0) % seqs
    place_in = lax.broadcasted_iota(jnp.int32, (rows, HD), 1)
    queries16 = queries.astype(BF16)
    scores = jnp.zeros((rows, HD), F32)
    length = jnp.zeros((rows, HD), jnp.int32)
    for s in range(seqs):
        scores = jnp.where(row == s, mm_t(queries16, k_ref[s]), scores)
        length = jnp.where(row == s, lens_ref[s], length)
    scores = jnp.where(place_in < length, scores * scale, -jnp.inf)
    own_score = jnp.sum(queries * own_key, axis=1, keepdims=True) * scale
    highest = jnp.maximum(jnp.max(scores, axis=1, keepdims=True), own_score)
    weights = jnp.exp(scores - highest)
    own_weight = jnp.exp(own_score - highest)
    denominator = jnp.sum(weights, axis=1, keepdims=True) + own_weight
    probs = (weights / denominator).astype(BF16)
    own_prob = (own_weight / denominator).astype(BF16).astype(F32)
    mixed = jnp.zeros((rows, HD), F32)
    for s in range(seqs):
        mixed = jnp.where(row == s, mm(probs, v_ref[s]), mixed)
    attn = (mixed + own_prob * own_value).astype(BF16).astype(F32)
    attn_ref[...] = attn
    turned = jnp.concatenate([attn[seqs:], attn[:seqs]], axis=0)
    both = jnp.concatenate([attn, turned], axis=1).astype(BF16)
    blocks = w_ref.shape[1] // HD
    shards = blocks // 4
    for copy in copies[-WEIGHT_COPIES:]:
        copy.wait()
    for first in range(0, blocks, 4):
        part = mm(both, w_ref[:, first * HD : (first + 4) * HD])
        for c in range(4):
            own = rows_at(c * seqs * shards + first // 4, seqs, shards)
            out_ref[own, :] = part[:seqs, c * HD : (c + 1) * HD]
    slots = place_ref.shape[0]
    groups = slots // CAP
    down = lax.broadcasted_iota(jnp.int32, (HD, HD), 0)
    across = lax.broadcasted_iota(jnp.int32, (HD, HD), 1)
    routing = route_ref[...]
    route = routing[0:1]
    target = jnp.broadcast_to(route, (HD, HD))
    target_down = jnp.sum(jnp.where(down == across, target, 0.0), axis=1, keepdims=True)
    earlier = jnp.where(jnp.logical_and(target == target_down, down < across), 1.0, 0.0)
    rank = jnp.sum(earlier, axis=0, keepdims=True)
    slot = lax.broadcasted_iota(jnp.int32, (slots, HD), 0)
    group = (slot % groups).astype(F32)
    order = (slot // groups).astype(F32)
    held = jnp.logical_and(route == group, rank == order)
    place_ref[...] = jnp.where(held, 1.0, 0.0).astype(BF16)
    sent = jnp.where(lax.axis_index("tc") == 0, group, groups - 1 - group)
    held = jnp.logical_and(route == sent, rank == order)
    sent_ref[...] = jnp.where(held, 1.0, 0.0).astype(BF16)
    weight = score_ref[...].astype(F32)
    heads = weight.shape[0] // CORES
    weight = jnp.where(lax.axis_index("tc") == 0, weight[:heads], weight[heads:])
    for h in range(heads):
        own = slice(h * rows // heads, (h + 1) * rows // heads)
        tile_ref[own, :] = jnp.broadcast_to(weight[h : h + 1], (rows // heads, HD))
    block = jnp.broadcast_to(routing[2:3], (8, HD))
    row_block = jnp.floor(block / blocks)
    tile_ref[rows : rows + 8, :] = row_block
    tile_ref[rows + 8 : rows + 16, :] = block - row_block * blocks
    length_ref[...] = jnp.broadcast_to(routing[1:2], length_ref.shape)


def place_kernel(sources, x_ref, attn_ref, place_ref, out_ref, lay_ref):
    each = x_ref.shape[0] // sources
    body = each - 8
    groups = place_ref.shape[0] // CAP
    lay = out_ref.shape[1]
    tile = 2 * lay
    parts = lay // CAP
    heads = parts // PAIR
    seqs = body // parts
    total = x_ref[0:each, :]
    for k in range(1, sources):
        total = total + x_ref[k * each : (k + 1) * each, :]
    inverse = lax.rsqrt(total[body : body + 1, :] / RD + 1e-05) * (math.log2(math.e) / math.sqrt(HD))
    down = lax.broadcasted_iota(jnp.int32, (HD, HD), 0)
    across = lax.broadcasted_iota(jnp.int32, (HD, HD), 1)
    factor = jnp.sum(jnp.where(down == across, inverse, 0.0), axis=1, keepdims=True)
    pieces = []
    for h in range(heads):
        for p in range(PAIR):
            first = (h * PAIR + p) * seqs
            pieces.append(total[first : first + seqs, :] * factor[p * seqs : (p + 1) * seqs, :])
    normed = jnp.concatenate(pieces, axis=1)
    if seqs < HD:
        normed = jnp.concatenate([normed, jnp.zeros((HD - seqs, parts * HD), F32)], axis=0)
    place = place_ref[...]
    for k, term in enumerate(split2(normed)):
        placed = mm(place, term)
        for r in range(CAP):
            for q in range(parts):
                row = k * lay + (q // PAIR) * CAP * PAIR + r * PAIR + q % PAIR
                lay_ref[rows_at(row, groups, tile), :] = placed[
                    r * groups : (r + 1) * groups, q * HD : (q + 1) * HD
                ]
    attn = attn_ref[...].astype(BF16)
    for g in range(groups):
        for k in range(2):
            own = slice(g * tile + k * lay, g * tile + (k + 1) * lay)
            out_ref[3 * g + k] = lay_ref[own, :].astype(BF16)
        out_ref[3 * g + 2] = attn


def score_kernel(
    seqs, x_ref, keys_ref, values_ref, weight_ref, delta_ref, out_ref, lay_ref, in_order_ref
):
    tile = 2 * seqs
    senders = x_ref.shape[0] // 3
    keys = keys_ref[...]
    keys2 = jnp.concatenate([keys, keys], axis=1)
    values = values_ref[...]
    weight = weight_ref[0:tile, :][None]
    row_block = weight_ref[tile : tile + 1, :][None]
    column = weight_ref[tile + 8 : tile + 9, :]
    delta = delta_ref[...]
    at_once = min(AT_ONCE, senders)
    row = lax.broadcasted_iota(jnp.int32, (1, tile, HD), 1)
    core = lax.axis_index("tc")
    for w in range(senders):
        came = jnp.where(core == 0, w, senders - 1 - w)
        for k in range(3):
            in_order_ref[3 * w + k] = x_ref[3 * came + k]
    started = []
    for first in range(0, senders, at_once):
        x = in_order_ref[3 * first : 3 * (first + at_once)].astype(F32)
        x = x.reshape(at_once, 3, tile, HD)
        flat = [x[:, k].reshape(at_once * tile, HD).astype(BF16) for k in range(3)]
        scores = mm_t(jnp.concatenate(flat[:2], axis=1), keys2)
        started.append((first, scores, mm(flat[2], delta)))
    for first, scores, product in started:
        highest = jnp.max(scores, axis=1, keepdims=True)
        weights = jnp.exp2(scores - highest)
        probs = (weights * (1.0 / jnp.sum(weights, axis=1, keepdims=True))).astype(BF16)
        context = mm(probs, values)
        gated = context / (1.0 + jnp.exp(-context))
        terms = gated.reshape(at_once, tile, HD) * weight
        by_head = jnp.broadcast_to(jnp.sum(terms, axis=2, keepdims=True), terms.shape)
        score = by_head + jnp.concatenate([by_head[:, seqs:], by_head[:, :seqs]], axis=1)
        product = product.reshape(at_once, tile, HD)
        turned = jnp.concatenate([product[:, seqs:], product[:, :seqs]], axis=1)
        result = jnp.where(row_block == 0.0, product, turned)
        result = jnp.where(row < seqs, result, score)
        span = slice(first * tile, (first + at_once) * tile)
        lay_ref[span, :] = result.reshape(at_once * tile, HD)
    for q in range(seqs):
        out_ref[rows_at(q, senders, seqs + 1), :] = lay_ref[rows_at(q, senders, tile), :]
    lane = lax.broadcasted_iota(jnp.int32, (senders, HD), 1)
    last = jnp.broadcast_to(column, (senders, HD))
    for q in range(seqs):
        last = jnp.where(lane == q, lay_ref[rows_at(seqs + q, senders, tile), :], last)
    out_ref[rows_at(seqs, senders, seqs + 1), :] = last


def merge_kernel(seqs, shards, x_ref, partial_ref, place_ref, out_ref):
    each = seqs + 1
    senders = x_ref.shape[0] // each
    blocks = partial_ref.shape[0] // seqs - 8
    own_blocks = blocks // shards
    message = out_ref.shape[0] // shards
    last = x_ref[rows_at(seqs, senders, each), :]
    column = last[:, HD - 1 :]
    pieces = split3(
        jnp.concatenate([x_ref[rows_at(s, senders, each), :] for s in range(seqs)], axis=1)
    )
    down = lax.broadcasted_iota(jnp.int32, (senders, senders), 0)
    across = lax.broadcasted_iota(jnp.int32, (senders, senders), 1)
    column_across = jnp.sum(
        jnp.where(down == across, jnp.broadcast_to(column, (senders, senders)), 0.0),
        axis=0,
        keepdims=True,
    )
    order = lax.broadcasted_iota(jnp.int32, (blocks, senders), 0)
    wanted = (order % shards * own_blocks + order // shards).astype(F32)
    pick = jnp.where(wanted == column_across, 1.0, 0.0).astype(BF16)
    high, mid, low = pieces
    added = (mm(pick, low) + mm(pick, mid)) + mm(pick, high)
    for c in range(own_blocks):
        for s in range(seqs):
            q = c * seqs + s
            out_ref[rows_at(q, shards, message), :] = (
                partial_ref[q * shards : (q + 1) * shards, :]
                + added[c * shards : (c + 1) * shards, s * HD : (s + 1) * HD]
            )
    place = place_ref[...].astype(F32)
    for p in range(PAIR):
        score = jnp.concatenate(
            [last[:, r * PAIR + p : r * PAIR + p + 1] for r in range(CAP)], axis=0
        )
        back = jnp.sum(place * score, axis=0, keepdims=True)
        out_ref[rows_at(own_blocks * seqs + p, shards, message), :] = jnp.broadcast_to(
            back, (shards, HD)
        )


def final_kernel(shards, x_ref, length_ref, decoded_ref, rewards_ref):
    each = x_ref.shape[0] // shards
    seqs = decoded_ref.shape[0]
    body = each - PAIR
    rows = [x_ref[rows_at(q, shards, each), :] for q in range(each)]
    sums = [jnp.sum(row, axis=0, keepdims=True) for row in rows[:body]]
    for c in range(body // seqs):
        block = jnp.concatenate(sums[c * seqs : (c + 1) * seqs], axis=0)
        decoded_ref[:, c * HD : (c + 1) * HD] = block.astype(BF16)
    length = length_ref[0:1, :]
    count = rewards_ref.shape[1]
    shard = lax.broadcasted_iota(jnp.int32, (shards, HD), 0)
    reward = jnp.zeros((1, HD), F32)
    for p in range(PAIR):
        token = (shard // CORES * PAIR + p).astype(F32)
        scored = jnp.where(length > token, rows[body + p], 0.0)
        reward = reward + jnp.sum(scored, axis=0, keepdims=True)
    rewards_ref[...] = (reward / length)[:, :count]


def per_device(
    query,
    key_cache,
    value_cache,
    new_key,
    new_value,
    cache_lengths,
    out_weight,
    delta_index,
    delta_values,
    fin_route,
    fin_lengths,
    fin_rows,
    reward_query,
    rubric_keys,
    rubric_values,
    score_weight,
):
    wide_count = lax.axis_size("wide")
    chips = lax.axis_size("th")
    tp_count = chips * lax.axis_size("tc")
    finished, row_len, features = fin_rows.shape
    heads = reward_query.shape[1] // HD // CORES
    seq_count = query.shape[0]
    tile = 2 * seq_count
    blocks = out_weight.shape[1] // HD
    slots = CAP * wide_count
    parts = PAIR * heads
    message = parts * finished + 8
    shape = jax.ShapeDtypeStruct

    rows = fin_rows.reshape(finished * row_len, features)
    partial = shape((chips * message, HD), F32)
    squares_shape = shape((chips * 8, HD), F32)
    acc = pltpu.VMEM((heads * finished * row_len, HD), F32)
    theirs, squares, rows, weights = local_call(
        functools.partial(project_kernel, False, row_len),
        "project_theirs",
        (rows, reward_query),
        [partial, squares_shape, shape(rows.shape, BF16), shape(reward_query.shape, BF16)],
        [
            acc,
            pltpu.VMEM((finished * row_len, HD), F32),
            pltpu.SemaphoreType.DMA((2 * FEATURE_COPIES + 1,)),
        ],
        fetched=2,
    )
    got = lax.ppermute(theirs, "tc", [(0, 1), (1, 0)])
    (kept,) = local_call(
        functools.partial(project_kernel, True, row_len),
        "project_kept",
        (squares, rows, weights),
        [partial],
        [acc],
    )
    (both,) = local_call(add_kernel, "add", (kept, got), [partial])
    summed_tokens = lax.all_to_all(
        both.reshape(chips, message, HD), "th", split_axis=0, concat_axis=0, tiled=True
    ).reshape(partial.shape)

    pad = ((0, 0), (0, HD - finished))
    routing = jnp.concatenate(
        [
            jnp.pad(fin_route.reshape(1, finished), pad, constant_values=-1),
            jnp.pad(fin_lengths.reshape(1, finished), pad, constant_values=1),
            jnp.broadcast_to(delta_index.reshape(1, 1), (1, HD)),
        ]
    ).astype(F32)
    weights = score_weight.reshape(heads * CORES, HD)
    small = (cache_lengths, query, new_key, new_value, routing, weights, delta_values[0])
    large = (key_cache, value_cache, out_weight)
    attn, partial_out, place, sent, weight_tile, delta, lengths = local_call(
        decode_kernel,
        "decode",
        small + large,
        [
            shape((tile, HD), F32),
            shape(((blocks + 8) * seq_count, HD), F32),
            shape((slots, HD), BF16),
            shape((slots, HD), BF16),
            shape((tile + 16, HD), F32),
            shape(delta_values.shape[1:], BF16),
            shape((8, HD), F32),
        ],
        [pltpu.SMEM(cache_lengths.shape, jnp.int32)]
        + [pltpu.VMEM(a.shape, a.dtype) for a in small[1:-1] + large]
        + [pltpu.SemaphoreType.DMA((len(small) + 2 + WEIGHT_COPIES,))],
        fetched=len(small) + len(large),
    )

    lay = CAP * parts
    (outgoing,) = local_call(
        functools.partial(place_kernel, chips),
        "place",
        (summed_tokens, attn, sent),
        [shape((wide_count * 3, lay, HD), BF16)],
        [pltpu.VMEM((wide_count * 2 * lay, HD), F32)],
    )
    received = exchange_both_ways(outgoing)

    answer = seq_count + 1
    (answers,) = local_call(
        functools.partial(score_kernel, seq_count),
        "score",
        (
            received,
            rubric_keys[0],
            rubric_values[0],
            weight_tile,
            delta,
        ),
        [shape((wide_count * answer, HD), F32)],
        [pltpu.VMEM((wide_count * tile, HD), F32), pltpu.VMEM(received.shape, BF16)],
    )
    returned = lax.all_to_all(
        answers.reshape(wide_count, 1, answer * HD), "wide", split_axis=0, concat_axis=0, tiled=True
    ).reshape(answers.shape)

    share = blocks // tp_count * seq_count + PAIR
    (merged,) = local_call(
        functools.partial(merge_kernel, seq_count, tp_count),
        "merge",
        (returned, partial_out, place),
        [shape((tp_count * share, HD), F32)],
    )
    shares = lax.all_to_all(
        merged.reshape(tp_count, 1, share * HD),
        ("th", "tc"),
        split_axis=0,
        concat_axis=0,
        tiled=True,
    ).reshape(merged.shape)

    decoded, rewards = local_call(
        functools.partial(final_kernel, tp_count),
        "final",
        (shares, lengths),
        [shape((seq_count, blocks // tp_count * HD), BF16), shape((1, finished), F32)],
    )
    return decoded, rewards.reshape(finished)


def solution(mesh):
    tp = ("th", "tc")
    wide_count, tp_count = mesh.devices.shape
    split = jax.sharding.Mesh(
        mesh.devices.reshape(wide_count, tp_count // CORES, CORES), ("wide",) + tp
    )
    in_specs = (
        P("wide", tp),
        P("wide", None, tp),
        P("wide", None, tp),
        P("wide", tp),
        P("wide", tp),
        P("wide"),
        P(tp, None),
        P("wide"),
        P("wide", tp, None),
        P("wide", None),
        P("wide"),
        P("wide", None, tp),
        P(tp, None),
        P("wide", None, None),
        P("wide", None, None),
        P(),
    )
    out_specs = (P("wide", tp), P("wide"))
    return jax.shard_map(
        per_device, mesh=split, in_specs=in_specs, out_specs=out_specs, check_vma=False
    )
```

```python
import functools
import math

import jax
import jax.numpy as jnp
from jax import lax
from jax.experimental import pallas as pl
from jax.experimental.pallas import tpu as pltpu
from jax.sharding import PartitionSpec as P

HD = 128
RD = 8192
CAP = 2
CORES = 2
PAIR = 2
AXES = ("wide", "th", "tc")
VMEM_LIMIT = 16 * 2**20
WEIGHT_COPIES = 4
FEATURE_COPIES = 2
AT_ONCE = 32
F32 = jnp.float32
BF16 = jnp.bfloat16


def split2(x):
    high = x.astype(BF16)
    return high, (x - high.astype(F32)).astype(BF16)


def split3(x):
    high, mid = split2(x)
    return high, mid, (x - high.astype(F32) - mid.astype(F32)).astype(BF16)


def mm(a, b):
    return jnp.dot(a, b, preferred_element_type=F32)


def mm_t(a, b):
    return lax.dot_general(a, b, (((1,), (1,)), ((), ())), preferred_element_type=F32)


def rows_at(first, count, stride):
    return pl.ds(first, count, stride=stride)


def local_call(kernel, name, operands, outs, scratch=(), fetched=0):
    vmem = pl.BlockSpec(memory_space=pltpu.VMEM)
    hbm = pl.BlockSpec(memory_space=pltpu.HBM)
    kept = len(operands) - fetched
    operands = list(operands[:kept]) + [
        pltpu.with_memory_space_constraint(a, pltpu.HBM) for a in operands[kept:]
    ]
    return pl.pallas_call(
        kernel,
        in_specs=[vmem] * kept + [hbm] * fetched,
        out_specs=[vmem] * len(outs),
        out_shape=outs,
        scratch_shapes=list(scratch),
        compiler_params=pltpu.CompilerParams(vmem_limit_bytes=VMEM_LIMIT),
        name=name,
    )(*operands)


def start_copies(pairs, sems):
    copies = [pltpu.make_async_copy(a, b, sems.at[k]) for k, (a, b) in enumerate(pairs)]
    for copy in copies:
        copy.start()
    return copies


def project_kernel(mine, row_len, *refs):
    if mine:
        squares_ref, rows_ref, wq_ref, out_ref, acc_ref = refs
    else:
        rows_hbm, wq_hbm, out_ref, squares_ref, rows_ref, wq_ref, acc_ref, sq_ref, sems = refs
    many = rows_ref.shape[0]
    width = wq_ref.shape[1] // CORES
    heads = width // HD
    core = lax.axis_index("tc")
    half = core if mine else 1 - core
    columns = pl.ds(pl.multiple_of(half * width, width), width)
    steps = 1 if mine else FEATURE_COPIES
    depth = wq_ref.shape[0] // steps
    spans = [pl.ds(k * depth, depth) for k in range(steps)]
    if not mine:
        kept = pl.ds(pl.multiple_of(core * width, width), width)
        pieces = []
        for k in spans:
            pieces += [(wq_hbm.at[k, columns], wq_ref.at[k, columns])]
            pieces += [(rows_hbm.at[:, k], rows_ref.at[:, k])]
        pieces += [(wq_hbm.at[:, kept], wq_ref.at[:, kept])]
        copies = start_copies(pieces, sems)
    chunk = many // row_len
    pairs = row_len // PAIR
    each = out_ref.shape[0] // pairs
    body = each - 8
    seqs = body // (heads * PAIR)
    product = sums = None
    for step, k in enumerate(spans):
        if not mine:
            copies[2 * step].wait()
            copies[2 * step + 1].wait()
        rows = rows_ref[:, k]
        part = mm(rows, wq_ref[k, columns])
        product = part if product is None else product + part
        if not mine:
            wide_rows = rows.astype(F32)
            wide_rows = wide_rows * wide_rows
            for first in range(0, depth, HD):
                slab = wide_rows[:, first : first + HD]
                sums = slab if sums is None else sums + slab
    for h in range(heads):
        acc_ref[h * many : (h + 1) * many, :] = product[:, h * HD : (h + 1) * HD]
    for t in range(row_len):
        for h in range(heads):
            first = (t // PAIR) * each + (h * PAIR + t % PAIR) * seqs
            out_ref[first : first + chunk, :] = acc_ref[rows_at(h * many + t, chunk, row_len), :]
    if mine:
        for p in range(pairs):
            tail = slice(p * each + body, (p + 1) * each)
            out_ref[tail, :] = squares_ref[p * 8 : (p + 1) * 8, :]
        return
    sq_ref[...] = jnp.broadcast_to(jnp.sum(sums, axis=1, keepdims=True), sq_ref.shape)
    across = lax.broadcasted_iota(jnp.int32, (chunk, HD), 0)
    lane = lax.broadcasted_iota(jnp.int32, (chunk, HD), 1)
    for p in range(pairs):
        total = jnp.zeros((1, HD), F32)
        for t in range(p * PAIR, (p + 1) * PAIR):
            spot = lane == across + (t % PAIR) * seqs
            picked = jnp.where(spot, sq_ref[rows_at(t, chunk, row_len), :], 0.0)
            total += jnp.sum(picked, axis=0, keepdims=True)
        tail = jnp.broadcast_to(total, (8, HD))
        squares_ref[p * 8 : (p + 1) * 8, :] = tail
        out_ref[p * each + body : (p + 1) * each, :] = tail
    copies[-1].wait()


def add_kernel(a_ref, b_ref, out_ref):
    out_ref[...] = a_ref[...] + b_ref[...]


def exchange_both_ways(x):
    wide_count, chips, cores = (lax.axis_size(name) for name in AXES)
    groups = []
    for core in range(cores):
        for chip in range(chips):
            group = [(w * chips + chip) * cores + core for w in range(wide_count)]
            groups.append(group if core == 1 else group[::-1])
    return lax.all_to_all(
        x, AXES, split_axis=0, concat_axis=0, axis_index_groups=groups, tiled=True
    )


def decode_kernel(
    lens_hbm,
    q_hbm,
    nk_hbm,
    nv_hbm,
    route_hbm,
    score_hbm,
    delta_hbm,
    k_hbm,
    v_hbm,
    w_hbm,
    attn_ref,
    out_ref,
    place_ref,
    sent_ref,
    tile_ref,
    delta_ref,
    length_ref,
    lens_ref,
    q_ref,
    nk_ref,
    nv_ref,
    route_ref,
    score_ref,
    k_ref,
    v_ref,
    w_ref,
    sems,
):
    w_cols = w_ref.shape[1] // WEIGHT_COPIES
    copies = start_copies(
        [
            (lens_hbm, lens_ref),
            (q_hbm, q_ref),
            (nk_hbm, nk_ref),
            (nv_hbm, nv_ref),
            (route_hbm, route_ref),
            (score_hbm, score_ref),
            (delta_hbm, delta_ref),
            (k_hbm, k_ref),
            (v_hbm, v_ref),
        ]
        + [
            (w_hbm.at[:, pl.ds(c, w_cols)], w_ref.at[:, pl.ds(c, w_cols)])
            for c in range(0, w_ref.shape[1], w_cols)
        ],
        sems,
    )
    for copy in copies[:-WEIGHT_COPIES]:
        copy.wait()
    seqs = q_ref.shape[0]
    rows = 2 * seqs
    scale = 1.0 / math.sqrt(HD)
    q = q_ref[...].astype(F32)
    queries = jnp.concatenate([q[:, :HD], q[:, HD:]], axis=0)
    nk = nk_ref[...].astype(F32)
    nv = nv_ref[...].astype(F32)
    own_key = jnp.concatenate([nk, nk], axis=0)
    own_value = jnp.concatenate([nv, nv], axis=0)
    row = lax.broadcasted_iota(jnp.int32, (rows, HD), 0) % seqs
    place_in = lax.broadcasted_iota(jnp.int32, (rows, HD), 1)
    queries16 = queries.astype(BF16)
    scores = jnp.zeros((rows, HD), F32)
    length = jnp.zeros((rows, HD), jnp.int32)
    for s in range(seqs):
        scores = jnp.where(row == s, mm_t(queries16, k_ref[s]), scores)
        length = jnp.where(row == s, lens_ref[s], length)
    scores = jnp.where(place_in < length, scores * scale, -jnp.inf)
    own_score = jnp.sum(queries * own_key, axis=1, keepdims=True) * scale
    highest = jnp.maximum(jnp.max(scores, axis=1, keepdims=True), own_score)
    weights = jnp.exp(scores - highest)
    own_weight = jnp.exp(own_score - highest)
    denominator = jnp.sum(weights, axis=1, keepdims=True) + own_weight
    probs = (weights / denominator).astype(BF16)
    own_prob = (own_weight / denominator).astype(BF16).astype(F32)
    mixed = jnp.zeros((rows, HD), F32)
    for s in range(seqs):
        mixed = jnp.where(row == s, mm(probs, v_ref[s]), mixed)
    attn = (mixed + own_prob * own_value).astype(BF16).astype(F32)
    attn_ref[...] = attn
    turned = jnp.concatenate([attn[seqs:], attn[:seqs]], axis=0)
    both = jnp.concatenate([attn, turned], axis=1).astype(BF16)
    blocks = w_ref.shape[1] // HD
    shards = blocks // 4
    for copy in copies[-WEIGHT_COPIES:]:
        copy.wait()
    for first in range(0, blocks, 4):
        part = mm(both, w_ref[:, first * HD : (first + 4) * HD])
        for c in range(4):
            own = rows_at(c * seqs * shards + first // 4, seqs, shards)
            out_ref[own, :] = part[:seqs, c * HD : (c + 1) * HD]
    slots = place_ref.shape[0]
    groups = slots // CAP
    down = lax.broadcasted_iota(jnp.int32, (HD, HD), 0)
    across = lax.broadcasted_iota(jnp.int32, (HD, HD), 1)
    routing = route_ref[...]
    route = routing[0:1]
    target = jnp.broadcast_to(route, (HD, HD))
    target_down = jnp.sum(jnp.where(down == across, target, 0.0), axis=1, keepdims=True)
    earlier = jnp.where(jnp.logical_and(target == target_down, down < across), 1.0, 0.0)
    rank = jnp.sum(earlier, axis=0, keepdims=True)
    slot = lax.broadcasted_iota(jnp.int32, (slots, HD), 0)
    group = (slot % groups).astype(F32)
    order = (slot // groups).astype(F32)
    held = jnp.logical_and(route == group, rank == order)
    place_ref[...] = jnp.where(held, 1.0, 0.0).astype(BF16)
    sent = jnp.where(lax.axis_index("tc") == 1, group, groups - 1 - group)
    held = jnp.logical_and(route == sent, rank == order)
    sent_ref[...] = jnp.where(held, 1.0, 0.0).astype(BF16)
    weight = score_ref[...].astype(F32)
    heads = weight.shape[0] // CORES
    weight = jnp.where(lax.axis_index("tc") == 0, weight[:heads], weight[heads:])
    for h in range(heads):
        own = slice(h * rows // heads, (h + 1) * rows // heads)
        tile_ref[own, :] = jnp.broadcast_to(weight[h : h + 1], (rows // heads, HD))
    block = jnp.broadcast_to(routing[2:3], (8, HD))
    row_block = jnp.floor(block / blocks)
    tile_ref[rows : rows + 8, :] = row_block
    tile_ref[rows + 8 : rows + 16, :] = block - row_block * blocks
    length_ref[...] = jnp.broadcast_to(routing[1:2], length_ref.shape)


def place_kernel(sources, x_ref, attn_ref, place_ref, out_ref, lay_ref):
    each = x_ref.shape[0] // sources
    body = each - 8
    groups = place_ref.shape[0] // CAP
    lay = out_ref.shape[1]
    tile = 2 * lay
    parts = lay // CAP
    heads = parts // PAIR
    seqs = body // parts
    total = x_ref[0:each, :]
    for k in range(1, sources):
        total = total + x_ref[k * each : (k + 1) * each, :]
    inverse = lax.rsqrt(total[body : body + 1, :] / RD + 1e-05) * (math.log2(math.e) / math.sqrt(HD))
    down = lax.broadcasted_iota(jnp.int32, (HD, HD), 0)
    across = lax.broadcasted_iota(jnp.int32, (HD, HD), 1)
    factor = jnp.sum(jnp.where(down == across, inverse, 0.0), axis=1, keepdims=True)
    pieces = []
    for h in range(heads):
        for p in range(PAIR):
            first = (h * PAIR + p) * seqs
            pieces.append(total[first : first + seqs, :] * factor[p * seqs : (p + 1) * seqs, :])
    normed = jnp.concatenate(pieces, axis=1)
    if seqs < HD:
        normed = jnp.concatenate([normed, jnp.zeros((HD - seqs, parts * HD), F32)], axis=0)
    place = place_ref[...]
    for k, term in enumerate(split2(normed)):
        placed = mm(place, term)
        for r in range(CAP):
            for q in range(parts):
                row = k * lay + (q // PAIR) * CAP * PAIR + r * PAIR + q % PAIR
                lay_ref[rows_at(row, groups, tile), :] = placed[
                    r * groups : (r + 1) * groups, q * HD : (q + 1) * HD
                ]
    attn = attn_ref[...].astype(BF16)
    for g in range(groups):
        for k in range(2):
            own = slice(g * tile + k * lay, g * tile + (k + 1) * lay)
            out_ref[3 * g + k] = lay_ref[own, :].astype(BF16)
        out_ref[3 * g + 2] = attn


def score_kernel(
    seqs, x_ref, keys_ref, values_ref, weight_ref, delta_ref, out_ref, lay_ref, in_order_ref
):
    tile = 2 * seqs
    senders = x_ref.shape[0] // 3
    keys = keys_ref[...]
    keys2 = jnp.concatenate([keys, keys], axis=1)
    values = values_ref[...]
    weight = weight_ref[0:tile, :][None]
    row_block = weight_ref[tile : tile + 1, :][None]
    column = weight_ref[tile + 8 : tile + 9, :]
    delta = delta_ref[...]
    at_once = min(AT_ONCE, senders)
    row = lax.broadcasted_iota(jnp.int32, (1, tile, HD), 1)
    core = lax.axis_index("tc")
    for w in range(senders):
        came = jnp.where(core == 1, w, senders - 1 - w)
        for k in range(3):
            in_order_ref[3 * w + k] = x_ref[3 * came + k]
    started = []
    for first in range(0, senders, at_once):
        x = in_order_ref[3 * first : 3 * (first + at_once)].astype(F32)
        x = x.reshape(at_once, 3, tile, HD)
        flat = [x[:, k].reshape(at_once * tile, HD).astype(BF16) for k in range(3)]
        scores = mm_t(jnp.concatenate(flat[:2], axis=1), keys2)
        started.append((first, scores, mm(flat[2], delta)))
    for first, scores, product in started:
        highest = jnp.max(scores, axis=1, keepdims=True)
        weights = jnp.exp2(scores - highest)
        probs = (weights * (1.0 / jnp.sum(weights, axis=1, keepdims=True))).astype(BF16)
        context = mm(probs, values)
        gated = context / (1.0 + jnp.exp(-context))
        terms = gated.reshape(at_once, tile, HD) * weight
        by_head = jnp.broadcast_to(jnp.sum(terms, axis=2, keepdims=True), terms.shape)
        score = by_head + jnp.concatenate([by_head[:, seqs:], by_head[:, :seqs]], axis=1)
        product = product.reshape(at_once, tile, HD)
        turned = jnp.concatenate([product[:, seqs:], product[:, :seqs]], axis=1)
        result = jnp.where(row_block == 0.0, product, turned)
        result = jnp.where(row < seqs, result, score)
        span = slice(first * tile, (first + at_once) * tile)
        lay_ref[span, :] = result.reshape(at_once * tile, HD)
    for q in range(seqs):
        out_ref[rows_at(q, senders, seqs + 1), :] = lay_ref[rows_at(q, senders, tile), :]
    lane = lax.broadcasted_iota(jnp.int32, (senders, HD), 1)
    last = jnp.broadcast_to(column, (senders, HD))
    for q in range(seqs):
        last = jnp.where(lane == q, lay_ref[rows_at(seqs + q, senders, tile), :], last)
    out_ref[rows_at(seqs, senders, seqs + 1), :] = last


def merge_kernel(seqs, shards, x_ref, partial_ref, place_ref, out_ref):
    each = seqs + 1
    senders = x_ref.shape[0] // each
    blocks = partial_ref.shape[0] // seqs - 8
    own_blocks = blocks // shards
    message = out_ref.shape[0] // shards
    last = x_ref[rows_at(seqs, senders, each), :]
    column = last[:, HD - 1 :]
    pieces = split3(
        jnp.concatenate([x_ref[rows_at(s, senders, each), :] for s in range(seqs)], axis=1)
    )
    down = lax.broadcasted_iota(jnp.int32, (senders, senders), 0)
    across = lax.broadcasted_iota(jnp.int32, (senders, senders), 1)
    column_across = jnp.sum(
        jnp.where(down == across, jnp.broadcast_to(column, (senders, senders)), 0.0),
        axis=0,
        keepdims=True,
    )
    order = lax.broadcasted_iota(jnp.int32, (blocks, senders), 0)
    wanted = (order % shards * own_blocks + order // shards).astype(F32)
    pick = jnp.where(wanted == column_across, 1.0, 0.0).astype(BF16)
    high, mid, low = pieces
    added = (mm(pick, low) + mm(pick, mid)) + mm(pick, high)
    for c in range(own_blocks):
        for s in range(seqs):
            q = c * seqs + s
            out_ref[rows_at(q, shards, message), :] = (
                partial_ref[q * shards : (q + 1) * shards, :]
                + added[c * shards : (c + 1) * shards, s * HD : (s + 1) * HD]
            )
    place = place_ref[...].astype(F32)
    for p in range(PAIR):
        score = jnp.concatenate(
            [last[:, r * PAIR + p : r * PAIR + p + 1] for r in range(CAP)], axis=0
        )
        back = jnp.sum(place * score, axis=0, keepdims=True)
        out_ref[rows_at(own_blocks * seqs + p, shards, message), :] = jnp.broadcast_to(
            back, (shards, HD)
        )


def final_kernel(shards, x_ref, length_ref, decoded_ref, rewards_ref):
    each = x_ref.shape[0] // shards
    seqs = decoded_ref.shape[0]
    body = each - PAIR
    rows = [x_ref[rows_at(q, shards, each), :] for q in range(each)]
    sums = [jnp.sum(row, axis=0, keepdims=True) for row in rows[:body]]
    for c in range(body // seqs):
        block = jnp.concatenate(sums[c * seqs : (c + 1) * seqs], axis=0)
        decoded_ref[:, c * HD : (c + 1) * HD] = block.astype(BF16)
    length = length_ref[0:1, :]
    count = rewards_ref.shape[1]
    shard = lax.broadcasted_iota(jnp.int32, (shards, HD), 0)
    reward = jnp.zeros((1, HD), F32)
    for p in range(PAIR):
        token = (shard // CORES * PAIR + p).astype(F32)
        scored = jnp.where(length > token, rows[body + p], 0.0)
        reward = reward + jnp.sum(scored, axis=0, keepdims=True)
    rewards_ref[...] = (reward / length)[:, :count]


def per_device(
    query,
    key_cache,
    value_cache,
    new_key,
    new_value,
    cache_lengths,
    out_weight,
    delta_index,
    delta_values,
    fin_route,
    fin_lengths,
    fin_rows,
    reward_query,
    rubric_keys,
    rubric_values,
    score_weight,
):
    wide_count = lax.axis_size("wide")
    chips = lax.axis_size("th")
    tp_count = chips * lax.axis_size("tc")
    finished, row_len, features = fin_rows.shape
    heads = reward_query.shape[1] // HD // CORES
    seq_count = query.shape[0]
    tile = 2 * seq_count
    blocks = out_weight.shape[1] // HD
    slots = CAP * wide_count
    parts = PAIR * heads
    message = parts * finished + 8
    shape = jax.ShapeDtypeStruct

    rows = fin_rows.reshape(finished * row_len, features)
    partial = shape((chips * message, HD), F32)
    squares_shape = shape((chips * 8, HD), F32)
    acc = pltpu.VMEM((heads * finished * row_len, HD), F32)
    theirs, squares, rows, weights = local_call(
        functools.partial(project_kernel, False, row_len),
        "project_theirs",
        (rows, reward_query),
        [partial, squares_shape, shape(rows.shape, BF16), shape(reward_query.shape, BF16)],
        [
            acc,
            pltpu.VMEM((finished * row_len, HD), F32),
            pltpu.SemaphoreType.DMA((2 * FEATURE_COPIES + 1,)),
        ],
        fetched=2,
    )
    got = lax.ppermute(theirs, "tc", [(0, 1), (1, 0)])
    (kept,) = local_call(
        functools.partial(project_kernel, True, row_len),
        "project_kept",
        (squares, rows, weights),
        [partial],
        [acc],
    )
    (both,) = local_call(add_kernel, "add", (kept, got), [partial])
    summed_tokens = lax.all_to_all(
        both.reshape(chips, message, HD), "th", split_axis=0, concat_axis=0, tiled=True
    ).reshape(partial.shape)

    pad = ((0, 0), (0, HD - finished))
    routing = jnp.concatenate(
        [
            jnp.pad(fin_route.reshape(1, finished), pad, constant_values=-1),
            jnp.pad(fin_lengths.reshape(1, finished), pad, constant_values=1),
            jnp.broadcast_to(delta_index.reshape(1, 1), (1, HD)),
        ]
    ).astype(F32)
    weights = score_weight.reshape(heads * CORES, HD)
    small = (cache_lengths, query, new_key, new_value, routing, weights, delta_values[0])
    large = (key_cache, value_cache, out_weight)
    attn, partial_out, place, sent, weight_tile, delta, lengths = local_call(
        decode_kernel,
        "decode",
        small + large,
        [
            shape((tile, HD), F32),
            shape(((blocks + 8) * seq_count, HD), F32),
            shape((slots, HD), BF16),
            shape((slots, HD), BF16),
            shape((tile + 16, HD), F32),
            shape(delta_values.shape[1:], BF16),
            shape((8, HD), F32),
        ],
        [pltpu.SMEM(cache_lengths.shape, jnp.int32)]
        + [pltpu.VMEM(a.shape, a.dtype) for a in small[1:-1] + large]
        + [pltpu.SemaphoreType.DMA((len(small) + 2 + WEIGHT_COPIES,))],
        fetched=len(small) + len(large),
    )

    lay = CAP * parts
    (outgoing,) = local_call(
        functools.partial(place_kernel, chips),
        "place",
        (summed_tokens, attn, sent),
        [shape((wide_count * 3, lay, HD), BF16)],
        [pltpu.VMEM((wide_count * 2 * lay, HD), F32)],
    )
    received = exchange_both_ways(outgoing)

    answer = seq_count + 1
    (answers,) = local_call(
        functools.partial(score_kernel, seq_count),
        "score",
        (
            received,
            rubric_keys[0],
            rubric_values[0],
            weight_tile,
            delta,
        ),
        [shape((wide_count * answer, HD), F32)],
        [pltpu.VMEM((wide_count * tile, HD), F32), pltpu.VMEM(received.shape, BF16)],
    )
    returned = lax.all_to_all(
        answers.reshape(wide_count, 1, answer * HD), "wide", split_axis=0, concat_axis=0, tiled=True
    ).reshape(answers.shape)

    share = blocks // tp_count * seq_count + PAIR
    (merged,) = local_call(
        functools.partial(merge_kernel, seq_count, tp_count),
        "merge",
        (returned, partial_out, place),
        [shape((tp_count * share, HD), F32)],
    )
    shares = lax.all_to_all(
        merged.reshape(tp_count, 1, share * HD),
        ("th", "tc"),
        split_axis=0,
        concat_axis=0,
        tiled=True,
    ).reshape(merged.shape)

    decoded, rewards = local_call(
        functools.partial(final_kernel, tp_count),
        "final",
        (shares, lengths),
        [shape((seq_count, blocks // tp_count * HD), BF16), shape((1, finished), F32)],
    )
    return decoded, rewards.reshape(finished)


def solution(mesh):
    tp = ("th", "tc")
    wide_count, tp_count = mesh.devices.shape
    split = jax.sharding.Mesh(
        mesh.devices.reshape(wide_count, tp_count // CORES, CORES), ("wide",) + tp
    )
    in_specs = (
        P("wide", tp),
        P("wide", None, tp),
        P("wide", None, tp),
        P("wide", tp),
        P("wide", tp),
        P("wide"),
        P(tp, None),
        P("wide"),
        P("wide", tp, None),
        P("wide", None),
        P("wide"),
        P("wide", None, tp),
        P(tp, None),
        P("wide", None, None),
        P("wide", None, None),
        P(),
    )
    out_specs = (P("wide", tp), P("wide"))
    return jax.shard_map(
        per_device, mesh=split, in_specs=in_specs, out_specs=out_specs, check_vma=False
    )
```

```python
import functools
import math

import jax
import jax.numpy as jnp
from jax import lax
from jax.experimental import pallas as pl
from jax.experimental.pallas import tpu as pltpu
from jax.sharding import PartitionSpec as P

HD = 128
RD = 8192
CAP = 2
CORES = 2
PAIR = 2
AXES = ("wide", "th", "tc")
VMEM_LIMIT = 16 * 2**20
WEIGHT_COPIES = 4
FEATURE_COPIES = 2
AT_ONCE = 32
F32 = jnp.float32
BF16 = jnp.bfloat16


def split2(x):
    high = x.astype(BF16)
    return high, (x - high.astype(F32)).astype(BF16)


def split3(x):
    high, mid = split2(x)
    return high, mid, (x - high.astype(F32) - mid.astype(F32)).astype(BF16)


def mm(a, b):
    return jnp.dot(a, b, preferred_element_type=F32)


def mm_t(a, b):
    return lax.dot_general(a, b, (((1,), (1,)), ((), ())), preferred_element_type=F32)


def rows_at(first, count, stride):
    return pl.ds(first, count, stride=stride)


def local_call(kernel, name, operands, outs, scratch=(), fetched=0):
    vmem = pl.BlockSpec(memory_space=pltpu.VMEM)
    hbm = pl.BlockSpec(memory_space=pltpu.HBM)
    kept = len(operands) - fetched
    operands = list(operands[:kept]) + [
        pltpu.with_memory_space_constraint(a, pltpu.HBM) for a in operands[kept:]
    ]
    return pl.pallas_call(
        kernel,
        in_specs=[vmem] * kept + [hbm] * fetched,
        out_specs=[vmem] * len(outs),
        out_shape=outs,
        scratch_shapes=list(scratch),
        compiler_params=pltpu.CompilerParams(vmem_limit_bytes=VMEM_LIMIT),
        name=name,
    )(*operands)


def start_copies(pairs, sems):
    copies = [pltpu.make_async_copy(a, b, sems.at[k]) for k, (a, b) in enumerate(pairs)]
    for copy in copies:
        copy.start()
    return copies


def project_kernel(mine, row_len, *refs):
    if mine:
        squares_ref, rows_ref, wq_ref, out_ref, acc_ref = refs
    else:
        rows_hbm, wq_hbm, out_ref, squares_ref, rows_ref, wq_ref, acc_ref, sq_ref, sems = refs
    many = rows_ref.shape[0]
    width = wq_ref.shape[1] // CORES
    heads = width // HD
    core = lax.axis_index("tc")
    half = core if mine else 1 - core
    columns = pl.ds(pl.multiple_of(half * width, width), width)
    steps = 1 if mine else FEATURE_COPIES
    depth = wq_ref.shape[0] // steps
    spans = [pl.ds(k * depth, depth) for k in range(steps)]
    if not mine:
        kept = pl.ds(pl.multiple_of(core * width, width), width)
        pieces = []
        for k in spans:
            pieces += [(wq_hbm.at[k, columns], wq_ref.at[k, columns])]
            pieces += [(rows_hbm.at[:, k], rows_ref.at[:, k])]
        pieces += [(wq_hbm.at[:, kept], wq_ref.at[:, kept])]
        copies = start_copies(pieces, sems)
    chunk = many // row_len
    pairs = row_len // PAIR
    each = out_ref.shape[0] // pairs
    body = each - 8
    seqs = body // (heads * PAIR)
    product = sums = None
    for step, k in enumerate(spans):
        if not mine:
            copies[2 * step].wait()
            copies[2 * step + 1].wait()
        rows = rows_ref[:, k]
        part = mm(rows, wq_ref[k, columns])
        product = part if product is None else product + part
        if not mine:
            wide_rows = rows.astype(F32)
            wide_rows = wide_rows * wide_rows
            for first in range(0, depth, HD):
                slab = wide_rows[:, first : first + HD]
                sums = slab if sums is None else sums + slab
    for h in range(heads):
        acc_ref[h * many : (h + 1) * many, :] = product[:, h * HD : (h + 1) * HD]
    for t in range(row_len):
        for h in range(heads):
            first = (t // PAIR) * each + (h * PAIR + t % PAIR) * seqs
            out_ref[first : first + chunk, :] = acc_ref[rows_at(h * many + t, chunk, row_len), :]
    if mine:
        for p in range(pairs):
            tail = slice(p * each + body, (p + 1) * each)
            out_ref[tail, :] = squares_ref[p * 8 : (p + 1) * 8, :]
        return
    sq_ref[...] = jnp.broadcast_to(jnp.sum(sums, axis=1, keepdims=True), sq_ref.shape)
    across = lax.broadcasted_iota(jnp.int32, (chunk, HD), 0)
    lane = lax.broadcasted_iota(jnp.int32, (chunk, HD), 1)
    for p in range(pairs):
        total = jnp.zeros((1, HD), F32)
        for t in range(p * PAIR, (p + 1) * PAIR):
            spot = lane == across + (t % PAIR) * seqs
            picked = jnp.where(spot, sq_ref[rows_at(t, chunk, row_len), :], 0.0)
            total += jnp.sum(picked, axis=0, keepdims=True)
        tail = jnp.broadcast_to(total, (8, HD))
        squares_ref[p * 8 : (p + 1) * 8, :] = tail
        out_ref[p * each + body : (p + 1) * each, :] = tail
    copies[-1].wait()


def add_kernel(a_ref, b_ref, out_ref):
    out_ref[...] = a_ref[...] + b_ref[...]


def exchange_both_ways(x):
    wide_count, chips, cores = (lax.axis_size(name) for name in AXES)
    groups = []
    for core in range(cores):
        for chip in range(chips):
            group = [(w * chips + chip) * cores + core for w in range(wide_count)]
            groups.append(group if core == 1 else group[::-1])
    return lax.all_to_all(
        x, AXES, split_axis=0, concat_axis=0, axis_index_groups=groups, tiled=True
    )


def decode_kernel(
    lens_hbm,
    q_hbm,
    nk_hbm,
    nv_hbm,
    route_hbm,
    score_hbm,
    delta_hbm,
    k_hbm,
    v_hbm,
    w_hbm,
    attn_ref,
    out_ref,
    place_ref,
    sent_ref,
    tile_ref,
    delta_ref,
    length_ref,
    lens_ref,
    q_ref,
    nk_ref,
    nv_ref,
    route_ref,
    score_ref,
    k_ref,
    v_ref,
    w_ref,
    sems,
):
    w_cols = w_ref.shape[1] // WEIGHT_COPIES
    copies = start_copies(
        [
            (lens_hbm, lens_ref),
            (q_hbm, q_ref),
            (nk_hbm, nk_ref),
            (nv_hbm, nv_ref),
            (route_hbm, route_ref),
            (score_hbm, score_ref),
            (delta_hbm, delta_ref),
            (k_hbm, k_ref),
            (v_hbm, v_ref),
        ]
        + [
            (w_hbm.at[:, pl.ds(c, w_cols)], w_ref.at[:, pl.ds(c, w_cols)])
            for c in range(0, w_ref.shape[1], w_cols)
        ],
        sems,
    )
    for copy in copies[:-WEIGHT_COPIES]:
        copy.wait()
    seqs = q_ref.shape[0]
    rows = 2 * seqs
    scale = 1.0 / math.sqrt(HD)
    q = q_ref[...].astype(F32)
    queries = jnp.concatenate([q[:, :HD], q[:, HD:]], axis=0)
    nk = nk_ref[...].astype(F32)
    nv = nv_ref[...].astype(F32)
    own_key = jnp.concatenate([nk, nk], axis=0)
    own_value = jnp.concatenate([nv, nv], axis=0)
    row = lax.broadcasted_iota(jnp.int32, (rows, HD), 0) % seqs
    place_in = lax.broadcasted_iota(jnp.int32, (rows, HD), 1)
    queries16 = queries.astype(BF16)
    scores = jnp.zeros((rows, HD), F32)
    length = jnp.zeros((rows, HD), jnp.int32)
    for s in range(seqs):
        scores = jnp.where(row == s, mm_t(queries16, k_ref[s]), scores)
        length = jnp.where(row == s, lens_ref[s], length)
    scores = jnp.where(place_in < length, scores * scale, -jnp.inf)
    own_score = jnp.sum(queries * own_key, axis=1, keepdims=True) * scale
    highest = jnp.maximum(jnp.max(scores, axis=1, keepdims=True), own_score)
    weights = jnp.exp(scores - highest)
    own_weight = jnp.exp(own_score - highest)
    denominator = jnp.sum(weights, axis=1, keepdims=True) + own_weight
    probs = (weights / denominator).astype(BF16)
    own_prob = (own_weight / denominator).astype(BF16).astype(F32)
    mixed = jnp.zeros((rows, HD), F32)
    for s in range(seqs):
        mixed = jnp.where(row == s, mm(probs, v_ref[s]), mixed)
    attn = (mixed + own_prob * own_value).astype(BF16).astype(F32)
    attn_ref[...] = attn
    turned = jnp.concatenate([attn[seqs:], attn[:seqs]], axis=0)
    both = jnp.concatenate([attn, turned], axis=1).astype(BF16)
    blocks = w_ref.shape[1] // HD
    shards = blocks // 4
    for copy in copies[-WEIGHT_COPIES:]:
        copy.wait()
    for first in range(0, blocks, 4):
        part = mm(both, w_ref[:, first * HD : (first + 4) * HD])
        for c in range(4):
            own = rows_at(c * seqs * shards + first // 4, seqs, shards)
            out_ref[own, :] = part[:seqs, c * HD : (c + 1) * HD]
    slots = place_ref.shape[0]
    groups = slots // CAP
    down = lax.broadcasted_iota(jnp.int32, (HD, HD), 0)
    across = lax.broadcasted_iota(jnp.int32, (HD, HD), 1)
    routing = route_ref[...]
    route = routing[0:1]
    target = jnp.broadcast_to(route, (HD, HD))
    target_down = jnp.sum(jnp.where(down == across, target, 0.0), axis=1, keepdims=True)
    earlier = jnp.where(jnp.logical_and(target == target_down, down < across), 1.0, 0.0)
    rank = jnp.sum(earlier, axis=0, keepdims=True)
    slot = lax.broadcasted_iota(jnp.int32, (slots, HD), 0)
    group = (slot % groups).astype(F32)
    order = (slot // groups).astype(F32)
    held = jnp.logical_and(route == group, rank == order)
    place_ref[...] = jnp.where(held, 1.0, 0.0).astype(BF16)
    sent = jnp.where(lax.axis_index("tc") == 1, group, groups - 1 - group)
    held = jnp.logical_and(route == sent, rank == order)
    sent_ref[...] = jnp.where(held, 1.0, 0.0).astype(BF16)
    weight = score_ref[...].astype(F32)
    heads = weight.shape[0] // CORES
    weight = jnp.where(lax.axis_index("tc") == 0, weight[:heads], weight[heads:])
    for h in range(heads):
        own = slice(h * rows // heads, (h + 1) * rows // heads)
        tile_ref[own, :] = jnp.broadcast_to(weight[h : h + 1], (rows // heads, HD))
    block = jnp.broadcast_to(routing[2:3], (8, HD))
    row_block = jnp.floor(block / blocks)
    tile_ref[rows : rows + 8, :] = row_block
    tile_ref[rows + 8 : rows + 16, :] = block - row_block * blocks
    length_ref[...] = jnp.broadcast_to(routing[1:2], length_ref.shape)


def place_kernel(sources, x_ref, attn_ref, place_ref, out_ref, lay_ref):
    each = x_ref.shape[0] // sources
    body = each - 8
    groups = place_ref.shape[0] // CAP
    lay = out_ref.shape[1]
    tile = 2 * lay
    parts = lay // CAP
    heads = parts // PAIR
    seqs = body // parts
    total = x_ref[0:each, :]
    for k in range(1, sources):
        total = total + x_ref[k * each : (k + 1) * each, :]
    inverse = lax.rsqrt(total[body : body + 1, :] / RD + 1e-05) * (math.log2(math.e) / math.sqrt(HD))
    down = lax.broadcasted_iota(jnp.int32, (HD, HD), 0)
    across = lax.broadcasted_iota(jnp.int32, (HD, HD), 1)
    factor = jnp.sum(jnp.where(down == across, inverse, 0.0), axis=1, keepdims=True)
    pieces = []
    for h in range(heads):
        for p in range(PAIR):
            first = (h * PAIR + p) * seqs
            pieces.append(total[first : first + seqs, :] * factor[p * seqs : (p + 1) * seqs, :])
    normed = jnp.concatenate(pieces, axis=1)
    if seqs < HD:
        normed = jnp.concatenate([normed, jnp.zeros((HD - seqs, parts * HD), F32)], axis=0)
    place = place_ref[...]
    for k, term in enumerate(split2(normed)):
        placed = mm(place, term)
        for r in range(CAP):
            for q in range(parts):
                row = k * lay + (q // PAIR) * CAP * PAIR + r * PAIR + q % PAIR
                lay_ref[rows_at(row, groups, tile), :] = placed[
                    r * groups : (r + 1) * groups, q * HD : (q + 1) * HD
                ]
    attn = attn_ref[...].astype(BF16)
    for g in range(groups):
        for k in range(2):
            own = slice(g * tile + k * lay, g * tile + (k + 1) * lay)
            out_ref[3 * g + k] = lay_ref[own, :].astype(BF16)
        out_ref[3 * g + 2] = attn


def score_kernel(
    seqs, x_ref, keys_ref, values_ref, weight_ref, delta_ref, out_ref, lay_ref, in_order_ref
):
    tile = 2 * seqs
    senders = x_ref.shape[0] // 3
    keys = keys_ref[...]
    keys2 = jnp.concatenate([keys, keys], axis=1)
    values = values_ref[...]
    weight = weight_ref[0:tile, :][None]
    row_block = weight_ref[tile : tile + 1, :][None]
    column = weight_ref[tile + 8 : tile + 9, :]
    delta = delta_ref[...]
    at_once = min(AT_ONCE, senders)
    row = lax.broadcasted_iota(jnp.int32, (1, tile, HD), 1)
    core = lax.axis_index("tc")
    for w in range(senders):
        came = jnp.where(core == 1, w, senders - 1 - w)
        for k in range(3):
            in_order_ref[k, w * tile : (w + 1) * tile, :] = x_ref[3 * came + k].astype(F32)
    started = []
    for first in range(0, senders, at_once):
        span = slice(first * tile, (first + at_once) * tile)
        flat = [in_order_ref[k, span, :].astype(BF16) for k in range(3)]
        scores = mm_t(jnp.concatenate(flat[:2], axis=1), keys2)
        started.append((first, scores, mm(flat[2], delta)))
    for first, scores, product in started:
        highest = jnp.max(scores, axis=1, keepdims=True)
        weights = jnp.exp2(scores - highest)
        probs = (weights * (1.0 / jnp.sum(weights, axis=1, keepdims=True))).astype(BF16)
        context = mm(probs, values)
        gated = context / (1.0 + jnp.exp(-context))
        terms = gated.reshape(at_once, tile, HD) * weight
        by_head = jnp.broadcast_to(jnp.sum(terms, axis=2, keepdims=True), terms.shape)
        score = by_head + jnp.concatenate([by_head[:, seqs:], by_head[:, :seqs]], axis=1)
        product = product.reshape(at_once, tile, HD)
        turned = jnp.concatenate([product[:, seqs:], product[:, :seqs]], axis=1)
        result = jnp.where(row_block == 0.0, product, turned)
        result = jnp.where(row < seqs, result, score)
        span = slice(first * tile, (first + at_once) * tile)
        lay_ref[span, :] = result.reshape(at_once * tile, HD)
    for q in range(seqs):
        out_ref[rows_at(q, senders, seqs + 1), :] = lay_ref[rows_at(q, senders, tile), :]
    lane = lax.broadcasted_iota(jnp.int32, (senders, HD), 1)
    last = jnp.broadcast_to(column, (senders, HD))
    for q in range(seqs):
        last = jnp.where(lane == q, lay_ref[rows_at(seqs + q, senders, tile), :], last)
    out_ref[rows_at(seqs, senders, seqs + 1), :] = last


def merge_kernel(seqs, shards, x_ref, partial_ref, place_ref, out_ref):
    each = seqs + 1
    senders = x_ref.shape[0] // each
    blocks = partial_ref.shape[0] // seqs - 8
    own_blocks = blocks // shards
    message = out_ref.shape[0] // shards
    last = x_ref[rows_at(seqs, senders, each), :]
    column = last[:, HD - 1 :]
    pieces = split3(
        jnp.concatenate([x_ref[rows_at(s, senders, each), :] for s in range(seqs)], axis=1)
    )
    down = lax.broadcasted_iota(jnp.int32, (senders, senders), 0)
    across = lax.broadcasted_iota(jnp.int32, (senders, senders), 1)
    column_across = jnp.sum(
        jnp.where(down == across, jnp.broadcast_to(column, (senders, senders)), 0.0),
        axis=0,
        keepdims=True,
    )
    order = lax.broadcasted_iota(jnp.int32, (blocks, senders), 0)
    wanted = (order % shards * own_blocks + order // shards).astype(F32)
    pick = jnp.where(wanted == column_across, 1.0, 0.0).astype(BF16)
    high, mid, low = pieces
    added = (mm(pick, low) + mm(pick, mid)) + mm(pick, high)
    for c in range(own_blocks):
        for s in range(seqs):
            q = c * seqs + s
            out_ref[rows_at(q, shards, message), :] = (
                partial_ref[q * shards : (q + 1) * shards, :]
                + added[c * shards : (c + 1) * shards, s * HD : (s + 1) * HD]
            )
    place = place_ref[...].astype(F32)
    for p in range(PAIR):
        score = jnp.concatenate(
            [last[:, r * PAIR + p : r * PAIR + p + 1] for r in range(CAP)], axis=0
        )
        back = jnp.sum(place * score, axis=0, keepdims=True)
        out_ref[rows_at(own_blocks * seqs + p, shards, message), :] = jnp.broadcast_to(
            back, (shards, HD)
        )


def final_kernel(shards, x_ref, length_ref, decoded_ref, rewards_ref):
    each = x_ref.shape[0] // shards
    seqs = decoded_ref.shape[0]
    body = each - PAIR
    rows = [x_ref[rows_at(q, shards, each), :] for q in range(each)]
    sums = [jnp.sum(row, axis=0, keepdims=True) for row in rows[:body]]
    for c in range(body // seqs):
        block = jnp.concatenate(sums[c * seqs : (c + 1) * seqs], axis=0)
        decoded_ref[:, c * HD : (c + 1) * HD] = block.astype(BF16)
    length = length_ref[0:1, :]
    count = rewards_ref.shape[1]
    shard = lax.broadcasted_iota(jnp.int32, (shards, HD), 0)
    reward = jnp.zeros((1, HD), F32)
    for p in range(PAIR):
        token = (shard // CORES * PAIR + p).astype(F32)
        scored = jnp.where(length > token, rows[body + p], 0.0)
        reward = reward + jnp.sum(scored, axis=0, keepdims=True)
    rewards_ref[...] = (reward / length)[:, :count]


def per_device(
    query,
    key_cache,
    value_cache,
    new_key,
    new_value,
    cache_lengths,
    out_weight,
    delta_index,
    delta_values,
    fin_route,
    fin_lengths,
    fin_rows,
    reward_query,
    rubric_keys,
    rubric_values,
    score_weight,
):
    wide_count = lax.axis_size("wide")
    chips = lax.axis_size("th")
    tp_count = chips * lax.axis_size("tc")
    finished, row_len, features = fin_rows.shape
    heads = reward_query.shape[1] // HD // CORES
    seq_count = query.shape[0]
    tile = 2 * seq_count
    blocks = out_weight.shape[1] // HD
    slots = CAP * wide_count
    parts = PAIR * heads
    message = parts * finished + 8
    shape = jax.ShapeDtypeStruct

    rows = fin_rows.reshape(finished * row_len, features)
    partial = shape((chips * message, HD), F32)
    squares_shape = shape((chips * 8, HD), F32)
    acc = pltpu.VMEM((heads * finished * row_len, HD), F32)
    theirs, squares, rows, weights = local_call(
        functools.partial(project_kernel, False, row_len),
        "project_theirs",
        (rows, reward_query),
        [partial, squares_shape, shape(rows.shape, BF16), shape(reward_query.shape, BF16)],
        [
            acc,
            pltpu.VMEM((finished * row_len, HD), F32),
            pltpu.SemaphoreType.DMA((2 * FEATURE_COPIES + 1,)),
        ],
        fetched=2,
    )
    got = lax.ppermute(theirs, "tc", [(0, 1), (1, 0)])
    (kept,) = local_call(
        functools.partial(project_kernel, True, row_len),
        "project_kept",
        (squares, rows, weights),
        [partial],
        [acc],
    )
    (both,) = local_call(add_kernel, "add", (kept, got), [partial])
    summed_tokens = lax.all_to_all(
        both.reshape(chips, message, HD), "th", split_axis=0, concat_axis=0, tiled=True
    ).reshape(partial.shape)

    pad = ((0, 0), (0, HD - finished))
    routing = jnp.concatenate(
        [
            jnp.pad(fin_route.reshape(1, finished), pad, constant_values=-1),
            jnp.pad(fin_lengths.reshape(1, finished), pad, constant_values=1),
            jnp.broadcast_to(delta_index.reshape(1, 1), (1, HD)),
        ]
    ).astype(F32)
    weights = score_weight.reshape(heads * CORES, HD)
    small = (cache_lengths, query, new_key, new_value, routing, weights, delta_values[0])
    large = (key_cache, value_cache, out_weight)
    attn, partial_out, place, sent, weight_tile, delta, lengths = local_call(
        decode_kernel,
        "decode",
        small + large,
        [
            shape((tile, HD), F32),
            shape(((blocks + 8) * seq_count, HD), F32),
            shape((slots, HD), BF16),
            shape((slots, HD), BF16),
            shape((tile + 16, HD), F32),
            shape(delta_values.shape[1:], BF16),
            shape((8, HD), F32),
        ],
        [pltpu.SMEM(cache_lengths.shape, jnp.int32)]
        + [pltpu.VMEM(a.shape, a.dtype) for a in small[1:-1] + large]
        + [pltpu.SemaphoreType.DMA((len(small) + 2 + WEIGHT_COPIES,))],
        fetched=len(small) + len(large),
    )

    lay = CAP * parts
    (outgoing,) = local_call(
        functools.partial(place_kernel, chips),
        "place",
        (summed_tokens, attn, sent),
        [shape((wide_count * 3, lay, HD), BF16)],
        [pltpu.VMEM((wide_count * 2 * lay, HD), F32)],
    )
    received = exchange_both_ways(outgoing)

    answer = seq_count + 1
    (answers,) = local_call(
        functools.partial(score_kernel, seq_count),
        "score",
        (
            received,
            rubric_keys[0],
            rubric_values[0],
            weight_tile,
            delta,
        ),
        [shape((wide_count * answer, HD), F32)],
        [pltpu.VMEM((wide_count * tile, HD), F32), pltpu.VMEM((3, wide_count * tile, HD), F32)],
    )
    returned = lax.all_to_all(
        answers.reshape(wide_count, 1, answer * HD), "wide", split_axis=0, concat_axis=0, tiled=True
    ).reshape(answers.shape)

    share = blocks // tp_count * seq_count + PAIR
    (merged,) = local_call(
        functools.partial(merge_kernel, seq_count, tp_count),
        "merge",
        (returned, partial_out, place),
        [shape((tp_count * share, HD), F32)],
    )
    shares = lax.all_to_all(
        merged.reshape(tp_count, 1, share * HD),
        ("th", "tc"),
        split_axis=0,
        concat_axis=0,
        tiled=True,
    ).reshape(merged.shape)

    decoded, rewards = local_call(
        functools.partial(final_kernel, tp_count),
        "final",
        (shares, lengths),
        [shape((seq_count, blocks // tp_count * HD), BF16), shape((1, finished), F32)],
    )
    return decoded, rewards.reshape(finished)


def solution(mesh):
    tp = ("th", "tc")
    wide_count, tp_count = mesh.devices.shape
    split = jax.sharding.Mesh(
        mesh.devices.reshape(wide_count, tp_count // CORES, CORES), ("wide",) + tp
    )
    in_specs = (
        P("wide", tp),
        P("wide", None, tp),
        P("wide", None, tp),
        P("wide", tp),
        P("wide", tp),
        P("wide"),
        P(tp, None),
        P("wide"),
        P("wide", tp, None),
        P("wide", None),
        P("wide"),
        P("wide", None, tp),
        P(tp, None),
        P("wide", None, None),
        P("wide", None, None),
        P(),
    )
    out_specs = (P("wide", tp), P("wide"))
    return jax.shard_map(
        per_device, mesh=split, in_specs=in_specs, out_specs=out_specs, check_vma=False
    )
```
